32 devices in a mesh: dp: 4 (over x, core), expert: 8 (over z, y).
Axes of the slice: x: 2, y: 2, z: 4, core: 2. Of those that a mesh axis runs over, the one named last changes fastest.
Arguments:
- grad_rows: bfloat16 [4, 16, 16, 3584], P('dp', 'expert'), may hold values from -6 to 6
- router_weight: float32 [4, 16, 16], P('dp', 'expert'), may hold values from 0.05 to 0.6
- send_counts: int32 [4, 16], P('dp', 'expert'), may hold values from 1 to 16, as said below
- gate_stash: bfloat16 [4, 128, 2048], P('dp', None, 'expert'), may hold values from -6 to 6
- up_stash: bfloat16 [4, 128, 2048], P('dp', None, 'expert'), may hold values from -6 to 6
- master_weight: float32 [3584, 2048], P('dp', 'expert'), may hold values from -0.1875 to 0.1875
- first_moment: float32 [3584, 2048], P('dp', 'expert'), may hold values from -18 to 18
- second_moment: float32 [3584, 2048], P('dp', 'expert'), may hold values from 10 to 100
Outputs:
- d_gate: bfloat16 [4, 128, 2048], P('dp', None, 'expert')
- d_up: bfloat16 [4, 128, 2048], P('dp', None, 'expert')
- new_master: float32 [3584, 2048], P('dp', 'expert')
- new_first: float32 [3584, 2048], P('dp', 'expert')
- new_second: float32 [3584, 2048], P('dp', 'expert')
- fresh_weight: bfloat16 [3584, 2048], P(None, 'expert')
The draws below stay inside these ranges and needn't reach their ends.
Inputs may be any that keep to these rules, and one draw needn't show every extreme that they name: `send_counts`: in every replica one expert in flight receives exactly 16 rows from every source; the other counts are at most 8.
All inputs are finite; a program needn't handle non-finite values.
Results may differ from the reference program's by a relative error of at most 0.009.
Values may be sent and summed in bfloat16 or wider, within the bound.
No kernel may reach another device: no remote copies, remote signals or barrier semaphores. Data moves between devices by JAX's collectives and lax.ppermute only.
A program may use at most 64 MiB of HBM per device.

```python
import math
import jax
import jax.numpy as jnp
from jax import lax

D_W = 3584
FF = 1024
SLOT = 16
FLIGHT = 2
N_DP = 4
N_EXPERT = 8


def draw_send_counts(key, part):
    key = jax.random.fold_in(key, 7)
    base = jax.random.randint(jax.random.fold_in(key, 1), (N_DP, N_EXPERT, FLIGHT), 1, SLOT // 2 + 1)
    hottest = jax.random.randint(jax.random.fold_in(key, 2), (N_DP, 1, 1), 0, FLIGHT)
    experts = jnp.arange(FLIGHT, dtype=jnp.int32)[None, None, :]
    counts = jnp.where(experts == hottest, SLOT, base)
    return counts.reshape(N_DP, N_EXPERT * FLIGHT).astype(jnp.int32)


def steps_of(own_key, dims, pieces, smallest, largest):
    def one(axis_at, parts):
        heights = jax.random.uniform(jax.random.fold_in(jax.random.fold_in(own_key, 6), axis_at), (parts,), jnp.float32, smallest / len(pieces), largest / len(pieces))
        return jnp.repeat(jnp.exp(heights), dims[axis_at] // parts).reshape((-1,) + (1,) * (len(dims) - axis_at - 1))

    loudness = one(*pieces[0])
    for cut in pieces[1:]:
        loudness = loudness * one(*cut)
    return loudness


def centred(key, dims, scale, most, pieces=(), kind=jnp.bfloat16):
    gain = steps_of(key, dims, pieces, -0.22, 0.18) if pieces else 1.0
    drawn = jax.random.normal(key, dims, jnp.float32) * scale * gain
    return jnp.minimum(jnp.maximum(drawn, -most), most).astype(kind)


def setup_inputs(seed: int = 0) -> dict:
    key_of = jax.random.split(jax.random.key(seed), 9)
    return {
        "grad_rows": centred(key_of[0], (N_DP, N_EXPERT * FLIGHT, SLOT, D_W), 1.0, 6.0, ((0, 4), (1, 8))),
        "router_weight": jnp.clip(jnp.exp(math.log(0.6) - 2.4849067 * jax.random.uniform(key_of[1], (N_DP, N_EXPERT * FLIGHT, SLOT), jnp.float32) ** steps_of(key_of[1], (N_DP, N_EXPERT * FLIGHT, SLOT), ((0, 4), (1, 8)), -0.2, 0.2)), 0.05, 0.6),
        "send_counts": draw_send_counts(jax.random.fold_in(key_of[8], 71), 0),
        "gate_stash": centred(key_of[3], (N_DP, N_EXPERT * SLOT, FLIGHT * FF), 1.0, 6.0, ((0, 4), (2, 8))),
        "up_stash": centred(key_of[4], (N_DP, N_EXPERT * SLOT, FLIGHT * FF), 1.0, 6.0, ((0, 4), (2, 8))),
        "master_weight": centred(key_of[5], (D_W, FLIGHT * FF), FF ** -0.5, 0.1875, ((0, 4), (1, 8)), jnp.float32),
        "first_moment": centred(key_of[6], (D_W, FLIGHT * FF), 3.0, 18.0, ((0, 4), (1, 8)), jnp.float32),
        "second_moment": jnp.clip(jnp.exp(math.log(100.0) - 2.3025851 * jax.random.uniform(key_of[7], (D_W, FLIGHT * FF), jnp.float32) ** steps_of(key_of[7], (D_W, FLIGHT * FF), ((0, 4), (1, 8)), -0.2, 0.2)), 10.0, 100.0),
    }


learning_rate = 0.01
beta_one = 0.9
beta_two = 0.95
decay_rate = 0.1
epsilon = 1e-08

def reference(grad_rows, router_weight, send_counts, gate_stash, up_stash, master_weight, first_moment, second_moment):
    flight = master_weight.shape[1] // FF
    grads = grad_rows.reshape(N_DP, N_EXPERT, flight, SLOT, D_W)
    probs = router_weight.reshape(N_DP, N_EXPERT, flight, SLOT)
    counts = send_counts.reshape(N_DP, N_EXPERT, flight)
    slots = jnp.arange(SLOT, dtype=jnp.int32)

    def one_expert(which):
        which = which.astype(jnp.int32)
        rows_in = lax.dynamic_index_in_dim(grads, which, 2, keepdims=False)
        weights = lax.dynamic_index_in_dim(probs, which, 2, keepdims=False)
        limit = lax.dynamic_index_in_dim(counts, which, 2, keepdims=False)
        live = slots[None, None, :] < limit[:, :, None]
        scaled = jnp.where(live[..., None], weights[..., None] * rows_in.astype(jnp.float32), jnp.float32(0.0))
        scaled = scaled.astype(jnp.bfloat16).reshape(N_DP * N_EXPERT * SLOT, D_W)
        start = (which * FF).astype(jnp.int32)
        gate = lax.dynamic_slice_in_dim(gate_stash, start, FF, 2).astype(jnp.float32).reshape(-1, FF)
        up = lax.dynamic_slice_in_dim(up_stash, start, FF, 2).astype(jnp.float32).reshape(-1, FF)
        sigmoid_gate = jax.nn.sigmoid(gate)
        activated = gate * sigmoid_gate
        hidden = (activated * up).astype(jnp.bfloat16)
        gradient = lax.dot_general(scaled, hidden, (((0,), (0,)), ((), ())), preferred_element_type=jnp.float32)
        master = lax.dynamic_slice_in_dim(master_weight, start, FF, 1)
        moment_a = lax.dynamic_slice_in_dim(first_moment, start, FF, 1)
        moment_b = lax.dynamic_slice_in_dim(second_moment, start, FF, 1)
        current = master.astype(jnp.bfloat16)
        d_hidden = jnp.dot(scaled, current, preferred_element_type=jnp.float32)
        grad_gate = (d_hidden * up * sigmoid_gate * (1.0 + gate * (1.0 - sigmoid_gate))).astype(jnp.bfloat16)
        grad_up = (d_hidden * activated).astype(jnp.bfloat16)
        moment_a = beta_one * moment_a + (1.0 - beta_one) * gradient
        moment_b = beta_two * moment_b + (1.0 - beta_two) * gradient * gradient
        step_size = moment_a / (1.0 - beta_one ** 5) / (jnp.sqrt(moment_b / (1.0 - beta_two ** 5)) + epsilon)
        master = master - learning_rate * (step_size + decay_rate * master)
        return (grad_gate.reshape(N_DP, N_EXPERT * SLOT, FF), grad_up.reshape(N_DP, N_EXPERT * SLOT, FF), master, moment_a, moment_b, master.astype(jnp.bfloat16))
    outs = lax.map(one_expert, jnp.arange(flight, dtype=jnp.int32))

    def rows_layout(stacked):
        return stacked.transpose(1, 2, 0, 3).reshape(N_DP, N_EXPERT * SLOT, flight * FF)

    def weight_layout(stacked):
        return stacked.transpose(1, 0, 2).reshape(D_W, flight * FF)
    return (rows_layout(outs[0]), rows_layout(outs[1]), weight_layout(outs[2]), weight_layout(outs[3]), weight_layout(outs[4]), weight_layout(outs[5]))
```

```python
import functools

import jax
import jax.numpy as jnp
from jax import lax
from jax.experimental import pallas as pl
from jax.experimental.pallas import tpu as pltpu
from jax.sharding import PartitionSpec as P

learning_rate = 0.01
beta_one = 0.9
beta_two = 0.95
decay_rate = 0.1
epsilon = 1e-08

bf16 = jnp.bfloat16
f32 = jnp.float32
VMEM_LIMIT = 40 * 1024 * 1024


def params():
    return pltpu.CompilerParams(vmem_limit_bytes=VMEM_LIMIT)


def cost(flops, nbytes):
    return pl.CostEstimate(flops=flops, bytes_accessed=nbytes, transcendentals=0)


def scale_kernel(counts, router, rows, gate, up, out, hidden):
    flight, slots, width = rows.shape[1:]
    pieces = out.shape[0]
    piece = width // pieces
    ways = hidden.shape[0]
    diagonal = lax.broadcasted_iota(jnp.int32, (slots, slots), 0) == lax.broadcasted_iota(
        jnp.int32, (slots, slots), 1
    )
    row = lax.broadcasted_iota(jnp.int32, (slots, 1), 0)
    for f in range(flight):
        weight = jnp.sum(
            jnp.where(diagonal, jnp.broadcast_to(router[0, f : f + 1, :], (slots, slots)), 0.0),
            axis=1,
            keepdims=True,
        )
        live = row < counts[0, f]
        scaled = jnp.where(live, weight * rows[0, f].astype(f32), 0.0).astype(bf16)
        for i in range(pieces):
            out[i, f] = scaled[:, i * piece : (i + 1) * piece]
    g = gate[0].astype(f32)
    value = (g * jax.nn.sigmoid(g) * up[0].astype(f32)).astype(bf16)
    for f in range(flight):
        for v in range(ways):
            at = (f * ways + v) * slots
            hidden[v, f] = value[at : at + slots]


def update_kernel(ways, pieces, place, *refs):
    rows = refs[:ways]
    hiddens = refs[ways : ways + pieces]
    master, first, second = refs[ways + pieces : ways + pieces + 3]
    new_master, new_first, new_second, fresh, held = refs[ways + pieces + 3 :]
    me, lane = place[0], place[1]

    @pl.when(pl.program_id(0) == 0)
    def _():
        for d in range(pieces):
            held[:, me ^ d] = hiddens[d][...].reshape(held.shape[0], held.shape[2], held.shape[3])

    gradient = None
    for d in range(ways):
        part = held[lane ^ d].reshape(-1, held.shape[3])
        left = rows[d][...].reshape(-1, rows[d].shape[-1])
        term = lax.dot_general(left, part, (((0,), (0,)), ((), ())), preferred_element_type=f32)
        gradient = term if gradient is None else gradient + term
    moment_a = beta_one * first[...] + (1.0 - beta_one) * gradient
    moment_b = beta_two * second[...] + (1.0 - beta_two) * gradient * gradient
    old = master[...]
    step_size = (
        moment_a / (1.0 - beta_one**5) / (jnp.sqrt(moment_b / (1.0 - beta_two**5)) + epsilon)
    )
    updated = old - learning_rate * (step_size + decay_rate * old)
    new_master[...] = updated
    new_first[...] = moment_a
    new_second[...] = moment_b
    fresh[...] = updated.astype(bf16)


def partial_kernel(ways, pieces, place, *refs):
    rows = refs[:ways]
    master = refs[ways]
    outs = refs[ways + 1 : ways + 1 + pieces]
    held = refs[ways + 1 + pieces]
    me, lane = place[0], place[1]
    current = master[...].astype(bf16)
    for d in range(ways):
        left = rows[d][...].reshape(-1, rows[d].shape[-1])
        held[lane ^ d] = jnp.dot(left, current, preferred_element_type=f32).reshape(held.shape[1:])
    for d in range(pieces):
        outs[d][...] = held[:, me ^ d].astype(outs[d].dtype)


def gate_kernel(ways, pieces, gate, up, *refs):
    parts = refs[:pieces]
    d_gate, d_up = refs[pieces:]
    total = parts[0][...]
    for part in parts[1:]:
        total = total + part[...].astype(f32)
    flight = gate.shape[1] // ways // 16
    slots = total.shape[1] // flight
    for f in range(flight):
        for v in range(ways):
            at = pl.ds((f * ways + v) * slots, slots)
            grad = total[v, f * slots : (f + 1) * slots]
            g = gate[0, at].astype(f32)
            u = up[0, at].astype(f32)
            sig = jax.nn.sigmoid(g)
            d_gate[0, at] = (grad * u * sig * (1.0 + g * (1.0 - sig))).astype(bf16)
            d_up[0, at] = (grad * (g * sig)).astype(bf16)


def join_kernel(count, place, *refs):
    shards = refs[:count]
    out = refs[count]
    sems = refs[count + 1]
    me = place[0]
    high = shards[0].shape[0]
    copies = []
    for d in range(count):
        copy = pltpu.make_async_copy(
            shards[d], out.at[pl.ds(pl.multiple_of((me ^ d) * high, high), high)], sems.at[d]
        )
        copy.start()
        copies.append(copy)
    for copy in copies:
        copy.wait()


def whole(memory=pltpu.VMEM):
    return pl.BlockSpec(memory_space=memory)


def local(
    grad_rows,
    router_weight,
    send_counts,
    gate_stash,
    up_stash,
    master_weight,
    first_moment,
    second_moment,
):
    _, flight, slots, width = grad_rows.shape
    pieces = lax.axis_size("dp")
    sources = lax.axis_size("expert")
    ways = sources // flight
    high, across = master_weight.shape
    me = lax.axis_index("dp")
    lane = lax.axis_index("expert") % ways
    place = jnp.stack([me, lane]).astype(jnp.int32)
    smem = whole(pltpu.SMEM)

    def over_dp(x, d):
        return lax.ppermute(x, "dp", [(i, i ^ d) for i in range(pieces)])

    out, hidden = pl.pallas_call(
        scale_kernel,
        out_shape=(
            jax.ShapeDtypeStruct((pieces, flight, slots, high), bf16),
            jax.ShapeDtypeStruct((ways, flight, slots, across), bf16),
        ),
        in_specs=[smem] + [whole()] * 4,
        out_specs=[whole()] * 2,
        compiler_params=params(),
        name="scale",
    )(send_counts, router_weight, grad_rows, gate_stash, up_stash)
    hiddens = [hidden] + [over_dp(hidden, d) for d in range(1, pieces)]

    groups = [
        [i * sources + g * ways + v for i in range(pieces) for g in range(flight)]
        for v in range(ways)
    ]
    mine = lax.all_to_all(
        out.reshape(pieces * flight, slots, high),
        ("dp", "expert"),
        split_axis=0,
        concat_axis=0,
        axis_index_groups=groups,
        tiled=True,
    )
    rows = [mine] + [
        lax.ppermute(mine, "expert", [(k, k ^ d) for k in range(sources)]) for d in range(1, ways)
    ]

    count = pieces * flight * slots
    tile = 128 if high % 128 == 0 else high
    shard = pl.BlockSpec((tile, across), lambda i, s: (i, 0))
    new_master, new_first, new_second, fresh = pl.pallas_call(
        functools.partial(update_kernel, ways, pieces),
        out_shape=[jax.ShapeDtypeStruct((high, across), f32)] * 3
        + [jax.ShapeDtypeStruct((high, across), bf16)],
        grid_spec=pltpu.PrefetchScalarGridSpec(
            num_scalar_prefetch=1,
            grid=(high // tile,),
            in_specs=[
                pl.BlockSpec((pieces * flight, slots, tile), lambda i, s: (0, 0, i))
            ]
            * ways
            + [pl.BlockSpec((ways, flight, slots, across), lambda i, s: (0, 0, 0, 0))] * pieces
            + [shard] * 3,
            out_specs=[shard] * 4,
            scratch_shapes=[pltpu.VMEM((ways, pieces, flight * slots, across), bf16)],
        ),
        compiler_params=params(),
        cost_estimate=cost(2 * ways * count * high * across, high * across * 26),
        name="update",
    )(place, *rows, *hiddens, master_weight, first_moment, second_moment)

    parts = pl.pallas_call(
        functools.partial(partial_kernel, ways, pieces),
        out_shape=[
            jax.ShapeDtypeStruct((ways, flight * slots, across), bf16 if d else f32)
            for d in range(pieces)
        ],
        in_specs=[smem] + [whole()] * (ways + 1),
        out_specs=[whole()] * pieces,
        scratch_shapes=[pltpu.VMEM((ways, pieces, flight * slots, across), f32)],
        compiler_params=params(),
        cost_estimate=cost(2 * ways * count * high * across, high * across * 8),
        name="partial",
    )(place, *rows, master_weight)
    arrived = [parts[0]] + [over_dp(parts[d], d) for d in range(1, pieces)]
    d_gate, d_up = pl.pallas_call(
        functools.partial(gate_kernel, ways, pieces),
        out_shape=[jax.ShapeDtypeStruct(gate_stash.shape, bf16)] * 2,
        in_specs=[whole()] * (2 + pieces),
        out_specs=[whole()] * 2,
        compiler_params=params(),
        name="gates",
    )(gate_stash, up_stash, *arrived)

    shards = {0: fresh}
    bit = pieces // 2
    while bit:
        for d in list(shards):
            shards[d ^ bit] = over_dp(shards[d], bit)
        bit //= 2
    joined = pl.pallas_call(
        functools.partial(join_kernel, pieces),
        out_shape=jax.ShapeDtypeStruct((pieces * high, across), bf16),
        in_specs=[smem] + [whole(pl.ANY)] * pieces,
        out_specs=whole(pl.ANY),
        scratch_shapes=[pltpu.SemaphoreType.DMA((pieces,))],
        compiler_params=params(),
        name="join",
    )(place, *[shards[d] for d in range(pieces)])
    return (d_gate, d_up, new_master, new_first, new_second, joined)


def solution(mesh):
    placed = (
        P("dp", "expert", None, None),
        P("dp", "expert", None),
        P("dp", "expert"),
        P("dp", None, "expert"),
        P("dp", None, "expert"),
        P("dp", "expert"),
        P("dp", "expert"),
        P("dp", "expert"),
    )
    return jax.shard_map(
        local,
        mesh=mesh,
        in_specs=placed,
        out_specs=(
            P("dp", None, "expert"),
            P("dp", None, "expert"),
            P("dp", "expert"),
            P("dp", "expert"),
            P("dp", "expert"),
            P(None, "expert"),
        ),
        check_vma=False,
    )
```

```python
import functools

import jax
import jax.numpy as jnp
from jax import lax
from jax.experimental import pallas as pl
from jax.experimental.pallas import tpu as pltpu
from jax.sharding import PartitionSpec as P

learning_rate = 0.01
beta_one = 0.9
beta_two = 0.95
decay_rate = 0.1
epsilon = 1e-08

bf16 = jnp.bfloat16
f32 = jnp.float32
VMEM_LIMIT = 40 * 1024 * 1024
TILE = 128


def params():
    return pltpu.CompilerParams(vmem_limit_bytes=VMEM_LIMIT)


def cost(flops, nbytes):
    return pl.CostEstimate(flops=flops, bytes_accessed=nbytes, transcendentals=0)


def tile_rows(high):
    return TILE if high % TILE == 0 else high


def chunks_of(high):
    tiles = high // tile_rows(high)
    cut = (tiles + 1) // 2 * tile_rows(high)
    return [(0, cut), (cut, high)] if cut < high else [(0, high)]


def scale_kernel(counts_in, router_in, rows_in, gate_in, up_in, out, hidden, *scratch):
    counts, router, rows, gate, up, sems = scratch
    copies = [
        pltpu.make_async_copy(source, target, sems.at[n])
        for n, (source, target) in enumerate(
            [
                (gate_in, gate),
                (up_in, up),
                (counts_in, counts),
                (router_in, router),
                (rows_in, rows),
            ]
        )
    ]
    for copy in copies:
        copy.start()
    flight, slots, width = rows.shape[1:]
    pieces = out.shape[0]
    piece = width // pieces
    ways = hidden.shape[0]
    copies[0].wait()
    copies[1].wait()
    g = gate[0].astype(f32)
    value = (g * jax.nn.sigmoid(g) * up[0].astype(f32)).astype(bf16)
    for f in range(flight):
        for v in range(ways):
            at = (f * ways + v) * slots
            hidden[v, f] = value[at : at + slots]
    for copy in copies[2:]:
        copy.wait()
    diagonal = lax.broadcasted_iota(jnp.int32, (slots, slots), 0) == lax.broadcasted_iota(
        jnp.int32, (slots, slots), 1
    )
    row = lax.broadcasted_iota(jnp.int32, (slots, 1), 0)
    for f in range(flight):
        weight = jnp.sum(
            jnp.where(diagonal, jnp.broadcast_to(router[0, f : f + 1, :], (slots, slots)), 0.0),
            axis=1,
            keepdims=True,
        )
        live = row < counts[0, f]
        scaled = jnp.where(live, weight * rows[0, f].astype(f32), 0.0).astype(bf16)
        for i in range(pieces):
            out[i, f] = scaled[:, i * piece : (i + 1) * piece]


def update_kernel(ways, pieces, start, stop, last, place, *refs):
    refs = list(refs)

    def take(count):
        taken = refs[:count]
        del refs[:count]
        return taken

    rows = take(ways)
    opening = start == 0
    if opening:
        hiddens = take(pieces)
        state = take(3)
    else:
        right, carried = take(2)
        state = take(3)
        take(3)
    outs = take(3)
    (fresh,) = take(1)
    if opening and not last:
        right, total = take(2)
    if last:
        parts = take(pieces)
    if opening and last:
        (right,) = take(1)
    held, gradient, old, new, sems_in, sems_out = refs
    me, lane = place[0], place[1]
    high = stop - start
    tile = tile_rows(high)
    steps = high // tile
    ins = []
    for t in range(steps):
        for n in range(3):
            copy = pltpu.make_async_copy(
                state[n].at[pl.ds(start + t * tile, tile)],
                old.at[n, pl.ds(t * tile, tile)],
                sems_in.at[n, t],
            )
            copy.start()
            ins.append(copy)
    across = fresh.shape[1]
    count = rows[0].shape[0] * rows[0].shape[1]
    group = count // pieces
    if opening:
        for d in range(pieces):
            for v in range(ways):
                right[v, pl.ds((me ^ d) * group, group)] = hiddens[d][v].reshape(group, across)
    left = jnp.concatenate([rows[d][...].reshape(count, high) for d in range(ways)], axis=0)
    hidden = jnp.concatenate([right[lane ^ d] for d in range(ways)], axis=0)
    gradient[...] = lax.dot_general(
        left, hidden, (((0,), (0,)), ((), ())), preferred_element_type=f32
    )
    backs = []
    for t in range(steps):
        for n in range(3):
            ins[3 * t + n].wait()
        at = pl.ds(t * tile, tile)
        grad = gradient[at]
        master = old[0, at]
        moment_a = beta_one * old[1, at] + (1.0 - beta_one) * grad
        moment_b = beta_two * old[2, at] + (1.0 - beta_two) * grad * grad
        step_size = (moment_a * (1.0 / (1.0 - beta_one**5))) / (
            jnp.sqrt(moment_b * (1.0 / (1.0 - beta_two**5))) + epsilon
        )
        updated = master - learning_rate * (step_size + decay_rate * master)
        fresh[at] = updated.astype(bf16)
        new[0, at] = updated
        new[1, at] = moment_a
        new[2, at] = moment_b
        for n in range(3):
            copy = pltpu.make_async_copy(
                new.at[n, at], outs[n].at[pl.ds(start + t * tile, tile)], sems_out.at[n, t]
            )
            copy.start()
            backs.append(copy)
    share = jnp.dot(left, old[0].astype(bf16), preferred_element_type=f32)
    for d in range(ways):
        held[lane ^ d] = share[d * count : (d + 1) * count]
    if last:
        for d in range(pieces):
            at = pl.ds((me ^ d) * group, group)
            value = held[:, at]
            if not opening:
                value = value + carried[:, at]
            parts[d][...] = value.astype(parts[d].dtype)
    else:
        total[...] = held[...]
    for copy in backs:
        copy.wait()


def gate_kernel(ways, pieces, gate, up, *refs):
    parts = refs[:pieces]
    d_gate, d_up = refs[pieces:]
    total = parts[0][...]
    for part in parts[1:]:
        total = total + part[...].astype(f32)
    group = total.shape[1]
    flight = gate.shape[1] // (ways * 16)
    slots = group // flight
    for f in range(flight):
        for v in range(ways):
            at = pl.ds((f * ways + v) * slots, slots)
            grad = total[v, f * slots : (f + 1) * slots]
            g = gate[0, at].astype(f32)
            u = up[0, at].astype(f32)
            sig = jax.nn.sigmoid(g)
            d_gate[0, at] = (grad * u * sig * (1.0 + g * (1.0 - sig))).astype(bf16)
            d_up[0, at] = (grad * (g * sig)).astype(bf16)


def join_kernel(high, spans, pieces, place, *refs):
    out = refs[len(spans) * pieces]
    sems = refs[len(spans) * pieces + 1]
    me = place[0]
    copies = []
    for c, (start, stop) in enumerate(spans):
        for d in range(pieces):
            n = c * pieces + d
            at = pl.multiple_of((me ^ d) * high + start, 16)
            copy = pltpu.make_async_copy(refs[n], out.at[pl.ds(at, stop - start)], sems.at[n])
            copy.start()
            copies.append(copy)
    for copy in copies:
        copy.wait()


def whole(memory=pltpu.VMEM):
    return pl.BlockSpec(memory_space=memory)


def local(
    grad_rows,
    router_weight,
    send_counts,
    gate_stash,
    up_stash,
    master_weight,
    first_moment,
    second_moment,
):
    _, flight, slots, width = grad_rows.shape
    pieces = lax.axis_size("dp")
    sources = lax.axis_size("expert")
    ways = sources // flight
    high, across = master_weight.shape
    me = lax.axis_index("dp")
    lane = lax.axis_index("expert") % ways
    place = jnp.stack([me, lane]).astype(jnp.int32)
    smem = whole(pltpu.SMEM)
    hbm = whole(pltpu.HBM)

    def pinned(x):
        return pltpu.with_memory_space_constraint(x, pltpu.HBM)

    def over_dp(x, d):
        return lax.ppermute(x, "dp", [(i, i ^ d) for i in range(pieces)])

    out, hidden = pl.pallas_call(
        scale_kernel,
        out_shape=(
            jax.ShapeDtypeStruct((pieces, flight, slots, high), bf16),
            jax.ShapeDtypeStruct((ways, flight, slots, across), bf16),
        ),
        in_specs=[hbm] * 5,
        out_specs=[whole()] * 2,
        scratch_shapes=[
            pltpu.SMEM(send_counts.shape, jnp.int32),
            pltpu.VMEM(router_weight.shape, f32),
            pltpu.VMEM(grad_rows.shape, bf16),
            pltpu.VMEM(gate_stash.shape, bf16),
            pltpu.VMEM(up_stash.shape, bf16),
            pltpu.SemaphoreType.DMA((5,)),
        ],
        compiler_params=params(),
        name="scale",
    )(
        pinned(send_counts),
        pinned(router_weight),
        pinned(grad_rows),
        pinned(gate_stash),
        pinned(up_stash),
    )
    hiddens = [hidden] + [over_dp(hidden, d) for d in range(1, pieces)]

    groups = [
        [i * sources + g * ways + v for i in range(pieces) for g in range(flight)]
        for v in range(ways)
    ]
    mine = lax.all_to_all(
        out.reshape(pieces * flight, slots, high),
        ("dp", "expert"),
        split_axis=0,
        concat_axis=0,
        axis_index_groups=groups,
        tiled=True,
    )
    spans = chunks_of(high)
    count = pieces * flight * slots
    group = flight * slots
    state = [pinned(master_weight), pinned(first_moment), pinned(second_moment)]
    states = [jax.ShapeDtypeStruct((high, across), f32)] * 3
    fresh = []
    carried = None
    for start, stop in spans:
        opening, last = start == 0, stop == high
        tall = stop - start
        piece = mine[:, :, start:stop]
        rows = [piece] + [
            lax.ppermute(piece, "expert", [(k, k ^ d) for k in range(sources)])
            for d in range(1, ways)
        ]
        operands = [place] + rows
        in_specs = [smem] + [whole()] * ways
        if opening:
            operands += hiddens + state
            in_specs += [whole()] * pieces + [hbm] * 3
            aliases = {}
        else:
            operands += [right, carried] + state + list(news)
            in_specs += [whole()] * 2 + [hbm] * 6
            aliases = {len(operands) - 3 + n: n for n in range(3)}
        out_shape = states + [jax.ShapeDtypeStruct((tall, across), bf16)]
        out_specs = [hbm] * 3 + [whole()]
        scratch = []
        if opening and not last:
            out_shape += [
                jax.ShapeDtypeStruct((ways, count, across), bf16),
                jax.ShapeDtypeStruct((ways, count, across), f32),
            ]
            out_specs += [whole()] * 2
        if last:
            out_shape += [
                jax.ShapeDtypeStruct((ways, group, across), bf16 if d else f32)
                for d in range(pieces)
            ]
            out_specs += [whole()] * pieces
        if opening and last:
            scratch += [pltpu.VMEM((ways, count, across), bf16)]
        steps = tall // tile_rows(tall)
        results = pl.pallas_call(
            functools.partial(update_kernel, ways, pieces, start, stop, last),
            out_shape=out_shape,
            in_specs=in_specs,
            out_specs=out_specs,
            input_output_aliases=aliases,
            scratch_shapes=scratch
            + [
                pltpu.VMEM((ways, count, across), f32),
                pltpu.VMEM((tall, across), f32),
                pltpu.VMEM((3, tall, across), f32),
                pltpu.VMEM((3, tall, across), f32),
                pltpu.SemaphoreType.DMA((3, steps)),
                pltpu.SemaphoreType.DMA((3, steps)),
            ],
            compiler_params=params(),
            cost_estimate=cost(4 * ways * count * tall * across, tall * across * 26),
            name="update",
        )(*operands)
        news = results[:3]
        shards = {0: results[3]}
        if opening and not last:
            right, carried = results[4:]
        if last:
            parts = results[4:]
        bit = pieces // 2
        while bit:
            for d in list(shards):
                shards[d ^ bit] = over_dp(shards[d], bit)
            bit //= 2
        fresh += [shards[d] for d in range(pieces)]

    arrived = [parts[0]] + [over_dp(parts[d], d) for d in range(1, pieces)]
    d_gate, d_up = pl.pallas_call(
        functools.partial(gate_kernel, ways, pieces),
        out_shape=[jax.ShapeDtypeStruct(gate_stash.shape, bf16)] * 2,
        in_specs=[whole()] * (2 + pieces),
        out_specs=[whole()] * 2,
        compiler_params=params(),
        name="gates",
    )(gate_stash, up_stash, *arrived)

    joined = pl.pallas_call(
        functools.partial(join_kernel, high, spans, pieces),
        out_shape=jax.ShapeDtypeStruct((pieces * high, across), bf16),
        in_specs=[smem] + [whole(pl.ANY)] * len(fresh),
        out_specs=hbm,
        scratch_shapes=[pltpu.SemaphoreType.DMA((len(fresh),))],
        compiler_params=params(),
        name="join",
    )(place, *fresh)
    return (d_gate, d_up, *news, joined)


def solution(mesh):
    placed = (
        P("dp", "expert", None, None),
        P("dp", "expert", None),
        P("dp", "expert"),
        P("dp", None, "expert"),
        P("dp", None, "expert"),
        P("dp", "expert"),
        P("dp", "expert"),
        P("dp", "expert"),
    )
    return jax.shard_map(
        local,
        mesh=mesh,
        in_specs=placed,
        out_specs=(
            P("dp", None, "expert"),
            P("dp", None, "expert"),
            P("dp", "expert"),
            P("dp", "expert"),
            P("dp", "expert"),
            P(None, "expert"),
        ),
        check_vma=False,
    )
```

```python
import functools

import jax
import jax.numpy as jnp
from jax import lax
from jax.experimental import pallas as pl
from jax.experimental.pallas import tpu as pltpu
from jax.sharding import PartitionSpec as P

learning_rate = 0.01
beta_one = 0.9
beta_two = 0.95
decay_rate = 0.1
epsilon = 1e-08

bf16 = jnp.bfloat16
f32 = jnp.float32
VMEM_LIMIT = 40 * 1024 * 1024
LANES = 128


def params():
    return pltpu.CompilerParams(vmem_limit_bytes=VMEM_LIMIT)


def cost(flops, nbytes):
    return pl.CostEstimate(flops=flops, bytes_accessed=nbytes, transcendentals=0)


def take(refs, count):
    taken = refs[:count]
    del refs[:count]
    return taken


def wide(tiles):
    return tiles[0] if len(tiles) == 1 else jnp.concatenate(tiles, axis=1)


def tall(blocks):
    return blocks[0] if len(blocks) == 1 else jnp.concatenate(blocks, axis=0)


def scale_kernel(pieces, place, *refs):
    refs = list(refs)
    sources = take(refs, 5)
    scratch = refs[-7:]
    outs = refs[:-7]
    targets, cut, sems = scratch[:5], scratch[5], scratch[6]
    copies = [
        pltpu.make_async_copy(source, target, sems.at[n])
        for n, (source, target) in enumerate(zip(sources, targets))
    ]
    for n in (2, 0, 1, 3, 4):
        copies[n].start()
    counts, router, rows, gate, up = targets
    flight, slots, width = rows.shape[1:]
    high = width // pieces
    tiles = cut.shape[2]
    me, own = place[0], place[2]
    if tiles * LANES != high:
        cut[...] = jnp.zeros_like(cut)
    for n in range(3):
        copies[n].wait()
    diagonal = lax.broadcasted_iota(jnp.int32, (slots, slots), 0) == lax.broadcasted_iota(
        jnp.int32, (slots, slots), 1
    )
    row = lax.broadcasted_iota(jnp.int32, (slots, 1), 0)
    for f in range(flight):
        weight = jnp.sum(
            jnp.where(diagonal, jnp.broadcast_to(router[0, f : f + 1, :], (slots, slots)), 0.0),
            axis=1,
            keepdims=True,
        )
        live = row < counts[0, f]
        scaled = jnp.where(live, weight * rows[0, f].astype(f32), 0.0).astype(bf16)
        for i in range(pieces):
            for t in range(tiles):
                low, end = t * LANES, min((t + 1) * LANES, high)
                cut[i, f, t, :, : end - low] = scaled[:, i * high + low : i * high + end]
    for n in (3, 4):
        copies[n].wait()
    g = gate[0].astype(f32)
    hidden = (g * jax.nn.sigmoid(g) * up[0].astype(f32)).astype(bf16)
    across = hidden.shape[1]
    columns = across // LANES
    for dj in range(pieces):
        for dg in range(flight):
            out = outs[dj * flight + dg]
            out[:tiles] = cut[me ^ dj, own ^ dg]
            if dg == 0:
                for n in range(hidden.shape[0] // slots):
                    for c in range(columns):
                        out[tiles + n * columns + c] = hidden[
                            n * slots : (n + 1) * slots, c * LANES : (c + 1) * LANES
                        ]


def pack_kernel(cuts, *refs):
    blocks, outs = refs[: -len(cuts)], refs[-len(cuts) :]
    slots = blocks[0].shape[1]
    for (low, end), out in zip(cuts, outs):
        for t in range(low, end):
            for n, block in enumerate(blocks):
                out[t - low, n * slots : (n + 1) * slots] = block[t]


def fetch_kernel(ways, tiles, place, *refs):
    refs = list(refs)
    state = take(refs, 3)
    bundles = refs[:-5]
    outs, right, sems = refs[-5:-2], refs[-2], refs[-1]
    copies = [pltpu.make_async_copy(state[n], outs[n], sems.at[n]) for n in range(3)]
    for copy in copies:
        copy.start()
    lane, own = place[1], place[2]
    slots = bundles[0].shape[1]
    columns = right.shape[2] // LANES
    pieces = len(bundles)
    flight = right.shape[1] // (pieces * slots)
    for d in range(ways):
        for dj in range(pieces):
            for dg in range(flight):
                at = (dj * flight + dg) * slots
                source = (own ^ dg) * ways + (lane ^ d)
                for c in range(columns):
                    right[d, at : at + slots, c * LANES : (c + 1) * LANES] = bundles[dj][
                        tiles + source * columns + c
                    ]
    for copy in copies:
        copy.wait()


def update_kernel(ways, start, stop, *refs):
    refs = list(refs)
    rows = take(refs, ways)
    right, master, first, second = take(refs, 4)
    fresh, new_master, new_first, new_second, gradient = refs
    left = tall([wide([block[t] for t in range(block.shape[0])]) for block in rows])
    hidden = tall([right[d] for d in range(ways)])
    gradient[...] = lax.dot_general(
        left, hidden, (((0,), (0,)), ((), ())), preferred_element_type=f32
    )
    for low in range(start, stop, 128):
        end = min(low + 128, stop)
        here = pl.ds(low, end - low)
        there = pl.ds(low - start, end - low)
        grad = gradient[there]
        old = master[here]
        moment_a = beta_one * first[here] + (1.0 - beta_one) * grad
        moment_b = beta_two * second[here] + (1.0 - beta_two) * grad * grad
        step_size = (moment_a * (1.0 / (1.0 - beta_one**5))) / (
            jnp.sqrt(moment_b * (1.0 / (1.0 - beta_two**5))) + epsilon
        )
        updated = old - learning_rate * (step_size + decay_rate * old)
        fresh[there] = updated.astype(bf16)
        new_master[there] = updated
        new_first[there] = moment_a
        new_second[there] = moment_b


def store_kernel(ways, spans, place, *refs):
    refs = list(refs)
    parts_in = len(spans)
    rows = take(refs, ways * parts_in)
    news = take(refs, 3 * parts_in)
    fresh = take(refs, parts_in)
    (master,) = take(refs, 1)
    outs = take(refs, 3)
    own_fresh, sems = refs[-2], refs[-1]
    parts = refs[:-2]
    copies = []
    for c, (start, stop) in enumerate(spans):
        for n in range(3):
            copy = pltpu.make_async_copy(
                news[3 * c + n], outs[n].at[pl.ds(start, stop - start)], sems.at[c, n]
            )
            copy.start()
            copies.append(copy)
    lane, own = place[1], place[2]
    high = master.shape[0]
    flight, slots = parts[0].shape[1:3]
    current = master[...].astype(bf16)
    for d in range(ways):
        blocks = [rows[c * ways + d] for c in range(parts_in)]
        left = wide([block[t] for block in blocks for t in range(block.shape[0])])
        share = jnp.dot(left[:, :high], current, preferred_element_type=f32)
        for dj, part in enumerate(parts):
            for dg in range(flight):
                at = (dj * flight + dg) * slots
                part[lane ^ d, own ^ dg] = share[at : at + slots].astype(part.dtype)
    for c, (start, stop) in enumerate(spans):
        own_fresh[start:stop] = fresh[c][...]
    for copy in copies:
        copy.wait()


def gate_kernel(gate, up, *refs):
    parts = refs[:-2]
    d_gate, d_up = refs[-2:]
    total = parts[0][...]
    for part in parts[1:]:
        total = total + part[...].astype(f32)
    ways, flight, slots = total.shape[:3]
    for f in range(flight):
        for v in range(ways):
            at = pl.ds((f * ways + v) * slots, slots)
            grad = total[v, f]
            g = gate[0, at].astype(f32)
            u = up[0, at].astype(f32)
            sig = jax.nn.sigmoid(g)
            d_gate[0, at] = (grad * u * sig * (1.0 + g * (1.0 - sig))).astype(bf16)
            d_up[0, at] = (grad * (g * sig)).astype(bf16)


def join_kernel(high, entries, place, *refs):
    out, sems = refs[len(entries)], refs[len(entries) + 1]
    me = place[0]
    copies = []
    for n, (d, start, stop) in enumerate(entries):
        at = pl.multiple_of((me ^ d) * high + start, 16)
        copy = pltpu.make_async_copy(refs[n], out.at[pl.ds(at, stop - start)], sems.at[n])
        copy.start()
        copies.append(copy)
    for copy in copies:
        copy.wait()


def whole(memory=pltpu.VMEM):
    return pl.BlockSpec(memory_space=memory)


def shape(dims, kind):
    return jax.ShapeDtypeStruct(dims, kind)


def pinned(x):
    return pltpu.with_memory_space_constraint(x, pltpu.HBM)


def local(
    grad_rows,
    router_weight,
    send_counts,
    gate_stash,
    up_stash,
    master_weight,
    first_moment,
    second_moment,
):
    _, flight, slots, width = grad_rows.shape
    pieces = lax.axis_size("dp")
    sources = lax.axis_size("expert")
    ways = sources // flight
    high, across = master_weight.shape
    me = lax.axis_index("dp")
    seat = lax.axis_index("expert")
    place = jnp.stack([me, seat % ways, seat // ways]).astype(jnp.int32)
    smem = whole(pltpu.SMEM)
    hbm = whole(pltpu.HBM)
    tiles = -(-high // LANES)
    carried = tiles + sources * (across // LANES)
    count = pieces * flight * slots

    def over_dp(x, d):
        return lax.ppermute(x, "dp", [(i, i ^ d) for i in range(pieces)])

    offsets = [(dj, dg) for dj in range(pieces) for dg in range(flight)]
    blocks = pl.pallas_call(
        functools.partial(scale_kernel, pieces),
        out_shape=[shape((tiles if dg else carried, slots, LANES), bf16) for _, dg in offsets],
        in_specs=[smem] + [hbm] * 5,
        out_specs=[whole()] * len(offsets),
        scratch_shapes=[
            pltpu.SMEM(send_counts.shape, jnp.int32),
            pltpu.VMEM(router_weight.shape, f32),
            pltpu.VMEM(grad_rows.shape, bf16),
            pltpu.VMEM(gate_stash.shape, bf16),
            pltpu.VMEM(up_stash.shape, bf16),
            pltpu.VMEM((pieces, flight, tiles, slots, LANES), bf16),
            pltpu.SemaphoreType.DMA((5,)),
        ],
        compiler_params=params(),
        name="scale",
    )(
        place,
        pinned(send_counts),
        pinned(router_weight),
        pinned(grad_rows),
        pinned(gate_stash),
        pinned(up_stash),
    )
    here = []
    for (dj, dg), block in zip(offsets, blocks):
        if dj or dg:
            step = dg * ways
            pairs = [
                (i * sources + k, (i ^ dj) * sources + (k ^ step))
                for i in range(pieces)
                for k in range(sources)
            ]
            block = lax.ppermute(block, ("dp", "expert"), pairs)
        here.append(block)

    cut = (tiles + 1) // 2
    cuts = [(0, cut), (cut, tiles)] if cut < tiles else [(0, tiles)]
    spans = [(low * LANES, min(end * LANES, high)) for low, end in cuts]
    mine = pl.pallas_call(
        functools.partial(pack_kernel, cuts),
        out_shape=[shape((end - low, count, LANES), bf16) for low, end in cuts],
        in_specs=[whole()] * len(here),
        out_specs=[whole()] * len(cuts),
        compiler_params=params(),
        name="pack",
    )(*here)
    rows = [
        [piece]
        + [
            lax.ppermute(piece, "expert", [(k, k ^ d) for k in range(sources)])
            for d in range(1, ways)
        ]
        for piece in mine
    ]

    bundles = [here[dj * flight] for dj in range(pieces)]
    *state, right = pl.pallas_call(
        functools.partial(fetch_kernel, ways, tiles),
        out_shape=[shape((high, across), f32)] * 3 + [shape((ways, count, across), bf16)],
        in_specs=[smem] + [hbm] * 3 + [whole()] * pieces,
        out_specs=[whole()] * 4,
        scratch_shapes=[pltpu.SemaphoreType.DMA((3,))],
        compiler_params=params(),
        cost_estimate=cost(0, high * across * 24),
        name="fetch",
    )(place, pinned(master_weight), pinned(first_moment), pinned(second_moment), *bundles)

    fresh, news = [], []
    for (start, stop), chunk in zip(spans, rows):
        out = pl.pallas_call(
            functools.partial(update_kernel, ways, start, stop),
            out_shape=[shape((stop - start, across), bf16)]
            + [shape((stop - start, across), f32)] * 3,
            in_specs=[whole()] * (ways + 4),
            out_specs=[whole()] * 4,
            scratch_shapes=[pltpu.VMEM((chunk[0].shape[0] * LANES, across), f32)],
            compiler_params=params(),
            cost_estimate=cost(2 * ways * count * (stop - start) * across, high * across * 26),
            name="update",
        )(*chunk, right, *state)
        fresh.append(out[0])
        news += out[1:]

    new_master, new_first, new_second, *rest = pl.pallas_call(
        functools.partial(store_kernel, ways, spans),
        out_shape=[shape((high, across), f32)] * 3
        + [shape((ways, flight, slots, across), bf16 if d else f32) for d in range(pieces)]
        + [shape((high, across), bf16)],
        in_specs=[smem] + [whole()] * ((ways + 4) * len(spans) + 1),
        out_specs=[hbm] * 3 + [whole()] * (pieces + 1),
        scratch_shapes=[pltpu.SemaphoreType.DMA((len(spans), 3))],
        compiler_params=params(),
        cost_estimate=cost(2 * ways * count * high * across, high * across * 24),
        name="store",
    )(place, *[block for chunk in rows for block in chunk], *news, *fresh, state[0])
    parts, own_fresh = rest[:-1], rest[-1]

    bit = pieces // 2
    if len(spans) > 1:
        fresh[0], _ = lax.optimization_barrier((fresh[0], rows[-1]))
    crossed = [over_dp(piece, bit) for piece in fresh]
    arrived = [over_dp(parts[d], d) for d in range(1, pieces)]
    crossed[-1], arrived = lax.optimization_barrier((crossed[-1], arrived))
    d_gate, d_up = pl.pallas_call(
        gate_kernel,
        out_shape=[shape(gate_stash.shape, bf16)] * 2,
        in_specs=[whole()] * (2 + pieces),
        out_specs=[whole()] * 2,
        compiler_params=params(),
        name="gates",
    )(gate_stash, up_stash, parts[0], *arrived)

    entries = [(0, 0, high, own_fresh)] + [
        (bit, start, stop, piece) for (start, stop), piece in zip(spans, crossed)
    ]
    while bit > 1:
        bit //= 2
        entries += [(d ^ bit, start, stop, over_dp(piece, bit)) for d, start, stop, piece in entries]
    joined = pl.pallas_call(
        functools.partial(join_kernel, high, [entry[:3] for entry in entries]),
        out_shape=shape((pieces * high, across), bf16),
        in_specs=[smem] + [whole(pl.ANY)] * len(entries),
        out_specs=hbm,
        scratch_shapes=[pltpu.SemaphoreType.DMA((len(entries),))],
        compiler_params=params(),
        name="join",
    )(place, *[entry[3] for entry in entries])
    return (d_gate, d_up, new_master, new_first, new_second, joined)


def solution(mesh):
    placed = (
        P("dp", "expert", None, None),
        P("dp", "expert", None),
        P("dp", "expert"),
        P("dp", None, "expert"),
        P("dp", None, "expert"),
        P("dp", "expert"),
        P("dp", "expert"),
        P("dp", "expert"),
    )
    return jax.shard_map(
        local,
        mesh=mesh,
        in_specs=placed,
        out_specs=(
            P("dp", None, "expert"),
            P("dp", None, "expert"),
            P("dp", "expert"),
            P("dp", "expert"),
            P("dp", "expert"),
            P(None, "expert"),
        ),
        check_vma=False,
    )
```

```python
import functools

import jax
import jax.numpy as jnp
from jax import lax
from jax.experimental import pallas as pl
from jax.experimental.pallas import tpu as pltpu
from jax.sharding import PartitionSpec as P

learning_rate = 0.01
beta_one = 0.9
beta_two = 0.95
decay_rate = 0.1
epsilon = 1e-08

bf16 = jnp.bfloat16
f32 = jnp.float32
VMEM_LIMIT = 40 * 1024 * 1024
LANES = 128


def params():
    return pltpu.CompilerParams(vmem_limit_bytes=VMEM_LIMIT)


def cost(flops, nbytes):
    return pl.CostEstimate(flops=flops, bytes_accessed=nbytes, transcendentals=0)


def take(refs, count):
    taken = refs[:count]
    del refs[:count]
    return taken


def wide(tiles):
    return tiles[0] if len(tiles) == 1 else jnp.concatenate(tiles, axis=1)


def tall(blocks):
    return blocks[0] if len(blocks) == 1 else jnp.concatenate(blocks, axis=0)


def scale_kernel(counts_in, router_in, rows_in, gate_in, up_in, out, hidden, *scratch):
    counts, router, rows, gate, up, sems = scratch
    copies = [
        pltpu.make_async_copy(source, target, sems.at[n])
        for n, (source, target) in enumerate(
            [
                (gate_in, gate),
                (up_in, up),
                (counts_in, counts),
                (router_in, router),
                (rows_in, rows),
            ]
        )
    ]
    for copy in copies:
        copy.start()
    flight, slots, width = rows.shape[1:]
    pieces = out.shape[0]
    piece = width // pieces
    ways = hidden.shape[0]
    copies[0].wait()
    copies[1].wait()
    g = gate[0].astype(f32)
    value = (g * jax.nn.sigmoid(g) * up[0].astype(f32)).astype(bf16)
    for f in range(flight):
        for v in range(ways):
            at = (f * ways + v) * slots
            hidden[v, f] = value[at : at + slots]
    for copy in copies[2:]:
        copy.wait()
    diagonal = lax.broadcasted_iota(jnp.int32, (slots, slots), 0) == lax.broadcasted_iota(
        jnp.int32, (slots, slots), 1
    )
    row = lax.broadcasted_iota(jnp.int32, (slots, 1), 0)
    for f in range(flight):
        weight = jnp.sum(
            jnp.where(diagonal, jnp.broadcast_to(router[0, f : f + 1, :], (slots, slots)), 0.0),
            axis=1,
            keepdims=True,
        )
        live = row < counts[0, f]
        scaled = jnp.where(live, weight * rows[0, f].astype(f32), 0.0).astype(bf16)
        for i in range(pieces):
            out[i, f] = scaled[:, i * piece : (i + 1) * piece]


def fetch_kernel(place, *refs):
    refs = list(refs)
    state = take(refs, 3)
    hiddens = refs[:-5]
    outs, right, sems = refs[-5:-2], refs[-2], refs[-1]
    copies = [pltpu.make_async_copy(state[n], outs[n], sems.at[n]) for n in range(3)]
    for copy in copies:
        copy.start()
    me, lane = place[0], place[1]
    ways, flight, slots, across = hiddens[0].shape
    group = flight * slots
    for d in range(ways):
        for dj, hidden in enumerate(hiddens):
            at = pl.multiple_of((me ^ dj) * group, group)
            right[d, pl.ds(at, group)] = hidden[lane ^ d].reshape(group, across)
    for copy in copies:
        copy.wait()


def update_kernel(ways, start, stop, *refs):
    refs = list(refs)
    rows = take(refs, ways)
    right, master, first, second = take(refs, 4)
    fresh, new_master, new_first, new_second, gradient = refs
    left = tall([block[...].reshape(-1, stop - start) for block in rows])
    hidden = tall([right[d] for d in range(ways)])
    gradient[...] = lax.dot_general(
        left, hidden, (((0,), (0,)), ((), ())), preferred_element_type=f32
    )
    for low in range(start, stop, 128):
        end = min(low + 128, stop)
        here = pl.ds(low, end - low)
        there = pl.ds(low - start, end - low)
        grad = gradient[there]
        old = master[here]
        moment_a = beta_one * first[here] + (1.0 - beta_one) * grad
        moment_b = beta_two * second[here] + (1.0 - beta_two) * grad * grad
        step_size = (moment_a * (1.0 / (1.0 - beta_one**5))) / (
            jnp.sqrt(moment_b * (1.0 / (1.0 - beta_two**5))) + epsilon
        )
        updated = old - learning_rate * (step_size + decay_rate * old)
        fresh[there] = updated.astype(bf16)
        new_master[there] = updated
        new_first[there] = moment_a
        new_second[there] = moment_b


def partial_kernel(ways, spans, kept, place, *refs):
    refs = list(refs)
    rows = take(refs, ways * len(spans))
    fresh = take(refs, len(spans))
    master, keep, send, own_fresh, held = refs
    me, lane = place[0], place[1]
    current = master[...].astype(bf16)
    _, flight, slots, across = keep.shape[1:]
    group = flight * slots
    for d in range(ways):
        blocks = [rows[c * ways + d] for c in range(len(spans))]
        left = wide([block[...].reshape(-1, block.shape[2]) for block in blocks])
        held[lane ^ d] = jnp.dot(left, current, preferred_element_type=f32)
    for out, chosen in ((keep, kept[0]), (send, kept[1])):
        for n, d in enumerate(chosen):
            at = pl.multiple_of((me ^ d) * group, group)
            value = held[:, pl.ds(at, group)]
            out[n] = value.reshape(ways, flight, slots, across).astype(out.dtype)
    for c, (start, stop) in enumerate(spans):
        own_fresh[start:stop] = fresh[c][...]


def halve_kernel(kept, held, arrived, keep, send):
    for out, chosen in ((keep, kept[0]), (send, kept[1])):
        for n, m in enumerate(chosen):
            out[n] = (held[m] + arrived[m].astype(f32)).astype(out.dtype)


def store_kernel(spans, *refs):
    refs = list(refs)
    news = take(refs, 3 * len(spans))
    outs = take(refs, 3)
    (sems,) = refs
    copies = []
    for c, (start, stop) in enumerate(spans):
        for n in range(3):
            copy = pltpu.make_async_copy(
                news[3 * c + n], outs[n].at[pl.ds(start, stop - start)], sems.at[c, n]
            )
            copy.start()
            copies.append(copy)
    for copy in copies:
        copy.wait()


def gate_kernel(gate, up, held, arrived, d_gate, d_up):
    ways, flight, slots = held.shape[1:4]
    for f in range(flight):
        for v in range(ways):
            at = pl.ds((f * ways + v) * slots, slots)
            grad = held[0, v, f] + arrived[0, v, f].astype(f32)
            g = gate[0, at].astype(f32)
            u = up[0, at].astype(f32)
            sig = jax.nn.sigmoid(g)
            d_gate[0, at] = (grad * u * sig * (1.0 + g * (1.0 - sig))).astype(bf16)
            d_up[0, at] = (grad * (g * sig)).astype(bf16)


def join_kernel(high, entries, place, *refs):
    out, sems = refs[-2], refs[-1]
    me = place[0]
    copies = []
    for n, (d, start, stop) in enumerate(entries):
        at = pl.multiple_of((me ^ d) * high + start, 16)
        copy = pltpu.make_async_copy(refs[n], out.at[pl.ds(at, stop - start)], sems.at[n])
        copy.start()
        copies.append(copy)
    for copy in copies:
        copy.wait()


def whole(memory=pltpu.VMEM):
    return pl.BlockSpec(memory_space=memory)


def shape(dims, kind):
    return jax.ShapeDtypeStruct(dims, kind)


def pinned(x):
    return pltpu.with_memory_space_constraint(x, pltpu.HBM)


def local(
    grad_rows,
    router_weight,
    send_counts,
    gate_stash,
    up_stash,
    master_weight,
    first_moment,
    second_moment,
):
    _, flight, slots, width = grad_rows.shape
    pieces = lax.axis_size("dp")
    sources = lax.axis_size("expert")
    ways = sources // flight
    high, across = master_weight.shape
    me = lax.axis_index("dp")
    seat = lax.axis_index("expert")
    place = jnp.stack([me, seat % ways]).astype(jnp.int32)
    smem = whole(pltpu.SMEM)
    hbm = whole(pltpu.HBM)
    count = pieces * flight * slots

    def over_dp(x, d):
        return lax.ppermute(x, "dp", [(i, i ^ d) for i in range(pieces)])

    cut, hidden = pl.pallas_call(
        scale_kernel,
        out_shape=(
            shape((pieces, flight, slots, high), bf16),
            shape((ways, flight, slots, across), bf16),
        ),
        in_specs=[hbm] * 5,
        out_specs=[whole()] * 2,
        scratch_shapes=[
            pltpu.SMEM(send_counts.shape, jnp.int32),
            pltpu.VMEM(router_weight.shape, f32),
            pltpu.VMEM(grad_rows.shape, bf16),
            pltpu.VMEM(gate_stash.shape, bf16),
            pltpu.VMEM(up_stash.shape, bf16),
            pltpu.SemaphoreType.DMA((5,)),
        ],
        compiler_params=params(),
        name="scale",
    )(
        pinned(send_counts),
        pinned(router_weight),
        pinned(grad_rows),
        pinned(gate_stash),
        pinned(up_stash),
    )
    groups = [
        [i * sources + g * ways + v for i in range(pieces) for g in range(flight)]
        for v in range(ways)
    ]
    mine = lax.all_to_all(
        cut.reshape(pieces * flight, slots, high),
        ("dp", "expert"),
        split_axis=0,
        concat_axis=0,
        axis_index_groups=groups,
        tiled=True,
    )
    hiddens = [hidden] + [over_dp(hidden, d) for d in range(1, pieces)]
    *state, right = pl.pallas_call(
        fetch_kernel,
        out_shape=[shape((high, across), f32)] * 3 + [shape((ways, count, across), bf16)],
        in_specs=[smem] + [hbm] * 3 + [whole()] * pieces,
        out_specs=[whole()] * 4,
        scratch_shapes=[pltpu.SemaphoreType.DMA((3,))],
        compiler_params=params(),
        cost_estimate=cost(0, high * across * 24),
        name="fetch",
    )(place, pinned(master_weight), pinned(first_moment), pinned(second_moment), *hiddens)
    mine, state, right = lax.optimization_barrier((mine, state, right))

    tiles = -(-high // LANES)
    middle = (tiles + 1) // 2 * LANES
    spans = [(0, middle), (middle, high)] if middle < high else [(0, high)]
    rows = []
    for start, stop in spans:
        piece = mine[:, :, start:stop]
        rows.append(
            [piece]
            + [
                lax.ppermute(piece, "expert", [(k, k ^ d) for k in range(sources)])
                for d in range(1, ways)
            ]
        )

    fresh, news = [], []
    for (start, stop), chunk in zip(spans, rows):
        out = pl.pallas_call(
            functools.partial(update_kernel, ways, start, stop),
            out_shape=[shape((stop - start, across), bf16)]
            + [shape((stop - start, across), f32)] * 3,
            in_specs=[whole()] * (ways + 4),
            out_specs=[whole()] * 4,
            scratch_shapes=[pltpu.VMEM((stop - start, across), f32)],
            compiler_params=params(),
            cost_estimate=cost(2 * ways * count * (stop - start) * across, high * across * 26),
            name="update",
        )(*chunk, right, *state)
        fresh.append(out[0])
        news += out[1:]
    top = pieces // 2
    crossed = [over_dp(piece, top) for piece in fresh]

    part = (ways, flight, slots, across)
    bit = 1
    kept = [[d for d in range(pieces) if not d & bit], [d for d in range(pieces) if d & bit]]
    keep, send, own_fresh = pl.pallas_call(
        functools.partial(partial_kernel, ways, spans, kept),
        out_shape=[
            shape((pieces // 2, *part), f32),
            shape((pieces // 2, *part), bf16),
            shape((high, across), bf16),
        ],
        in_specs=[smem] + [whole()] * ((ways + 1) * len(spans) + 1),
        out_specs=[whole()] * 3,
        scratch_shapes=[pltpu.VMEM((ways, count, across), f32)],
        compiler_params=params(),
        cost_estimate=cost(2 * ways * count * high * across, high * across * 12),
        name="partial",
    )(place, *[block for chunk in rows for block in chunk], *fresh, state[0])
    arrived = over_dp(send, bit)
    while bit < top:
        bit *= 2
        left = kept[0]
        kept = [[d for d in left if not d & bit], [d for d in left if d & bit]]
        chosen = [[left.index(d) for d in half] for half in kept]
        keep, send = pl.pallas_call(
            functools.partial(halve_kernel, chosen),
            out_shape=[
                shape((len(kept[0]), *part), f32),
                shape((len(kept[1]), *part), bf16),
            ],
            in_specs=[whole()] * 2,
            out_specs=[whole()] * 2,
            compiler_params=params(),
            name="halve",
        )(keep, arrived)
        arrived = over_dp(send, bit)
    if len(spans) > 1:
        crossed[0], keep = lax.optimization_barrier((crossed[0], keep))
    d_gate, d_up = pl.pallas_call(
        gate_kernel,
        out_shape=[shape(gate_stash.shape, bf16)] * 2,
        in_specs=[whole()] * 4,
        out_specs=[whole()] * 2,
        compiler_params=params(),
        name="gates",
    )(gate_stash, up_stash, keep, arrived)

    states = pl.pallas_call(
        functools.partial(store_kernel, spans),
        out_shape=[shape((high, across), f32)] * 3,
        in_specs=[whole()] * len(news),
        out_specs=[hbm] * 3,
        scratch_shapes=[pltpu.SemaphoreType.DMA((len(spans), 3))],
        compiler_params=params(),
        cost_estimate=cost(0, high * across * 24),
        name="store",
    )(*news)

    def spread(entries):
        step = top
        while step > 1:
            step //= 2
            entries = entries + [(d ^ step, *span, over_dp(x, step)) for d, *span, x in entries]
        return entries

    def join(entries, before):
        return pl.pallas_call(
            functools.partial(join_kernel, high, [entry[:3] for entry in entries]),
            out_shape=shape((pieces * high, across), bf16),
            in_specs=[smem] + [whole(pl.ANY)] * len(entries) + [hbm] * len(before),
            out_specs=hbm,
            input_output_aliases={len(entries) + 1: 0} if before else {},
            scratch_shapes=[pltpu.SemaphoreType.DMA((len(entries),))],
            compiler_params=params(),
            name="join",
        )(place, *[entry[3] for entry in entries], *before)

    near, *far = spread([(0, 0, high, own_fresh)])
    early, late = [near], far
    for (start, stop), piece in zip(spans[:-1], crossed[:-1]):
        near, *far = spread([(top, start, stop, piece)])
        early.append(near)
        late += far
    joined = join(early, [])
    crossed[-1], joined, states, arrived = lax.optimization_barrier(
        (crossed[-1], joined, states, arrived)
    )
    joined = join(late + spread([(top, *spans[-1], crossed[-1])]), [joined])
    return (d_gate, d_up, *states, joined)


def solution(mesh):
    placed = (
        P("dp", "expert", None, None),
        P("dp", "expert", None),
        P("dp", "expert"),
        P("dp", None, "expert"),
        P("dp", None, "expert"),
        P("dp", "expert"),
        P("dp", "expert"),
        P("dp", "expert"),
    )
    return jax.shard_map(
        local,
        mesh=mesh,
        in_specs=placed,
        out_specs=(
            P("dp", None, "expert"),
            P("dp", None, "expert"),
            P("dp", "expert"),
            P("dp", "expert"),
            P("dp", "expert"),
            P(None, "expert"),
        ),
        check_vma=False,
    )
```

```python
import functools

import jax
import jax.numpy as jnp
from jax import lax
from jax.experimental import pallas as pl
from jax.experimental.pallas import tpu as pltpu
from jax.sharding import PartitionSpec as P

learning_rate = 0.01
beta_one = 0.9
beta_two = 0.95
decay_rate = 0.1
epsilon = 1e-08

bf16 = jnp.bfloat16
f32 = jnp.float32
VMEM_LIMIT = 40 * 1024 * 1024
LANES = 128
STEP = 128


def params():
    return pltpu.CompilerParams(vmem_limit_bytes=VMEM_LIMIT)


def cost(flops, nbytes):
    return pl.CostEstimate(flops=flops, bytes_accessed=nbytes, transcendentals=0)


def take(refs, count):
    taken = refs[:count]
    del refs[:count]
    return taken


def wide(tiles):
    return tiles[0] if len(tiles) == 1 else jnp.concatenate(tiles, axis=1)


def tall(blocks):
    return blocks[0] if len(blocks) == 1 else jnp.concatenate(blocks, axis=0)


def pieces_of(source, target, step, sems, first):
    copies = []
    for low in range(0, source.shape[0], step):
        at = pl.ds(low, min(step, source.shape[0] - low))
        copies.append(
            pltpu.make_async_copy(source.at[at], target.at[at], sems.at[first + len(copies)])
        )
    return copies


def scale_kernel(counts_in, router_in, rows_in, gate_in, up_in, out, hidden, *scratch):
    counts, router, rows, gate, up, sems = scratch
    copies = [
        pltpu.make_async_copy(source, target, sems.at[n])
        for n, (source, target) in enumerate(
            [
                (gate_in, gate),
                (up_in, up),
                (counts_in, counts),
                (router_in, router),
            ]
            + [(rows_in.at[0, f], rows.at[0, f]) for f in range(rows.shape[1])]
        )
    ]
    for copy in copies:
        copy.start()
    flight, slots, width = rows.shape[1:]
    pieces = out.shape[0]
    piece = width // pieces
    ways = hidden.shape[0]
    copies[0].wait()
    copies[1].wait()
    g = gate[0].astype(f32)
    value = (g * jax.nn.sigmoid(g) * up[0].astype(f32)).astype(bf16)
    for f in range(flight):
        for v in range(ways):
            at = (f * ways + v) * slots
            hidden[v, f] = value[at : at + slots]
    for copy in copies[2:]:
        copy.wait()
    diagonal = lax.broadcasted_iota(jnp.int32, (slots, slots), 0) == lax.broadcasted_iota(
        jnp.int32, (slots, slots), 1
    )
    row = lax.broadcasted_iota(jnp.int32, (slots, 1), 0)
    for f in range(flight):
        weight = jnp.sum(
            jnp.where(diagonal, jnp.broadcast_to(router[0, f : f + 1, :], (slots, slots)), 0.0),
            axis=1,
            keepdims=True,
        )
        live = row < counts[0, f]
        scaled = jnp.where(live, weight * rows[0, f].astype(f32), 0.0).astype(bf16)
        for i in range(pieces):
            out[i, f] = scaled[:, i * piece : (i + 1) * piece]


def fetch_kernel(*refs):
    sems = refs[6]
    copies = []
    for source, target in zip(refs[:3], refs[3:6]):
        copies += pieces_of(source, target, STEP, sems, len(copies))
    for copy in copies:
        copy.start()
    for copy in copies:
        copy.wait()


def order_kernel(place, *refs):
    hiddens, right = refs[:-1], refs[-1]
    me, lane = place[0], place[1]
    ways, flight, slots, across = hiddens[0].shape
    group = flight * slots
    for d in range(ways):
        for dj, hidden in enumerate(hiddens):
            at = pl.multiple_of((me ^ dj) * group, group)
            right[d, pl.ds(at, group)] = hidden[lane ^ d].reshape(group, across)


def update_kernel(ways, start, stop, *refs):
    refs = list(refs)
    rows = take(refs, ways)
    right, master, first, second = take(refs, 4)
    fresh, new_master, new_first, new_second, gradient = refs
    left = tall([block[...].reshape(-1, stop - start) for block in rows])
    hidden = tall([right[d] for d in range(ways)])
    gradient[...] = lax.dot_general(
        left, hidden, (((0,), (0,)), ((), ())), preferred_element_type=f32
    )
    for low in range(start, stop, 128):
        end = min(low + 128, stop)
        here = pl.ds(low, end - low)
        there = pl.ds(low - start, end - low)
        grad = gradient[there]
        old = master[here]
        moment_a = beta_one * first[here] + (1.0 - beta_one) * grad
        moment_b = beta_two * second[here] + (1.0 - beta_two) * grad * grad
        step_size = (moment_a * (1.0 / (1.0 - beta_one**5))) / (
            jnp.sqrt(moment_b * (1.0 / (1.0 - beta_two**5))) + epsilon
        )
        updated = old - learning_rate * (step_size + decay_rate * old)
        fresh[there] = updated.astype(bf16)
        new_master[there] = updated
        new_first[there] = moment_a
        new_second[there] = moment_b


def partial_kernel(ways, spans, kept, place, *refs):
    refs = list(refs)
    rows = take(refs, ways * len(spans))
    fresh = take(refs, len(spans))
    master, keep, send, own_fresh, held = refs
    me, lane = place[0], place[1]
    current = master[...].astype(bf16)
    _, flight, slots, across = keep.shape[1:]
    group = flight * slots
    for d in range(ways):
        blocks = [rows[c * ways + d] for c in range(len(spans))]
        left = wide([block[...].reshape(-1, block.shape[2]) for block in blocks])
        held[lane ^ d] = jnp.dot(left, current, preferred_element_type=f32)
    for out, chosen in ((keep, kept[0]), (send, kept[1])):
        for n, d in enumerate(chosen):
            at = pl.multiple_of((me ^ d) * group, group)
            value = held[:, pl.ds(at, group)]
            out[n] = value.reshape(ways, flight, slots, across).astype(out.dtype)
    for c, (start, stop) in enumerate(spans):
        own_fresh[start:stop] = fresh[c][...]


def halve_kernel(kept, held, arrived, keep, send):
    for out, chosen in ((keep, kept[0]), (send, kept[1])):
        for n, m in enumerate(chosen):
            out[n] = (held[m] + arrived[m].astype(f32)).astype(out.dtype)


def store_kernel(spans, *refs):
    refs = list(refs)
    news = take(refs, 3 * len(spans))
    outs = take(refs, 3)
    (sems,) = refs
    copies = []
    for c, (start, stop) in enumerate(spans):
        for n in range(3):
            target = outs[n].at[pl.ds(start, stop - start)]
            copies += pieces_of(news[3 * c + n], target, STEP, sems, len(copies))
    for copy in copies:
        copy.start()
    for copy in copies:
        copy.wait()


def gate_kernel(gate, up, held, arrived, d_gate, d_up):
    ways, flight, slots = held.shape[1:4]
    for f in range(flight):
        for v in range(ways):
            at = pl.ds((f * ways + v) * slots, slots)
            grad = held[0, v, f] + arrived[0, v, f].astype(f32)
            g = gate[0, at].astype(f32)
            u = up[0, at].astype(f32)
            sig = jax.nn.sigmoid(g)
            d_gate[0, at] = (grad * u * sig * (1.0 + g * (1.0 - sig))).astype(bf16)
            d_up[0, at] = (grad * (g * sig)).astype(bf16)


def join_kernel(high, entries, place, *refs):
    out, sems = refs[-2], refs[-1]
    me = place[0]
    copies = []
    for n, (d, start, stop) in enumerate(entries):
        at = pl.multiple_of((me ^ d) * high + start, 16)
        target = out.at[pl.ds(at, stop - start)]
        copies += pieces_of(refs[n], target, STEP, sems, len(copies))
    for copy in copies:
        copy.start()
    for copy in copies:
        copy.wait()


def steps_in(spans):
    return sum(-(-(stop - start) // STEP) for start, stop in spans)


def whole(memory=pltpu.VMEM):
    return pl.BlockSpec(memory_space=memory)


def shape(dims, kind):
    return jax.ShapeDtypeStruct(dims, kind)


def pinned(x):
    return pltpu.with_memory_space_constraint(x, pltpu.HBM)


def local(
    grad_rows,
    router_weight,
    send_counts,
    gate_stash,
    up_stash,
    master_weight,
    first_moment,
    second_moment,
):
    _, flight, slots, width = grad_rows.shape
    pieces = lax.axis_size("dp")
    sources = lax.axis_size("expert")
    ways = sources // flight
    high, across = master_weight.shape
    me = lax.axis_index("dp")
    seat = lax.axis_index("expert")
    place = jnp.stack([me, seat % ways]).astype(jnp.int32)
    smem = whole(pltpu.SMEM)
    hbm = whole(pltpu.HBM)
    count = pieces * flight * slots

    def over_dp(x, d):
        return lax.ppermute(x, "dp", [(i, i ^ d) for i in range(pieces)])

    cut, hidden = pl.pallas_call(
        scale_kernel,
        out_shape=(
            shape((pieces, flight, slots, high), bf16),
            shape((ways, flight, slots, across), bf16),
        ),
        in_specs=[hbm] * 5,
        out_specs=[whole()] * 2,
        scratch_shapes=[
            pltpu.SMEM(send_counts.shape, jnp.int32),
            pltpu.VMEM(router_weight.shape, f32),
            pltpu.VMEM(grad_rows.shape, bf16),
            pltpu.VMEM(gate_stash.shape, bf16),
            pltpu.VMEM(up_stash.shape, bf16),
            pltpu.SemaphoreType.DMA((4 + flight,)),
        ],
        compiler_params=params(),
        name="scale",
    )(
        pinned(send_counts),
        pinned(router_weight),
        pinned(grad_rows),
        pinned(gate_stash),
        pinned(up_stash),
    )
    groups = [
        [i * sources + g * ways + v for i in range(pieces) for g in range(flight)]
        for v in range(ways)
    ]
    mine = lax.all_to_all(
        cut.reshape(pieces * flight, slots, high),
        ("dp", "expert"),
        split_axis=0,
        concat_axis=0,
        axis_index_groups=groups,
        tiled=True,
    )
    top = pieces // 2

    def spread(entries, first):
        step = first
        while step:
            entries = entries + [(d ^ step, *span, over_dp(x, step)) for d, *span, x in entries]
            step //= 2
        return entries

    hiddens = [entry[1] for entry in sorted(spread([(0, hidden)], top), key=lambda e: e[0])]
    right = pl.pallas_call(
        order_kernel,
        out_shape=shape((ways, count, across), bf16),
        in_specs=[smem] + [whole()] * pieces,
        out_specs=whole(),
        compiler_params=params(),
        name="order",
    )(place, *hiddens)
    state = pl.pallas_call(
        fetch_kernel,
        out_shape=[shape((high, across), f32)] * 3,
        in_specs=[hbm] * 3,
        out_specs=[whole()] * 3,
        scratch_shapes=[pltpu.SemaphoreType.DMA((3 * steps_in([(0, high)]),))],
        compiler_params=params(),
        cost_estimate=cost(0, high * across * 24),
        name="fetch",
    )(pinned(master_weight), pinned(first_moment), pinned(second_moment))
    mine, state = lax.optimization_barrier((mine, state))

    tiles = -(-high // LANES)
    middle = (tiles + 1) // 2 * LANES
    spans = [(0, middle), (middle, high)] if middle < high else [(0, high)]
    rows = []
    for start, stop in spans:
        piece = mine[:, :, start:stop]
        if rows:
            piece, rows[-1], right = lax.optimization_barrier((piece, rows[-1], right))
        rows.append(
            [piece]
            + [
                lax.ppermute(piece, "expert", [(k, k ^ d) for k in range(sources)])
                for d in range(1, ways)
            ]
        )

    fresh, news = [], []
    for (start, stop), chunk in zip(spans, rows):
        out = pl.pallas_call(
            functools.partial(update_kernel, ways, start, stop),
            out_shape=[shape((stop - start, across), bf16)]
            + [shape((stop - start, across), f32)] * 3,
            in_specs=[whole()] * (ways + 4),
            out_specs=[whole()] * 4,
            scratch_shapes=[pltpu.VMEM((stop - start, across), f32)],
            compiler_params=params(),
            cost_estimate=cost(2 * ways * count * (stop - start) * across, high * across * 26),
            name="update",
        )(*chunk, right, *state)
        fresh.append(out[0])
        news += out[1:]
    crossed = [over_dp(piece, top) for piece in fresh]

    part = (ways, flight, slots, across)
    bit = 1
    kept = [[d for d in range(pieces) if not d & bit], [d for d in range(pieces) if d & bit]]
    keep, send, own_fresh = pl.pallas_call(
        functools.partial(partial_kernel, ways, spans, kept),
        out_shape=[
            shape((pieces // 2, *part), f32),
            shape((pieces // 2, *part), bf16),
            shape((high, across), bf16),
        ],
        in_specs=[smem] + [whole()] * ((ways + 1) * len(spans) + 1),
        out_specs=[whole()] * 3,
        scratch_shapes=[pltpu.VMEM((ways, count, across), f32)],
        compiler_params=params(),
        cost_estimate=cost(2 * ways * count * high * across, high * across * 12),
        name="partial",
    )(place, *[block for chunk in rows for block in chunk], *fresh, state[0])
    arrived = over_dp(send, bit)
    while bit < top:
        bit *= 2
        left = kept[0]
        kept = [[d for d in left if not d & bit], [d for d in left if d & bit]]
        chosen = [[left.index(d) for d in half] for half in kept]
        keep, send = pl.pallas_call(
            functools.partial(halve_kernel, chosen),
            out_shape=[
                shape((len(kept[0]), *part), f32),
                shape((len(kept[1]), *part), bf16),
            ],
            in_specs=[whole()] * 2,
            out_specs=[whole()] * 2,
            compiler_params=params(),
            name="halve",
        )(keep, arrived)
        arrived = over_dp(send, bit)
    if len(spans) > 1:
        crossed[0], keep = lax.optimization_barrier((crossed[0], keep))
    d_gate, d_up = pl.pallas_call(
        gate_kernel,
        out_shape=[shape(gate_stash.shape, bf16)] * 2,
        in_specs=[whole()] * 4,
        out_specs=[whole()] * 2,
        compiler_params=params(),
        name="gates",
    )(gate_stash, up_stash, keep, arrived)

    states = pl.pallas_call(
        functools.partial(store_kernel, spans),
        out_shape=[shape((high, across), f32)] * 3,
        in_specs=[whole()] * len(news),
        out_specs=[hbm] * 3,
        scratch_shapes=[pltpu.SemaphoreType.DMA((3 * steps_in(spans),))],
        compiler_params=params(),
        cost_estimate=cost(0, high * across * 24),
        name="store",
    )(*news)

    def join(entries, before):
        return pl.pallas_call(
            functools.partial(join_kernel, high, [entry[:3] for entry in entries]),
            out_shape=shape((pieces * high, across), bf16),
            in_specs=[smem] + [whole(pl.ANY)] * len(entries) + [hbm] * len(before),
            out_specs=hbm,
            input_output_aliases={len(entries) + 1: 0} if before else {},
            scratch_shapes=[pltpu.SemaphoreType.DMA((steps_in([e[1:3] for e in entries]),))],
            compiler_params=params(),
            name="join",
        )(place, *[entry[3] for entry in entries], *before)

    near, *far = spread([(0, 0, high, own_fresh)], top // 2)
    early, late = [near], far
    for (start, stop), piece in zip(spans[:-1], crossed[:-1]):
        near, *far = spread([(top, start, stop, piece)], top // 2)
        early.append(near)
        late += far
    joined = join(early, [])
    crossed[-1], joined, states, arrived = lax.optimization_barrier(
        (crossed[-1], joined, states, arrived)
    )
    joined = join(late + spread([(top, *spans[-1], crossed[-1])], top // 2), [joined])
    return (d_gate, d_up, *states, joined)


def solution(mesh):
    placed = (
        P("dp", "expert", None, None),
        P("dp", "expert", None),
        P("dp", "expert"),
        P("dp", None, "expert"),
        P("dp", None, "expert"),
        P("dp", "expert"),
        P("dp", "expert"),
        P("dp", "expert"),
    )
    return jax.shard_map(
        local,
        mesh=mesh,
        in_specs=placed,
        out_specs=(
            P("dp", None, "expert"),
            P("dp", None, "expert"),
            P("dp", "expert"),
            P("dp", "expert"),
            P("dp", "expert"),
            P(None, "expert"),
        ),
        check_vma=False,
    )
```

```python
import functools

import jax
import jax.numpy as jnp
from jax import lax
from jax.experimental import pallas as pl
from jax.experimental.pallas import tpu as pltpu
from jax.sharding import PartitionSpec as P

learning_rate = 0.01
beta_one = 0.9
beta_two = 0.95
decay_rate = 0.1
epsilon = 1e-08

bf16 = jnp.bfloat16
f32 = jnp.float32
VMEM_LIMIT = 40 * 1024 * 1024
LANES = 128


def params():
    return pltpu.CompilerParams(vmem_limit_bytes=VMEM_LIMIT)


def cost(flops, nbytes):
    return pl.CostEstimate(flops=flops, bytes_accessed=nbytes, transcendentals=0)


def take(refs, count):
    taken = refs[:count]
    del refs[:count]
    return taken


def wide(tiles):
    return tiles[0] if len(tiles) == 1 else jnp.concatenate(tiles, axis=1)


def tall(blocks):
    return blocks[0] if len(blocks) == 1 else jnp.concatenate(blocks, axis=0)


def seat_of(ways):
    seat = lax.axis_index("expert")
    return lax.axis_index("dp"), lax.rem(seat, ways), lax.div(seat, ways)


def scale_kernel(counts_in, router_in, rows_in, gate_in, up_in, out, hidden, *scratch):
    counts, router, rows, gate, up, sems = scratch
    copies = [
        pltpu.make_async_copy(source, target, sems.at[n])
        for n, (source, target) in enumerate(
            [
                (gate_in, gate),
                (up_in, up),
                (counts_in, counts),
                (router_in, router),
                (rows_in, rows),
            ]
        )
    ]
    for copy in copies:
        copy.start()
    flight, slots, width = rows.shape[1:]
    pieces = out.shape[0]
    piece = width // pieces
    ways = hidden.shape[0]
    _, _, own = seat_of(ways)
    copies[0].wait()
    copies[1].wait()
    g = gate[0].astype(f32)
    value = (g * jax.nn.sigmoid(g) * up[0].astype(f32)).astype(bf16)
    for f in range(flight):
        for v in range(ways):
            at = (f * ways + v) * slots
            hidden[v, f] = value[at : at + slots]
    for copy in copies[2:]:
        copy.wait()
    diagonal = lax.broadcasted_iota(jnp.int32, (slots, slots), 0) == lax.broadcasted_iota(
        jnp.int32, (slots, slots), 1
    )
    row = lax.broadcasted_iota(jnp.int32, (slots, 1), 0)
    for f in range(flight):
        weight = jnp.sum(
            jnp.where(diagonal, jnp.broadcast_to(router[0, f : f + 1, :], (slots, slots)), 0.0),
            axis=1,
            keepdims=True,
        )
        live = row < counts[0, f]
        scaled = jnp.where(live, weight * rows[0, f].astype(f32), 0.0).astype(bf16)
        for i in range(pieces):
            out[i, f ^ own] = scaled[:, i * piece : (i + 1) * piece]


def fetch_kernel(*refs):
    sems = refs[6]
    copies = [pltpu.make_async_copy(refs[n], refs[3 + n], sems.at[n]) for n in range(3)]
    for copy in copies:
        copy.start()
    for copy in copies:
        copy.wait()


def order_kernel(*refs):
    hiddens, right = refs[:-1], refs[-1]
    flight, ways = right.shape[:2]
    me, lane, own = seat_of(ways)
    for dj, hidden in enumerate(hiddens):
        for dg in range(flight):
            for d in range(ways):
                right[dg, d, me ^ dj] = hidden[lane ^ d, own ^ dg]


def stacked(rows, start, stop):
    return tall([block[...].reshape(-1, block.shape[-1])[:, start:stop] for block in rows])


def update_kernel(start, stop, *refs):
    refs = list(refs)
    rows = refs[:-9]
    right, master, first, second, fresh, new_master, new_first, new_second, gradient = refs[-9:]
    hidden = right[...].reshape(-1, right.shape[-1])
    gradient[...] = lax.dot_general(
        stacked(rows, start, stop), hidden, (((0,), (0,)), ((), ())), preferred_element_type=f32
    )
    for low in range(start, stop, 128):
        end = min(low + 128, stop)
        here = pl.ds(low, end - low)
        there = pl.ds(low - start, end - low)
        grad = gradient[there]
        old = master[here]
        moment_a = beta_one * first[here] + (1.0 - beta_one) * grad
        moment_b = beta_two * second[here] + (1.0 - beta_two) * grad * grad
        step_size = (moment_a * (1.0 / (1.0 - beta_one**5))) / (
            jnp.sqrt(moment_b * (1.0 / (1.0 - beta_two**5))) + epsilon
        )
        updated = old - learning_rate * (step_size + decay_rate * old)
        fresh[there] = updated.astype(bf16)
        new_master[there] = updated
        new_first[there] = moment_a
        new_second[there] = moment_b


def partial_kernel(spans, kept, *refs):
    refs = list(refs)
    master, keep, send, own_fresh, held = refs[-5:]
    fresh = refs[-5 - len(spans) : -5]
    rows = refs[: -5 - len(spans)]
    flight, ways = held.shape[:2]
    me, lane, own = seat_of(ways)
    left = stacked(rows, 0, master.shape[0])
    share = jnp.dot(left, master[...].astype(bf16), preferred_element_type=f32)
    held[...] = share.reshape(held.shape)
    for out, chosen in ((keep, kept[0]), (send, kept[1])):
        for n, dj in enumerate(chosen):
            for dg in range(flight):
                for d in range(ways):
                    out[n, lane ^ d, own ^ dg] = held[dg, d, me ^ dj].astype(out.dtype)
    for c, (start, stop) in enumerate(spans):
        own_fresh[start:stop] = fresh[c][...]


def halve_kernel(kept, held, arrived, keep, send):
    for out, chosen in ((keep, kept[0]), (send, kept[1])):
        for n, m in enumerate(chosen):
            out[n] = (held[m] + arrived[m].astype(f32)).astype(out.dtype)


def store_kernel(spans, *refs):
    refs = list(refs)
    news = take(refs, 3 * len(spans))
    outs = take(refs, 3)
    (sems,) = refs
    copies = []
    for c, (start, stop) in enumerate(spans):
        for n in range(3):
            copy = pltpu.make_async_copy(
                news[3 * c + n], outs[n].at[pl.ds(start, stop - start)], sems.at[c, n]
            )
            copy.start()
            copies.append(copy)
    for copy in copies:
        copy.wait()


def gate_kernel(gate, up, held, arrived, d_gate, d_up):
    ways, flight, slots = held.shape[1:4]
    for f in range(flight):
        for v in range(ways):
            at = pl.ds((f * ways + v) * slots, slots)
            grad = held[0, v, f] + arrived[0, v, f].astype(f32)
            g = gate[0, at].astype(f32)
            u = up[0, at].astype(f32)
            sig = jax.nn.sigmoid(g)
            d_gate[0, at] = (grad * u * sig * (1.0 + g * (1.0 - sig))).astype(bf16)
            d_up[0, at] = (grad * (g * sig)).astype(bf16)


def join_kernel(high, entries, *refs):
    out, sems = refs[-2], refs[-1]
    me = lax.axis_index("dp")
    copies = []
    for n, (d, start, stop) in enumerate(entries):
        at = pl.multiple_of((me ^ d) * high + start, 16)
        copy = pltpu.make_async_copy(refs[n], out.at[pl.ds(at, stop - start)], sems.at[n])
        copy.start()
        copies.append(copy)
    for copy in copies:
        copy.wait()


def whole(memory=pltpu.VMEM):
    return pl.BlockSpec(memory_space=memory)


def shape(dims, kind):
    return jax.ShapeDtypeStruct(dims, kind)


def pinned(x):
    return pltpu.with_memory_space_constraint(x, pltpu.HBM)


def local(
    grad_rows,
    router_weight,
    send_counts,
    gate_stash,
    up_stash,
    master_weight,
    first_moment,
    second_moment,
):
    _, flight, slots, width = grad_rows.shape
    pieces = lax.axis_size("dp")
    sources = lax.axis_size("expert")
    ways = sources // flight
    high, across = master_weight.shape
    hbm = whole(pltpu.HBM)
    count = pieces * flight * slots

    def over_dp(x, d):
        return lax.ppermute(x, "dp", [(i, i ^ d) for i in range(pieces)])

    cut, hidden = pl.pallas_call(
        scale_kernel,
        out_shape=(
            shape((pieces, flight, slots, high), bf16),
            shape((ways, flight, slots, across), bf16),
        ),
        in_specs=[hbm] * 5,
        out_specs=[whole()] * 2,
        scratch_shapes=[
            pltpu.SMEM(send_counts.shape, jnp.int32),
            pltpu.VMEM(router_weight.shape, f32),
            pltpu.VMEM(grad_rows.shape, bf16),
            pltpu.VMEM(gate_stash.shape, bf16),
            pltpu.VMEM(up_stash.shape, bf16),
            pltpu.SemaphoreType.DMA((5,)),
        ],
        compiler_params=params(),
        name="scale",
    )(
        pinned(send_counts),
        pinned(router_weight),
        pinned(grad_rows),
        pinned(gate_stash),
        pinned(up_stash),
    )
    mine = lax.all_to_all(cut, "dp", split_axis=0, concat_axis=0, tiled=True)

    def toward(x, d):
        return lax.ppermute(x, "expert", [(k, k ^ d) for k in range(sources)])

    def square(x):
        return [x] + [toward(x, d) for d in range(1, ways)]

    blocks = [mine[:, dg] for dg in range(flight)]
    state = pl.pallas_call(
        fetch_kernel,
        out_shape=[shape((high, across), f32)] * 3,
        in_specs=[hbm] * 3,
        out_specs=[whole()] * 3,
        scratch_shapes=[pltpu.SemaphoreType.DMA((3,))],
        compiler_params=params(),
        cost_estimate=cost(0, high * across * 24),
        name="fetch",
    )(pinned(master_weight), pinned(first_moment), pinned(second_moment))
    far = [toward(blocks[dg], dg * ways) for dg in range(1, flight)]
    rows = square(blocks[0])
    rows, far, state, hidden = lax.optimization_barrier((rows, far, state, hidden))
    for block in far:
        rows = rows + square(block)

    top = pieces // 2

    def spread(entries, first):
        step = first
        while step:
            entries = entries + [(d ^ step, *span, over_dp(x, step)) for d, *span, x in entries]
            step //= 2
        return entries

    hiddens = [entry[1] for entry in sorted(spread([(0, hidden)], top), key=lambda e: e[0])]
    right = pl.pallas_call(
        order_kernel,
        out_shape=shape((flight, ways, pieces, slots, across), bf16),
        in_specs=[whole()] * pieces,
        out_specs=whole(),
        compiler_params=params(),
        name="order",
    )(*hiddens)

    tiles = -(-high // LANES)
    middle = (tiles + 1) // 2 * LANES
    spans = [(0, middle), (middle, high)] if middle < high else [(0, high)]
    fresh, news = [], []
    for start, stop in spans:
        out = pl.pallas_call(
            functools.partial(update_kernel, start, stop),
            out_shape=[shape((stop - start, across), bf16)]
            + [shape((stop - start, across), f32)] * 3,
            in_specs=[whole()] * (len(rows) + 4),
            out_specs=[whole()] * 4,
            scratch_shapes=[pltpu.VMEM((stop - start, across), f32)],
            compiler_params=params(),
            cost_estimate=cost(2 * ways * count * (stop - start) * across, high * across * 26),
            name="update",
        )(*rows, right, *state)
        fresh.append(out[0])
        news += out[1:]
    crossed = [over_dp(piece, top) for piece in fresh]

    part = (ways, flight, slots, across)
    bit = 1
    kept = [[d for d in range(pieces) if not d & bit], [d for d in range(pieces) if d & bit]]
    keep, send, own_fresh = pl.pallas_call(
        functools.partial(partial_kernel, spans, kept),
        out_shape=[
            shape((pieces // 2, *part), f32),
            shape((pieces // 2, *part), bf16),
            shape((high, across), bf16),
        ],
        in_specs=[whole()] * (len(rows) + len(spans) + 1),
        out_specs=[whole()] * 3,
        scratch_shapes=[pltpu.VMEM((flight, ways, pieces, slots, across), f32)],
        compiler_params=params(),
        cost_estimate=cost(2 * ways * count * high * across, high * across * 12),
        name="partial",
    )(*rows, *fresh, state[0])
    arrived = over_dp(send, bit)
    while bit < top:
        bit *= 2
        left = kept[0]
        kept = [[d for d in left if not d & bit], [d for d in left if d & bit]]
        chosen = [[left.index(d) for d in half] for half in kept]
        keep, send = pl.pallas_call(
            functools.partial(halve_kernel, chosen),
            out_shape=[
                shape((len(kept[0]), *part), f32),
                shape((len(kept[1]), *part), bf16),
            ],
            in_specs=[whole()] * 2,
            out_specs=[whole()] * 2,
            compiler_params=params(),
            name="halve",
        )(keep, arrived)
        arrived = over_dp(send, bit)
    if len(spans) > 1:
        crossed[0], keep = lax.optimization_barrier((crossed[0], keep))
    d_gate, d_up = pl.pallas_call(
        gate_kernel,
        out_shape=[shape(gate_stash.shape, bf16)] * 2,
        in_specs=[whole()] * 4,
        out_specs=[whole()] * 2,
        compiler_params=params(),
        name="gates",
    )(gate_stash, up_stash, keep, arrived)

    states = pl.pallas_call(
        functools.partial(store_kernel, spans),
        out_shape=[shape((high, across), f32)] * 3,
        in_specs=[whole()] * len(news),
        out_specs=[hbm] * 3,
        scratch_shapes=[pltpu.SemaphoreType.DMA((len(spans), 3))],
        compiler_params=params(),
        cost_estimate=cost(0, high * across * 24),
        name="store",
    )(*news)

    def join(entries, before):
        return pl.pallas_call(
            functools.partial(join_kernel, high, [entry[:3] for entry in entries]),
            out_shape=shape((pieces * high, across), bf16),
            in_specs=[whole(pl.ANY)] * len(entries) + [hbm] * len(before),
            out_specs=hbm,
            input_output_aliases={len(entries): 0} if before else {},
            scratch_shapes=[pltpu.SemaphoreType.DMA((len(entries),))],
            compiler_params=params(),
            name="join",
        )(*[entry[3] for entry in entries], *before)

    near, *far = spread([(0, 0, high, own_fresh)], top // 2)
    early, late = [near], far
    for (start, stop), piece in zip(spans[:-1], crossed[:-1]):
        near, *far = spread([(top, start, stop, piece)], top // 2)
        early.append(near)
        late += far
    joined = join(early, [])
    crossed[-1], joined, states, arrived = lax.optimization_barrier(
        (crossed[-1], joined, states, arrived)
    )
    joined = join(late + spread([(top, *spans[-1], crossed[-1])], top // 2), [joined])
    return (d_gate, d_up, *states, joined)


def solution(mesh):
    placed = (
        P("dp", "expert", None, None),
        P("dp", "expert", None),
        P("dp", "expert"),
        P("dp", None, "expert"),
        P("dp", None, "expert"),
        P("dp", "expert"),
        P("dp", "expert"),
        P("dp", "expert"),
    )
    return jax.shard_map(
        local,
        mesh=mesh,
        in_specs=placed,
        out_specs=(
            P("dp", None, "expert"),
            P("dp", None, "expert"),
            P("dp", "expert"),
            P("dp", "expert"),
            P("dp", "expert"),
            P(None, "expert"),
        ),
        check_vma=False,
    )
```

```python
import functools

import jax
import jax.numpy as jnp
from jax import lax
from jax.experimental import pallas as pl
from jax.experimental.pallas import tpu as pltpu
from jax.sharding import PartitionSpec as P

learning_rate = 0.01
beta_one = 0.9
beta_two = 0.95
decay_rate = 0.1
epsilon = 1e-08

bf16 = jnp.bfloat16
f32 = jnp.float32
VMEM_LIMIT = 40 * 1024 * 1024
LANES = 128


def params():
    return pltpu.CompilerParams(vmem_limit_bytes=VMEM_LIMIT)


def cost(flops, nbytes):
    return pl.CostEstimate(flops=flops, bytes_accessed=nbytes, transcendentals=0)


def take(refs, count):
    taken = refs[:count]
    del refs[:count]
    return taken


def wide(tiles):
    return tiles[0] if len(tiles) == 1 else jnp.concatenate(tiles, axis=1)


def tall(blocks):
    return blocks[0] if len(blocks) == 1 else jnp.concatenate(blocks, axis=0)


def seat_of(ways):
    return lax.axis_index("dp"), lax.rem(lax.axis_index("expert"), ways)


def scale_kernel(counts_in, router_in, rows_in, gate_in, up_in, out, hidden, *scratch):
    counts, router, rows, gate, up, sems = scratch
    copies = [
        pltpu.make_async_copy(source, target, sems.at[n])
        for n, (source, target) in enumerate(
            [
                (gate_in, gate),
                (up_in, up),
                (counts_in, counts),
                (router_in, router),
                (rows_in, rows),
            ]
        )
    ]
    for copy in copies:
        copy.start()
    flight, slots, width = rows.shape[1:]
    pieces = out.shape[0]
    piece = width // pieces
    ways = hidden.shape[0]
    copies[0].wait()
    copies[1].wait()
    g = gate[0].astype(f32)
    value = (g * jax.nn.sigmoid(g) * up[0].astype(f32)).astype(bf16)
    for f in range(flight):
        for v in range(ways):
            at = (f * ways + v) * slots
            hidden[v, f] = value[at : at + slots]
    for copy in copies[2:]:
        copy.wait()
    diagonal = lax.broadcasted_iota(jnp.int32, (slots, slots), 0) == lax.broadcasted_iota(
        jnp.int32, (slots, slots), 1
    )
    row = lax.broadcasted_iota(jnp.int32, (slots, 1), 0)
    for f in range(flight):
        weight = jnp.sum(
            jnp.where(diagonal, jnp.broadcast_to(router[0, f : f + 1, :], (slots, slots)), 0.0),
            axis=1,
            keepdims=True,
        )
        live = row < counts[0, f]
        scaled = jnp.where(live, weight * rows[0, f].astype(f32), 0.0).astype(bf16)
        for i in range(pieces):
            out[i, f] = scaled[:, i * piece : (i + 1) * piece]


def fetch_kernel(*refs):
    sems = refs[6]
    copies = [pltpu.make_async_copy(refs[n], refs[3 + n], sems.at[n]) for n in range(3)]
    for copy in copies:
        copy.start()
    for copy in copies:
        copy.wait()


def order_kernel(*refs):
    hiddens, right = refs[:-1], refs[-1]
    ways = right.shape[0]
    me, lane = seat_of(ways)
    for dj, hidden in enumerate(hiddens):
        for d in range(ways):
            right[d, me ^ dj] = hidden[lane ^ d]


def update_kernel(start, stop, *refs):
    refs = list(refs)
    rows = refs[:-9]
    right, master, first, second, fresh, new_master, new_first, new_second, gradient = refs[-9:]
    hidden = right[...].reshape(-1, right.shape[-1])
    left = tall([block[...].reshape(-1, stop - start) for block in rows])
    gradient[...] = lax.dot_general(
        left, hidden, (((0,), (0,)), ((), ())), preferred_element_type=f32
    )
    for low in range(start, stop, 128):
        end = min(low + 128, stop)
        here = pl.ds(low, end - low)
        there = pl.ds(low - start, end - low)
        grad = gradient[there]
        old = master[here]
        moment_a = beta_one * first[here] + (1.0 - beta_one) * grad
        moment_b = beta_two * second[here] + (1.0 - beta_two) * grad * grad
        step_size = (moment_a * (1.0 / (1.0 - beta_one**5))) / (
            jnp.sqrt(moment_b * (1.0 / (1.0 - beta_two**5))) + epsilon
        )
        updated = old - learning_rate * (step_size + decay_rate * old)
        fresh[there] = updated.astype(bf16)
        new_master[there] = updated
        new_first[there] = moment_a
        new_second[there] = moment_b


def partial_kernel(spans, kept, *refs):
    refs = list(refs)
    chunks = len(spans)
    master, keep, send, own_fresh, held = refs[-5:]
    fresh = refs[-5 - chunks : -5]
    rows = refs[: -5 - chunks]
    ways = held.shape[0]
    me, lane = seat_of(ways)
    left = wide(
        [
            tall([block[...].reshape(-1, stop - start) for block in rows[c * ways : (c + 1) * ways]])
            for c, (start, stop) in enumerate(spans)
        ]
    )
    share = jnp.dot(left, master[...].astype(bf16), preferred_element_type=f32)
    held[...] = share.reshape(held.shape)
    for out, chosen in ((keep, kept[0]), (send, kept[1])):
        for n, dj in enumerate(chosen):
            for d in range(ways):
                out[n, lane ^ d] = held[d, me ^ dj].astype(out.dtype)
    for c, (start, stop) in enumerate(spans):
        own_fresh[start:stop] = fresh[c][...]


def halve_kernel(kept, held, arrived, keep, send):
    for out, chosen in ((keep, kept[0]), (send, kept[1])):
        for n, m in enumerate(chosen):
            out[n] = (held[m] + arrived[m].astype(f32)).astype(out.dtype)


def store_kernel(spans, *refs):
    refs = list(refs)
    news = take(refs, 3 * len(spans))
    outs = take(refs, 3)
    (sems,) = refs
    copies = []
    for c, (start, stop) in enumerate(spans):
        for n in range(3):
            copy = pltpu.make_async_copy(
                news[3 * c + n], outs[n].at[pl.ds(start, stop - start)], sems.at[c, n]
            )
            copy.start()
            copies.append(copy)
    for copy in copies:
        copy.wait()


def gate_kernel(gate, up, held, arrived, d_gate, d_up):
    ways, flight, slots = held.shape[1:4]
    for f in range(flight):
        for v in range(ways):
            at = pl.ds((f * ways + v) * slots, slots)
            grad = held[0, v, f] + arrived[0, v, f].astype(f32)
            g = gate[0, at].astype(f32)
            u = up[0, at].astype(f32)
            sig = jax.nn.sigmoid(g)
            d_gate[0, at] = (grad * u * sig * (1.0 + g * (1.0 - sig))).astype(bf16)
            d_up[0, at] = (grad * (g * sig)).astype(bf16)


def join_kernel(high, entries, *refs):
    out, sems = refs[-2], refs[-1]
    me = lax.axis_index("dp")
    copies = []
    for n, (d, start, stop) in enumerate(entries):
        at = pl.multiple_of((me ^ d) * high + start, 16)
        copy = pltpu.make_async_copy(refs[n], out.at[pl.ds(at, stop - start)], sems.at[n])
        copy.start()
        copies.append(copy)
    for copy in copies:
        copy.wait()


def whole(memory=pltpu.VMEM):
    return pl.BlockSpec(memory_space=memory)


def shape(dims, kind):
    return jax.ShapeDtypeStruct(dims, kind)


def pinned(x):
    return pltpu.with_memory_space_constraint(x, pltpu.HBM)


def local(
    grad_rows,
    router_weight,
    send_counts,
    gate_stash,
    up_stash,
    master_weight,
    first_moment,
    second_moment,
):
    _, flight, slots, width = grad_rows.shape
    pieces = lax.axis_size("dp")
    sources = lax.axis_size("expert")
    ways = sources // flight
    high, across = master_weight.shape
    hbm = whole(pltpu.HBM)
    count = pieces * flight * slots

    def over_dp(x, d):
        return lax.ppermute(x, "dp", [(i, i ^ d) for i in range(pieces)])

    cut, hidden = pl.pallas_call(
        scale_kernel,
        out_shape=(
            shape((pieces, flight, slots, high), bf16),
            shape((ways, flight, slots, across), bf16),
        ),
        in_specs=[hbm] * 5,
        out_specs=[whole()] * 2,
        scratch_shapes=[
            pltpu.SMEM(send_counts.shape, jnp.int32),
            pltpu.VMEM(router_weight.shape, f32),
            pltpu.VMEM(grad_rows.shape, bf16),
            pltpu.VMEM(gate_stash.shape, bf16),
            pltpu.VMEM(up_stash.shape, bf16),
            pltpu.SemaphoreType.DMA((5,)),
        ],
        compiler_params=params(),
        name="scale",
    )(
        pinned(send_counts),
        pinned(router_weight),
        pinned(grad_rows),
        pinned(gate_stash),
        pinned(up_stash),
    )
    groups = [
        [i * sources + g * ways + v for i in range(pieces) for g in range(flight)]
        for v in range(ways)
    ]
    mine = lax.all_to_all(
        cut.reshape(pieces * flight, slots, high),
        ("dp", "expert"),
        split_axis=0,
        concat_axis=0,
        axis_index_groups=groups,
        tiled=True,
    )
    top = pieces // 2

    def spread(entries, first):
        step = first
        while step:
            entries = entries + [(d ^ step, *span, over_dp(x, step)) for d, *span, x in entries]
            step //= 2
        return entries

    hiddens = [entry[1] for entry in sorted(spread([(0, hidden)], top), key=lambda e: e[0])]
    mine, hiddens = lax.optimization_barrier((mine, hiddens))
    right = pl.pallas_call(
        order_kernel,
        out_shape=shape((ways, pieces, flight, slots, across), bf16),
        in_specs=[whole()] * pieces,
        out_specs=whole(),
        compiler_params=params(),
        name="order",
    )(*hiddens)
    state = pl.pallas_call(
        fetch_kernel,
        out_shape=[shape((high, across), f32)] * 3,
        in_specs=[hbm] * 3,
        out_specs=[whole()] * 3,
        scratch_shapes=[pltpu.SemaphoreType.DMA((3,))],
        compiler_params=params(),
        cost_estimate=cost(0, high * across * 24),
        name="fetch",
    )(pinned(master_weight), pinned(first_moment), pinned(second_moment))

    tiles = -(-high // LANES)
    middle = (tiles + 1) // 2 * LANES
    spans = [(0, middle), (middle, high)] if middle < high else [(0, high)]
    rows = []
    for start, stop in spans:
        piece = mine[:, :, start:stop]
        rows.append(
            [piece]
            + [
                lax.ppermute(piece, "expert", [(k, k ^ d) for k in range(sources)])
                for d in range(1, ways)
            ]
        )

    fresh, news = [], []
    for c, (start, stop) in enumerate(spans):
        out = pl.pallas_call(
            functools.partial(update_kernel, start, stop),
            out_shape=[shape((stop - start, across), bf16)]
            + [shape((stop - start, across), f32)] * 3,
            in_specs=[whole()] * (ways + 4),
            out_specs=[whole()] * 4,
            scratch_shapes=[pltpu.VMEM((stop - start, across), f32)],
            compiler_params=params(),
            cost_estimate=cost(2 * ways * count * (stop - start) * across, high * across * 26),
            name="update",
        )(*rows[c], right, *state)
        fresh.append(out[0])
        news += out[1:]
    crossed = [over_dp(piece, top) for piece in fresh]

    part = (ways, flight, slots, across)
    bit = 1
    kept = [[d for d in range(pieces) if not d & bit], [d for d in range(pieces) if d & bit]]
    keep, send, own_fresh = pl.pallas_call(
        functools.partial(partial_kernel, spans, kept),
        out_shape=[
            shape((pieces // 2, *part), f32),
            shape((pieces // 2, *part), bf16),
            shape((high, across), bf16),
        ],
        in_specs=[whole()] * ((ways + 1) * len(spans) + 1),
        out_specs=[whole()] * 3,
        scratch_shapes=[pltpu.VMEM((ways, pieces, flight, slots, across), f32)],
        compiler_params=params(),
        cost_estimate=cost(2 * ways * count * high * across, high * across * 12),
        name="partial",
    )(*[block for chunk in rows for block in chunk], *fresh, state[0])
    arrived = over_dp(send, bit)
    while bit < top:
        bit *= 2
        left = kept[0]
        kept = [[d for d in left if not d & bit], [d for d in left if d & bit]]
        chosen = [[left.index(d) for d in half] for half in kept]
        keep, send = pl.pallas_call(
            functools.partial(halve_kernel, chosen),
            out_shape=[
                shape((len(kept[0]), *part), f32),
                shape((len(kept[1]), *part), bf16),
            ],
            in_specs=[whole()] * 2,
            out_specs=[whole()] * 2,
            compiler_params=params(),
            name="halve",
        )(keep, arrived)
        arrived = over_dp(send, bit)
    if len(spans) > 1:
        crossed[0], keep = lax.optimization_barrier((crossed[0], keep))
    d_gate, d_up = pl.pallas_call(
        gate_kernel,
        out_shape=[shape(gate_stash.shape, bf16)] * 2,
        in_specs=[whole()] * 4,
        out_specs=[whole()] * 2,
        compiler_params=params(),
        name="gates",
    )(gate_stash, up_stash, keep, arrived)

    states = pl.pallas_call(
        functools.partial(store_kernel, spans),
        out_shape=[shape((high, across), f32)] * 3,
        in_specs=[whole()] * len(news),
        out_specs=[hbm] * 3,
        scratch_shapes=[pltpu.SemaphoreType.DMA((len(spans), 3))],
        compiler_params=params(),
        cost_estimate=cost(0, high * across * 24),
        name="store",
    )(*news)

    def join(entries, before):
        return pl.pallas_call(
            functools.partial(join_kernel, high, [entry[:3] for entry in entries]),
            out_shape=shape((pieces * high, across), bf16),
            in_specs=[whole(pl.ANY)] * len(entries) + [hbm] * len(before),
            out_specs=hbm,
            input_output_aliases={len(entries): 0} if before else {},
            scratch_shapes=[pltpu.SemaphoreType.DMA((len(entries),))],
            compiler_params=params(),
            name="join",
        )(*[entry[3] for entry in entries], *before)

    near, *far = spread([(0, 0, high, own_fresh)], top // 2)
    early, late = [near], far
    for (start, stop), piece in zip(spans[:-1], crossed[:-1]):
        near, *far = spread([(top, start, stop, piece)], top // 2)
        early.append(near)
        late += far
    joined = join(early, [])
    crossed[-1], joined, states, arrived = lax.optimization_barrier(
        (crossed[-1], joined, states, arrived)
    )
    joined = join(late + spread([(top, *spans[-1], crossed[-1])], top // 2), [joined])
    return (d_gate, d_up, *states, joined)


def solution(mesh):
    placed = (
        P("dp", "expert", None, None),
        P("dp", "expert", None),
        P("dp", "expert"),
        P("dp", None, "expert"),
        P("dp", None, "expert"),
        P("dp", "expert"),
        P("dp", "expert"),
        P("dp", "expert"),
    )
    return jax.shard_map(
        local,
        mesh=mesh,
        in_specs=placed,
        out_specs=(
            P("dp", None, "expert"),
            P("dp", None, "expert"),
            P("dp", "expert"),
            P("dp", "expert"),
            P("dp", "expert"),
            P(None, "expert"),
        ),
        check_vma=False,
    )
```

```python
import functools

import jax
import jax.numpy as jnp
from jax import lax
from jax.experimental import pallas as pl
from jax.experimental.pallas import tpu as pltpu
from jax.sharding import PartitionSpec as P

learning_rate = 0.01
beta_one = 0.9
beta_two = 0.95
decay_rate = 0.1
epsilon = 1e-08

bf16 = jnp.bfloat16
f32 = jnp.float32
VMEM_LIMIT = 40 * 1024 * 1024
LANES = 128


def params():
    return pltpu.CompilerParams(vmem_limit_bytes=VMEM_LIMIT)


def cost(flops, nbytes):
    return pl.CostEstimate(flops=flops, bytes_accessed=nbytes, transcendentals=0)


def take(refs, count):
    taken = refs[:count]
    del refs[:count]
    return taken


def wide(tiles):
    return tiles[0] if len(tiles) == 1 else jnp.concatenate(tiles, axis=1)


def tall(blocks):
    return blocks[0] if len(blocks) == 1 else jnp.concatenate(blocks, axis=0)


def seat_of(ways):
    return lax.axis_index("dp"), lax.rem(lax.axis_index("expert"), ways)


def scale_kernel(counts_in, router_in, rows_in, gate_in, up_in, out, hidden, *scratch):
    counts, router, rows, gate, up, sems = scratch
    copies = [
        pltpu.make_async_copy(source, target, sems.at[n])
        for n, (source, target) in enumerate(
            [
                (gate_in, gate),
                (up_in, up),
                (counts_in, counts),
                (router_in, router),
                (rows_in, rows),
            ]
        )
    ]
    for copy in copies:
        copy.start()
    flight, slots, width = rows.shape[1:]
    pieces = out.shape[0]
    piece = width // pieces
    ways = hidden.shape[0]
    copies[0].wait()
    copies[1].wait()
    g = gate[0].astype(f32)
    value = (g * jax.nn.sigmoid(g) * up[0].astype(f32)).astype(bf16)
    for f in range(flight):
        for v in range(ways):
            at = (f * ways + v) * slots
            hidden[v, f] = value[at : at + slots]
    for copy in copies[2:]:
        copy.wait()
    diagonal = lax.broadcasted_iota(jnp.int32, (slots, slots), 0) == lax.broadcasted_iota(
        jnp.int32, (slots, slots), 1
    )
    row = lax.broadcasted_iota(jnp.int32, (slots, 1), 0)
    for f in range(flight):
        weight = jnp.sum(
            jnp.where(diagonal, jnp.broadcast_to(router[0, f : f + 1, :], (slots, slots)), 0.0),
            axis=1,
            keepdims=True,
        )
        live = row < counts[0, f]
        scaled = jnp.where(live, weight * rows[0, f].astype(f32), 0.0).astype(bf16)
        for i in range(pieces):
            out[i, f] = scaled[:, i * piece : (i + 1) * piece]


def fetch_kernel(after, *refs):
    del after
    sems = refs[6]
    copies = [pltpu.make_async_copy(refs[n], refs[3 + n], sems.at[n]) for n in range(3)]
    for copy in copies:
        copy.start()
    for copy in copies:
        copy.wait()


def order_kernel(*refs):
    hiddens, right = refs[:-1], refs[-1]
    ways = right.shape[0]
    me, lane = seat_of(ways)
    for dj, hidden in enumerate(hiddens):
        for d in range(ways):
            right[d, me ^ dj] = hidden[lane ^ d]


def update_kernel(start, stop, *refs):
    refs = list(refs)
    rows = refs[:-9]
    right, master, first, second, fresh, new_master, new_first, new_second, gradient = refs[-9:]
    hidden = right[...].reshape(-1, right.shape[-1])
    left = tall([block[...].reshape(-1, stop - start) for block in rows])
    gradient[...] = lax.dot_general(
        left, hidden, (((0,), (0,)), ((), ())), preferred_element_type=f32
    )
    for low in range(start, stop, 128):
        end = min(low + 128, stop)
        here = pl.ds(low, end - low)
        there = pl.ds(low - start, end - low)
        grad = gradient[there]
        old = master[here]
        moment_a = beta_one * first[here] + (1.0 - beta_one) * grad
        moment_b = beta_two * second[here] + (1.0 - beta_two) * grad * grad
        step_size = (moment_a * (1.0 / (1.0 - beta_one**5))) / (
            jnp.sqrt(moment_b * (1.0 / (1.0 - beta_two**5))) + epsilon
        )
        updated = old - learning_rate * (step_size + decay_rate * old)
        fresh[there] = updated.astype(bf16)
        new_master[there] = updated
        new_first[there] = moment_a
        new_second[there] = moment_b


def partial_kernel(spans, kept, *refs):
    refs = list(refs)
    chunks = len(spans)
    master, keep, send, own_fresh, held = refs[-5:]
    fresh = refs[-5 - chunks : -5]
    rows = refs[: -5 - chunks]
    ways = held.shape[0]
    me, lane = seat_of(ways)
    left = wide(
        [
            tall([block[...].reshape(-1, stop - start) for block in rows[c * ways : (c + 1) * ways]])
            for c, (start, stop) in enumerate(spans)
        ]
    )
    share = jnp.dot(left, master[...].astype(bf16), preferred_element_type=f32)
    held[...] = share.reshape(held.shape)
    for out, chosen in ((keep, kept[0]), (send, kept[1])):
        for n, dj in enumerate(chosen):
            for d in range(ways):
                out[n, lane ^ d] = held[d, me ^ dj].astype(out.dtype)
    for c, (start, stop) in enumerate(spans):
        own_fresh[start:stop] = fresh[c][...]


def halve_kernel(kept, held, arrived, keep, send):
    for out, chosen in ((keep, kept[0]), (send, kept[1])):
        for n, m in enumerate(chosen):
            out[n] = (held[m] + arrived[m].astype(f32)).astype(out.dtype)


def store_kernel(spans, *refs):
    refs = list(refs)
    news = take(refs, 3 * len(spans))
    outs = take(refs, 3)
    (sems,) = refs
    copies = []
    for c, (start, stop) in enumerate(spans):
        for n in range(3):
            copy = pltpu.make_async_copy(
                news[3 * c + n], outs[n].at[pl.ds(start, stop - start)], sems.at[c, n]
            )
            copy.start()
            copies.append(copy)
    for copy in copies:
        copy.wait()


def gate_kernel(gate, up, held, arrived, d_gate, d_up):
    ways, flight, slots = held.shape[1:4]
    for f in range(flight):
        for v in range(ways):
            at = pl.ds((f * ways + v) * slots, slots)
            grad = held[0, v, f] + arrived[0, v, f].astype(f32)
            g = gate[0, at].astype(f32)
            u = up[0, at].astype(f32)
            sig = jax.nn.sigmoid(g)
            d_gate[0, at] = (grad * u * sig * (1.0 + g * (1.0 - sig))).astype(bf16)
            d_up[0, at] = (grad * (g * sig)).astype(bf16)


def join_kernel(high, entries, *refs):
    out, sems = refs[-2], refs[-1]
    me = lax.axis_index("dp")
    copies = []
    for n, (d, start, stop) in enumerate(entries):
        at = pl.multiple_of((me ^ d) * high + start, 16)
        copy = pltpu.make_async_copy(refs[n], out.at[pl.ds(at, stop - start)], sems.at[n])
        copy.start()
        copies.append(copy)
    for copy in copies:
        copy.wait()


def whole(memory=pltpu.VMEM):
    return pl.BlockSpec(memory_space=memory)


def shape(dims, kind):
    return jax.ShapeDtypeStruct(dims, kind)


def pinned(x):
    return pltpu.with_memory_space_constraint(x, pltpu.HBM)


def local(
    grad_rows,
    router_weight,
    send_counts,
    gate_stash,
    up_stash,
    master_weight,
    first_moment,
    second_moment,
):
    _, flight, slots, width = grad_rows.shape
    pieces = lax.axis_size("dp")
    sources = lax.axis_size("expert")
    ways = sources // flight
    high, across = master_weight.shape
    hbm = whole(pltpu.HBM)
    count = pieces * flight * slots

    def over_dp(x, d):
        return lax.ppermute(x, "dp", [(i, i ^ d) for i in range(pieces)])

    cut, hidden = pl.pallas_call(
        scale_kernel,
        out_shape=(
            shape((pieces, flight, slots, high), bf16),
            shape((ways, flight, slots, across), bf16),
        ),
        in_specs=[hbm] * 5,
        out_specs=[whole()] * 2,
        scratch_shapes=[
            pltpu.SMEM(send_counts.shape, jnp.int32),
            pltpu.VMEM(router_weight.shape, f32),
            pltpu.VMEM(grad_rows.shape, bf16),
            pltpu.VMEM(gate_stash.shape, bf16),
            pltpu.VMEM(up_stash.shape, bf16),
            pltpu.SemaphoreType.DMA((5,)),
        ],
        compiler_params=params(),
        name="scale",
    )(
        pinned(send_counts),
        pinned(router_weight),
        pinned(grad_rows),
        pinned(gate_stash),
        pinned(up_stash),
    )
    groups = [
        [i * sources + g * ways + v for i in range(pieces) for g in range(flight)]
        for v in range(ways)
    ]
    mine = lax.all_to_all(
        cut.reshape(pieces * flight, slots, high),
        ("dp", "expert"),
        split_axis=0,
        concat_axis=0,
        axis_index_groups=groups,
        tiled=True,
    )
    mine, hidden = lax.optimization_barrier((mine, hidden))
    top = pieces // 2

    def spread(entries, first):
        step = first
        while step:
            entries = entries + [(d ^ step, *span, over_dp(x, step)) for d, *span, x in entries]
            step //= 2
        return entries

    hiddens = [entry[1] for entry in sorted(spread([(0, hidden)], top), key=lambda e: e[0])]
    right = pl.pallas_call(
        order_kernel,
        out_shape=shape((ways, pieces, flight, slots, across), bf16),
        in_specs=[whole()] * pieces,
        out_specs=whole(),
        compiler_params=params(),
        name="order",
    )(*hiddens)
    state = pl.pallas_call(
        fetch_kernel,
        out_shape=[shape((high, across), f32)] * 3,
        in_specs=[whole(pl.ANY)] + [hbm] * 3,
        out_specs=[whole()] * 3,
        scratch_shapes=[pltpu.SemaphoreType.DMA((3,))],
        compiler_params=params(),
        cost_estimate=cost(0, high * across * 24),
        name="fetch",
    )(hidden, pinned(master_weight), pinned(first_moment), pinned(second_moment))

    tiles = -(-high // LANES)
    middle = (tiles + 1) // 2 * LANES
    spans = [(0, middle), (middle, high)] if middle < high else [(0, high)]
    rows = []
    for start, stop in spans:
        piece = mine[:, :, start:stop]
        rows.append(
            [piece]
            + [
                lax.ppermute(piece, "expert", [(k, k ^ d) for k in range(sources)])
                for d in range(1, ways)
            ]
        )

    fresh, news = [], []
    for c, (start, stop) in enumerate(spans):
        out = pl.pallas_call(
            functools.partial(update_kernel, start, stop),
            out_shape=[shape((stop - start, across), bf16)]
            + [shape((stop - start, across), f32)] * 3,
            in_specs=[whole()] * (ways + 4),
            out_specs=[whole()] * 4,
            scratch_shapes=[pltpu.VMEM((stop - start, across), f32)],
            compiler_params=params(),
            cost_estimate=cost(2 * ways * count * (stop - start) * across, high * across * 26),
            name="update",
        )(*rows[c], right, *state)
        fresh.append(out[0])
        news += out[1:]
    crossed = [over_dp(piece, top) for piece in fresh]

    part = (ways, flight, slots, across)
    bit = 1
    kept = [[d for d in range(pieces) if not d & bit], [d for d in range(pieces) if d & bit]]
    keep, send, own_fresh = pl.pallas_call(
        functools.partial(partial_kernel, spans, kept),
        out_shape=[
            shape((pieces // 2, *part), f32),
            shape((pieces // 2, *part), bf16),
            shape((high, across), bf16),
        ],
        in_specs=[whole()] * ((ways + 1) * len(spans) + 1),
        out_specs=[whole()] * 3,
        scratch_shapes=[pltpu.VMEM((ways, pieces, flight, slots, across), f32)],
        compiler_params=params(),
        cost_estimate=cost(2 * ways * count * high * across, high * across * 12),
        name="partial",
    )(*[block for chunk in rows for block in chunk], *fresh, state[0])
    arrived = over_dp(send, bit)
    while bit < top:
        bit *= 2
        left = kept[0]
        kept = [[d for d in left if not d & bit], [d for d in left if d & bit]]
        chosen = [[left.index(d) for d in half] for half in kept]
        keep, send = pl.pallas_call(
            functools.partial(halve_kernel, chosen),
            out_shape=[
                shape((len(kept[0]), *part), f32),
                shape((len(kept[1]), *part), bf16),
            ],
            in_specs=[whole()] * 2,
            out_specs=[whole()] * 2,
            compiler_params=params(),
            name="halve",
        )(keep, arrived)
        arrived = over_dp(send, bit)
    if len(spans) > 1:
        crossed[0], keep = lax.optimization_barrier((crossed[0], keep))
    d_gate, d_up = pl.pallas_call(
        gate_kernel,
        out_shape=[shape(gate_stash.shape, bf16)] * 2,
        in_specs=[whole()] * 4,
        out_specs=[whole()] * 2,
        compiler_params=params(),
        name="gates",
    )(gate_stash, up_stash, keep, arrived)

    states = pl.pallas_call(
        functools.partial(store_kernel, spans),
        out_shape=[shape((high, across), f32)] * 3,
        in_specs=[whole()] * len(news),
        out_specs=[hbm] * 3,
        scratch_shapes=[pltpu.SemaphoreType.DMA((len(spans), 3))],
        compiler_params=params(),
        cost_estimate=cost(0, high * across * 24),
        name="store",
    )(*news)

    def join(entries, before):
        return pl.pallas_call(
            functools.partial(join_kernel, high, [entry[:3] for entry in entries]),
            out_shape=shape((pieces * high, across), bf16),
            in_specs=[whole(pl.ANY)] * len(entries) + [hbm] * len(before),
            out_specs=hbm,
            input_output_aliases={len(entries): 0} if before else {},
            scratch_shapes=[pltpu.SemaphoreType.DMA((len(entries),))],
            compiler_params=params(),
            name="join",
        )(*[entry[3] for entry in entries], *before)

    near, *far = spread([(0, 0, high, own_fresh)], top // 2)
    early, late = [near], far
    for (start, stop), piece in zip(spans[:-1], crossed[:-1]):
        near, *far = spread([(top, start, stop, piece)], top // 2)
        early.append(near)
        late += far
    joined = join(early, [])
    crossed[-1], joined, states, arrived = lax.optimization_barrier(
        (crossed[-1], joined, states, arrived)
    )
    joined = join(late + spread([(top, *spans[-1], crossed[-1])], top // 2), [joined])
    return (d_gate, d_up, *states, joined)


def solution(mesh):
    placed = (
        P("dp", "expert", None, None),
        P("dp", "expert", None),
        P("dp", "expert"),
        P("dp", None, "expert"),
        P("dp", None, "expert"),
        P("dp", "expert"),
        P("dp", "expert"),
        P("dp", "expert"),
    )
    return jax.shard_map(
        local,
        mesh=mesh,
        in_specs=placed,
        out_specs=(
            P("dp", None, "expert"),
            P("dp", None, "expert"),
            P("dp", "expert"),
            P("dp", "expert"),
            P("dp", "expert"),
            P(None, "expert"),
        ),
        check_vma=False,
    )
```

```python
import functools

import jax
import jax.numpy as jnp
from jax import lax
from jax.experimental import pallas as pl
from jax.experimental.pallas import tpu as pltpu
from jax.sharding import PartitionSpec as P

learning_rate = 0.01
beta_one = 0.9
beta_two = 0.95
decay_rate = 0.1
epsilon = 1e-08

bf16 = jnp.bfloat16
f32 = jnp.float32
VMEM_LIMIT = 40 * 1024 * 1024
LANES = 128


def params():
    return pltpu.CompilerParams(vmem_limit_bytes=VMEM_LIMIT)


def cost(flops, nbytes):
    return pl.CostEstimate(flops=flops, bytes_accessed=nbytes, transcendentals=0)


def take(refs, count):
    taken = refs[:count]
    del refs[:count]
    return taken


def wide(tiles):
    return tiles[0] if len(tiles) == 1 else jnp.concatenate(tiles, axis=1)


def tall(blocks):
    return blocks[0] if len(blocks) == 1 else jnp.concatenate(blocks, axis=0)


def seat_of(ways):
    return lax.axis_index("dp"), lax.rem(lax.axis_index("expert"), ways)


def scale_kernel(counts_in, router_in, rows_in, gate_in, up_in, out, hidden, *scratch):
    counts, router, rows, gate, up, sems = scratch
    copies = [
        pltpu.make_async_copy(source, target, sems.at[n])
        for n, (source, target) in enumerate(
            [
                (gate_in, gate),
                (up_in, up),
                (counts_in, counts),
                (router_in, router),
                (rows_in, rows),
            ]
        )
    ]
    for copy in copies:
        copy.start()
    flight, slots, width = rows.shape[1:]
    pieces = out.shape[0]
    piece = width // pieces
    ways = hidden.shape[0]
    copies[0].wait()
    copies[1].wait()
    g = gate[0].astype(f32)
    value = (g * jax.nn.sigmoid(g) * up[0].astype(f32)).astype(bf16)
    for f in range(flight):
        for v in range(ways):
            at = (f * ways + v) * slots
            hidden[v, f] = value[at : at + slots]
    for copy in copies[2:]:
        copy.wait()
    diagonal = lax.broadcasted_iota(jnp.int32, (slots, slots), 0) == lax.broadcasted_iota(
        jnp.int32, (slots, slots), 1
    )
    row = lax.broadcasted_iota(jnp.int32, (slots, 1), 0)
    for f in range(flight):
        weight = jnp.sum(
            jnp.where(diagonal, jnp.broadcast_to(router[0, f : f + 1, :], (slots, slots)), 0.0),
            axis=1,
            keepdims=True,
        )
        live = row < counts[0, f]
        scaled = jnp.where(live, weight * rows[0, f].astype(f32), 0.0).astype(bf16)
        for i in range(pieces):
            out[i, f] = scaled[:, i * piece : (i + 1) * piece]


def fetch_kernel(after, *refs):
    del after
    sems = refs[6]
    copies = [pltpu.make_async_copy(refs[n], refs[3 + n], sems.at[n]) for n in range(3)]
    for copy in copies:
        copy.start()
    for copy in copies:
        copy.wait()


def order_kernel(*refs):
    hiddens, right = refs[:-1], refs[-1]
    ways = right.shape[0]
    me, lane = seat_of(ways)
    for dj, hidden in enumerate(hiddens):
        for d in range(ways):
            right[d, me ^ dj] = hidden[lane ^ d]


def update_kernel(start, stop, *refs):
    refs = list(refs)
    rows = refs[:-9]
    right, master, first, second, fresh, new_master, new_first, new_second, gradient = refs[-9:]
    hidden = right[...].reshape(-1, right.shape[-1])
    left = tall([block[...].reshape(-1, stop - start) for block in rows])
    gradient[...] = lax.dot_general(
        left, hidden, (((0,), (0,)), ((), ())), preferred_element_type=f32
    )
    for low in range(start, stop, 128):
        end = min(low + 128, stop)
        here = pl.ds(low, end - low)
        there = pl.ds(low - start, end - low)
        grad = gradient[there]
        old = master[here]
        moment_a = beta_one * first[here] + (1.0 - beta_one) * grad
        moment_b = beta_two * second[here] + (1.0 - beta_two) * grad * grad
        step_size = (moment_a * (1.0 / (1.0 - beta_one**5))) / (
            jnp.sqrt(moment_b * (1.0 / (1.0 - beta_two**5))) + epsilon
        )
        updated = old - learning_rate * (step_size + decay_rate * old)
        fresh[there] = updated.astype(bf16)
        new_master[there] = updated
        new_first[there] = moment_a
        new_second[there] = moment_b


def partial_kernel(spans, kept, *refs):
    refs = list(refs)
    chunks = len(spans)
    master, keep, send, own_fresh, held = refs[-5:]
    fresh = refs[-5 - chunks : -5]
    rows = refs[: -5 - chunks]
    ways = held.shape[0]
    me, lane = seat_of(ways)
    left = wide(
        [
            tall([block[...].reshape(-1, stop - start) for block in rows[c * ways : (c + 1) * ways]])
            for c, (start, stop) in enumerate(spans)
        ]
    )
    share = jnp.dot(left, master[...].astype(bf16), preferred_element_type=f32)
    held[...] = share.reshape(held.shape)
    for out, chosen in ((keep, kept[0]), (send, kept[1])):
        for n, dj in enumerate(chosen):
            for d in range(ways):
                out[n, lane ^ d] = held[d, me ^ dj].astype(out.dtype)
    for c, (start, stop) in enumerate(spans):
        own_fresh[start:stop] = fresh[c][...]


def halve_kernel(kept, held, arrived, keep, send):
    for out, chosen in ((keep, kept[0]), (send, kept[1])):
        for n, m in enumerate(chosen):
            out[n] = (held[m] + arrived[m].astype(f32)).astype(out.dtype)


def store_kernel(spans, *refs):
    refs = list(refs)
    news = take(refs, 3 * len(spans))
    outs = take(refs, 3)
    (sems,) = refs
    copies = []
    for c, (start, stop) in enumerate(spans):
        for n in range(3):
            copy = pltpu.make_async_copy(
                news[3 * c + n], outs[n].at[pl.ds(start, stop - start)], sems.at[c, n]
            )
            copy.start()
            copies.append(copy)
    for copy in copies:
        copy.wait()


def gate_kernel(gate, up, held, arrived, d_gate, d_up):
    ways, flight, slots = held.shape[1:4]
    for f in range(flight):
        for v in range(ways):
            at = pl.ds((f * ways + v) * slots, slots)
            grad = held[0, v, f] + arrived[0, v, f].astype(f32)
            g = gate[0, at].astype(f32)
            u = up[0, at].astype(f32)
            sig = jax.nn.sigmoid(g)
            d_gate[0, at] = (grad * u * sig * (1.0 + g * (1.0 - sig))).astype(bf16)
            d_up[0, at] = (grad * (g * sig)).astype(bf16)


def join_kernel(high, entries, *refs):
    out, sems = refs[-2], refs[-1]
    me = lax.axis_index("dp")
    copies = []
    for n, (d, start, stop) in enumerate(entries):
        at = pl.multiple_of((me ^ d) * high + start, 16)
        copy = pltpu.make_async_copy(refs[n], out.at[pl.ds(at, stop - start)], sems.at[n])
        copy.start()
        copies.append(copy)
    for copy in copies:
        copy.wait()


def whole(memory=pltpu.VMEM):
    return pl.BlockSpec(memory_space=memory)


def shape(dims, kind):
    return jax.ShapeDtypeStruct(dims, kind)


def pinned(x):
    return pltpu.with_memory_space_constraint(x, pltpu.HBM)


def local(
    grad_rows,
    router_weight,
    send_counts,
    gate_stash,
    up_stash,
    master_weight,
    first_moment,
    second_moment,
):
    _, flight, slots, width = grad_rows.shape
    pieces = lax.axis_size("dp")
    sources = lax.axis_size("expert")
    ways = sources // flight
    high, across = master_weight.shape
    hbm = whole(pltpu.HBM)
    count = pieces * flight * slots

    def over_dp(x, d):
        return lax.ppermute(x, "dp", [(i, i ^ d) for i in range(pieces)])

    cut, hidden = pl.pallas_call(
        scale_kernel,
        out_shape=(
            shape((pieces, flight, slots, high), bf16),
            shape((ways, flight, slots, across), bf16),
        ),
        in_specs=[hbm] * 5,
        out_specs=[whole()] * 2,
        scratch_shapes=[
            pltpu.SMEM(send_counts.shape, jnp.int32),
            pltpu.VMEM(router_weight.shape, f32),
            pltpu.VMEM(grad_rows.shape, bf16),
            pltpu.VMEM(gate_stash.shape, bf16),
            pltpu.VMEM(up_stash.shape, bf16),
            pltpu.SemaphoreType.DMA((5,)),
        ],
        compiler_params=params(),
        name="scale",
    )(
        pinned(send_counts),
        pinned(router_weight),
        pinned(grad_rows),
        pinned(gate_stash),
        pinned(up_stash),
    )
    groups = [
        [i * sources + g * ways + v for i in range(pieces) for g in range(flight)]
        for v in range(ways)
    ]
    mine = lax.all_to_all(
        cut.reshape(pieces * flight, slots, high),
        ("dp", "expert"),
        split_axis=0,
        concat_axis=0,
        axis_index_groups=groups,
        tiled=True,
    )
    mine, hidden = lax.optimization_barrier((mine, hidden))
    top = pieces // 2

    def spread(entries, first):
        step = first
        while step:
            entries = entries + [(d ^ step, *span, over_dp(x, step)) for d, *span, x in entries]
            step //= 2
        return entries

    hiddens = [entry[1] for entry in sorted(spread([(0, hidden)], top), key=lambda e: e[0])]
    right = pl.pallas_call(
        order_kernel,
        out_shape=shape((ways, pieces, flight, slots, across), bf16),
        in_specs=[whole()] * pieces,
        out_specs=whole(),
        compiler_params=params(),
        name="order",
    )(*hiddens)
    state = pl.pallas_call(
        fetch_kernel,
        out_shape=[shape((high, across), f32)] * 3,
        in_specs=[whole(pl.ANY)] + [hbm] * 3,
        out_specs=[whole()] * 3,
        scratch_shapes=[pltpu.SemaphoreType.DMA((3,))],
        compiler_params=params(),
        cost_estimate=cost(0, high * across * 24),
        name="fetch",
    )(hidden, pinned(master_weight), pinned(first_moment), pinned(second_moment))

    tiles = -(-high // LANES)
    middle = (tiles + 1) // 2 * LANES
    spans = [(0, middle), (middle, high)] if middle < high else [(0, high)]
    def toward(x, d):
        return lax.ppermute(x, "expert", [(k, k ^ d) for k in range(sources)])

    rows = []
    for start, stop in spans:
        piece = mine[:, :, start:stop]
        direct = range(1, ways) if ways != 4 else (1, 2)
        rows.append([piece] + [toward(piece, d) for d in direct])
    if ways == 4:
        rows[0].append(toward(rows[0][2], 1))

    fresh, news = [], []
    for c, (start, stop) in enumerate(spans):
        if c and ways == 4:
            passed, _ = lax.optimization_barrier((rows[c][1], fresh[0]))
            rows[c].append(toward(passed, 2))
        out = pl.pallas_call(
            functools.partial(update_kernel, start, stop),
            out_shape=[shape((stop - start, across), bf16)]
            + [shape((stop - start, across), f32)] * 3,
            in_specs=[whole()] * (ways + 4),
            out_specs=[whole()] * 4,
            scratch_shapes=[pltpu.VMEM((stop - start, across), f32)],
            compiler_params=params(),
            cost_estimate=cost(2 * ways * count * (stop - start) * across, high * across * 26),
            name="update",
        )(*rows[c], right, *state)
        fresh.append(out[0])
        news += out[1:]
    crossed = [over_dp(piece, top) for piece in fresh]

    part = (ways, flight, slots, across)
    bit = 1
    kept = [[d for d in range(pieces) if not d & bit], [d for d in range(pieces) if d & bit]]
    keep, send, own_fresh = pl.pallas_call(
        functools.partial(partial_kernel, spans, kept),
        out_shape=[
            shape((pieces // 2, *part), f32),
            shape((pieces // 2, *part), bf16),
            shape((high, across), bf16),
        ],
        in_specs=[whole()] * ((ways + 1) * len(spans) + 1),
        out_specs=[whole()] * 3,
        scratch_shapes=[pltpu.VMEM((ways, pieces, flight, slots, across), f32)],
        compiler_params=params(),
        cost_estimate=cost(2 * ways * count * high * across, high * across * 12),
        name="partial",
    )(*[block for chunk in rows for block in chunk], *fresh, state[0])
    arrived = over_dp(send, bit)
    while bit < top:
        bit *= 2
        left = kept[0]
        kept = [[d for d in left if not d & bit], [d for d in left if d & bit]]
        chosen = [[left.index(d) for d in half] for half in kept]
        keep, send = pl.pallas_call(
            functools.partial(halve_kernel, chosen),
            out_shape=[
                shape((len(kept[0]), *part), f32),
                shape((len(kept[1]), *part), bf16),
            ],
            in_specs=[whole()] * 2,
            out_specs=[whole()] * 2,
            compiler_params=params(),
            name="halve",
        )(keep, arrived)
        arrived = over_dp(send, bit)
    if len(spans) > 1:
        crossed[0], keep = lax.optimization_barrier((crossed[0], keep))
    d_gate, d_up = pl.pallas_call(
        gate_kernel,
        out_shape=[shape(gate_stash.shape, bf16)] * 2,
        in_specs=[whole()] * 4,
        out_specs=[whole()] * 2,
        compiler_params=params(),
        name="gates",
    )(gate_stash, up_stash, keep, arrived)

    states = pl.pallas_call(
        functools.partial(store_kernel, spans),
        out_shape=[shape((high, across), f32)] * 3,
        in_specs=[whole()] * len(news),
        out_specs=[hbm] * 3,
        scratch_shapes=[pltpu.SemaphoreType.DMA((len(spans), 3))],
        compiler_params=params(),
        cost_estimate=cost(0, high * across * 24),
        name="store",
    )(*news)

    def join(entries, before):
        return pl.pallas_call(
            functools.partial(join_kernel, high, [entry[:3] for entry in entries]),
            out_shape=shape((pieces * high, across), bf16),
            in_specs=[whole(pl.ANY)] * len(entries) + [hbm] * len(before),
            out_specs=hbm,
            input_output_aliases={len(entries): 0} if before else {},
            scratch_shapes=[pltpu.SemaphoreType.DMA((len(entries),))],
            compiler_params=params(),
            name="join",
        )(*[entry[3] for entry in entries], *before)

    near, *far = spread([(0, 0, high, own_fresh)], top // 2)
    early, late = [near], far
    for (start, stop), piece in zip(spans[:-1], crossed[:-1]):
        near, *far = spread([(top, start, stop, piece)], top // 2)
        early.append(near)
        late += far
    joined = join(early, [])
    crossed[-1], joined, states, arrived = lax.optimization_barrier(
        (crossed[-1], joined, states, arrived)
    )
    joined = join(late + spread([(top, *spans[-1], crossed[-1])], top // 2), [joined])
    return (d_gate, d_up, *states, joined)


def solution(mesh):
    placed = (
        P("dp", "expert", None, None),
        P("dp", "expert", None),
        P("dp", "expert"),
        P("dp", None, "expert"),
        P("dp", None, "expert"),
        P("dp", "expert"),
        P("dp", "expert"),
        P("dp", "expert"),
    )
    return jax.shard_map(
        local,
        mesh=mesh,
        in_specs=placed,
        out_specs=(
            P("dp", None, "expert"),
            P("dp", None, "expert"),
            P("dp", "expert"),
            P("dp", "expert"),
            P("dp", "expert"),
            P(None, "expert"),
        ),
        check_vma=False,
    )
```

```python
import functools

import jax
import jax.numpy as jnp
from jax import lax
from jax.experimental import pallas as pl
from jax.experimental.pallas import tpu as pltpu
from jax.sharding import PartitionSpec as P

learning_rate = 0.01
beta_one = 0.9
beta_two = 0.95
decay_rate = 0.1
epsilon = 1e-08

bf16 = jnp.bfloat16
f32 = jnp.float32
VMEM_LIMIT = 40 * 1024 * 1024
LANES = 128
TILE = 128


def params():
    return pltpu.CompilerParams(vmem_limit_bytes=VMEM_LIMIT)


def cost(flops, nbytes):
    return pl.CostEstimate(flops=flops, bytes_accessed=nbytes, transcendentals=0)


def take(refs, count):
    taken = refs[:count]
    del refs[:count]
    return taken


def wide(tiles):
    return tiles[0] if len(tiles) == 1 else jnp.concatenate(tiles, axis=1)


def tall(blocks):
    return blocks[0] if len(blocks) == 1 else jnp.concatenate(blocks, axis=0)


def seat_of(ways):
    return lax.axis_index("dp"), lax.rem(lax.axis_index("expert"), ways)


def scale_kernel(counts_in, router_in, rows_in, gate_in, up_in, out, hidden, *scratch):
    counts, router, rows, gate, up, sems = scratch
    copies = [
        pltpu.make_async_copy(source, target, sems.at[n])
        for n, (source, target) in enumerate(
            [
                (gate_in, gate),
                (up_in, up),
                (counts_in, counts),
                (router_in, router),
                (rows_in, rows),
            ]
        )
    ]
    for copy in copies:
        copy.start()
    flight, slots, width = rows.shape[1:]
    pieces = out.shape[0]
    piece = width // pieces
    ways = hidden.shape[0]
    copies[0].wait()
    copies[1].wait()
    g = gate[0].astype(f32)
    value = (g * jax.nn.sigmoid(g) * up[0].astype(f32)).astype(bf16)
    for f in range(flight):
        for v in range(ways):
            at = (f * ways + v) * slots
            hidden[v, f] = value[at : at + slots]
    for copy in copies[2:]:
        copy.wait()
    diagonal = lax.broadcasted_iota(jnp.int32, (slots, slots), 0) == lax.broadcasted_iota(
        jnp.int32, (slots, slots), 1
    )
    row = lax.broadcasted_iota(jnp.int32, (slots, 1), 0)
    for f in range(flight):
        weight = jnp.sum(
            jnp.where(diagonal, jnp.broadcast_to(router[0, f : f + 1, :], (slots, slots)), 0.0),
            axis=1,
            keepdims=True,
        )
        live = row < counts[0, f]
        scaled = jnp.where(live, weight * rows[0, f].astype(f32), 0.0).astype(bf16)
        for i in range(pieces):
            out[i, f] = scaled[:, i * piece : (i + 1) * piece]


def order_kernel(*refs):
    hiddens, right = refs[:-1], refs[-1]
    ways = right.shape[0]
    me, lane = seat_of(ways)
    for dj, hidden in enumerate(hiddens):
        for d in range(ways):
            right[d, me ^ dj] = hidden[lane ^ d]


def update_kernel(start, stop, *refs):
    right, *state = refs[-14:-10]
    fresh, current, new_master, new_first, new_second, gradient, *old, sems = refs[-10:]
    rows = refs[:-14]
    tiles = [(low, min(low + TILE, stop)) for low in range(start, stop, TILE)]
    copies = [
        [
            pltpu.make_async_copy(
                state[n].at[low:end], old[n].at[low - start : end - start], sems.at[t, n]
            )
            for n in range(3)
        ]
        for t, (low, end) in enumerate(tiles)
    ]
    for tile in copies:
        for copy in tile:
            copy.start()
    left = tall([block[...].reshape(-1, stop - start) for block in rows])
    hidden = right[...].reshape(-1, right.shape[-1])
    gradient[...] = lax.dot_general(
        left, hidden, (((0,), (0,)), ((), ())), preferred_element_type=f32
    )
    for tile, (low, end) in zip(copies, tiles):
        for copy in tile:
            copy.wait()
        at = slice(low - start, end - start)
        grad = gradient[at]
        master = old[0][at]
        moment_a = beta_one * old[1][at] + (1.0 - beta_one) * grad
        moment_b = beta_two * old[2][at] + (1.0 - beta_two) * grad * grad
        step_size = (moment_a * (1.0 / (1.0 - beta_one**5))) / (
            jnp.sqrt(moment_b * (1.0 / (1.0 - beta_two**5))) + epsilon
        )
        updated = master - learning_rate * (step_size + decay_rate * master)
        fresh[at] = updated.astype(bf16)
        current[at] = master.astype(bf16)
        new_master[at] = updated
        new_first[at] = moment_a
        new_second[at] = moment_b


def partial_kernel(spans, kept, *refs):
    refs = list(refs)
    chunks = len(spans)
    keep, send, own_fresh, held = refs[-4:]
    rows, fresh, current = take(refs, chunks * held.shape[0]), take(refs, chunks), take(refs, chunks)
    ways = held.shape[0]
    me, lane = seat_of(ways)
    left = wide(
        [
            tall([block[...].reshape(-1, stop - start) for block in rows[c * ways : (c + 1) * ways]])
            for c, (start, stop) in enumerate(spans)
        ]
    )
    weight = tall([block[...] for block in current])
    share = jnp.dot(left, weight, preferred_element_type=f32)
    held[...] = share.reshape(held.shape)
    for out, chosen in ((keep, kept[0]), (send, kept[1])):
        for n, dj in enumerate(chosen):
            for d in range(ways):
                out[n, lane ^ d] = held[d, me ^ dj].astype(out.dtype)
    for c, (start, stop) in enumerate(spans):
        own_fresh[start:stop] = fresh[c][...]


def halve_kernel(kept, held, arrived, keep, send):
    for out, chosen in ((keep, kept[0]), (send, kept[1])):
        for n, m in enumerate(chosen):
            out[n] = (held[m] + arrived[m].astype(f32)).astype(out.dtype)


def store_kernel(spans, *refs):
    refs = list(refs)
    news = take(refs, 3 * len(spans))
    outs = take(refs, 3)
    (sems,) = refs
    copies = []
    for c, (start, stop) in enumerate(spans):
        for n in range(3):
            copy = pltpu.make_async_copy(
                news[3 * c + n], outs[n].at[pl.ds(start, stop - start)], sems.at[c, n]
            )
            copy.start()
            copies.append(copy)
    for copy in copies:
        copy.wait()


def gate_kernel(gate, up, held, arrived, d_gate, d_up):
    ways, flight, slots = held.shape[1:4]
    for f in range(flight):
        for v in range(ways):
            at = pl.ds((f * ways + v) * slots, slots)
            grad = held[0, v, f] + arrived[0, v, f].astype(f32)
            g = gate[0, at].astype(f32)
            u = up[0, at].astype(f32)
            sig = jax.nn.sigmoid(g)
            d_gate[0, at] = (grad * u * sig * (1.0 + g * (1.0 - sig))).astype(bf16)
            d_up[0, at] = (grad * (g * sig)).astype(bf16)


def join_kernel(high, entries, *refs):
    out, sems = refs[-2], refs[-1]
    me = lax.axis_index("dp")
    copies = []
    for n, (d, start, stop) in enumerate(entries):
        at = pl.multiple_of((me ^ d) * high + start, 16)
        copy = pltpu.make_async_copy(refs[n], out.at[pl.ds(at, stop - start)], sems.at[n])
        copy.start()
        copies.append(copy)
    for copy in copies:
        copy.wait()


def whole(memory=pltpu.VMEM):
    return pl.BlockSpec(memory_space=memory)


def shape(dims, kind):
    return jax.ShapeDtypeStruct(dims, kind)


def pinned(x):
    return pltpu.with_memory_space_constraint(x, pltpu.HBM)


def local(
    grad_rows,
    router_weight,
    send_counts,
    gate_stash,
    up_stash,
    master_weight,
    first_moment,
    second_moment,
):
    _, flight, slots, width = grad_rows.shape
    pieces = lax.axis_size("dp")
    sources = lax.axis_size("expert")
    ways = sources // flight
    high, across = master_weight.shape
    hbm = whole(pltpu.HBM)
    count = pieces * flight * slots

    def over_dp(x, d):
        return lax.ppermute(x, "dp", [(i, i ^ d) for i in range(pieces)])

    cut, hidden = pl.pallas_call(
        scale_kernel,
        out_shape=(
            shape((pieces, flight, slots, high), bf16),
            shape((ways, flight, slots, across), bf16),
        ),
        in_specs=[hbm] * 5,
        out_specs=[whole()] * 2,
        scratch_shapes=[
            pltpu.SMEM(send_counts.shape, jnp.int32),
            pltpu.VMEM(router_weight.shape, f32),
            pltpu.VMEM(grad_rows.shape, bf16),
            pltpu.VMEM(gate_stash.shape, bf16),
            pltpu.VMEM(up_stash.shape, bf16),
            pltpu.SemaphoreType.DMA((5,)),
        ],
        compiler_params=params(),
        name="scale",
    )(
        pinned(send_counts),
        pinned(router_weight),
        pinned(grad_rows),
        pinned(gate_stash),
        pinned(up_stash),
    )
    groups = [
        [i * sources + g * ways + v for i in range(pieces) for g in range(flight)]
        for v in range(ways)
    ]
    mine = lax.all_to_all(
        cut.reshape(pieces * flight, slots, high),
        ("dp", "expert"),
        split_axis=0,
        concat_axis=0,
        axis_index_groups=groups,
        tiled=True,
    )
    mine, hidden = lax.optimization_barrier((mine, hidden))
    top = pieces // 2

    def spread(entries, first):
        step = first
        while step:
            entries = entries + [(d ^ step, *span, over_dp(x, step)) for d, *span, x in entries]
            step //= 2
        return entries

    hiddens = [hidden] + [over_dp(hidden, d) for d in range(1, pieces)]
    right = pl.pallas_call(
        order_kernel,
        out_shape=shape((ways, pieces, flight, slots, across), bf16),
        in_specs=[whole()] * pieces,
        out_specs=whole(),
        compiler_params=params(),
        name="order",
    )(*hiddens)
    state = [pinned(master_weight), pinned(first_moment), pinned(second_moment)]

    tiles = -(-high // LANES)
    middle = (tiles + 1) // 2 * LANES
    spans = [(0, middle), (middle, high)] if middle < high else [(0, high)]
    rows = []
    for start, stop in spans:
        piece = mine[:, :, start:stop]
        rows.append(
            [piece]
            + [
                lax.ppermute(piece, "expert", [(k, k ^ d) for k in range(sources)])
                for d in range(1, ways)
            ]
        )

    fresh, current, news = [], [], []
    for c, (start, stop) in enumerate(spans):
        out = pl.pallas_call(
            functools.partial(update_kernel, start, stop),
            out_shape=[shape((stop - start, across), bf16)] * 2
            + [shape((stop - start, across), f32)] * 3,
            in_specs=[whole()] * (ways + 1) + [hbm] * 3,
            out_specs=[whole()] * 5,
            scratch_shapes=[pltpu.VMEM((stop - start, across), f32)] * 4
            + [pltpu.SemaphoreType.DMA((-(-(stop - start) // TILE), 3))],
            compiler_params=params(),
            cost_estimate=cost(2 * ways * count * (stop - start) * across, high * across * 26),
            name="update",
        )(*rows[c], right, *state)
        fresh.append(out[0])
        current.append(out[1])
        news += out[2:]
    crossed = [over_dp(piece, top) for piece in fresh]

    part = (ways, flight, slots, across)
    bit = 1
    kept = [[d for d in range(pieces) if not d & bit], [d for d in range(pieces) if d & bit]]
    keep, send, own_fresh = pl.pallas_call(
        functools.partial(partial_kernel, spans, kept),
        out_shape=[
            shape((pieces // 2, *part), f32),
            shape((pieces // 2, *part), bf16),
            shape((high, across), bf16),
        ],
        in_specs=[whole()] * ((ways + 2) * len(spans)),
        out_specs=[whole()] * 3,
        scratch_shapes=[pltpu.VMEM((ways, pieces, flight, slots, across), f32)],
        compiler_params=params(),
        cost_estimate=cost(2 * ways * count * high * across, high * across * 12),
        name="partial",
    )(*[block for chunk in rows for block in chunk], *fresh, *current)
    arrived = over_dp(send, bit)
    while bit < top:
        bit *= 2
        left = kept[0]
        kept = [[d for d in left if not d & bit], [d for d in left if d & bit]]
        chosen = [[left.index(d) for d in half] for half in kept]
        keep, send = pl.pallas_call(
            functools.partial(halve_kernel, chosen),
            out_shape=[
                shape((len(kept[0]), *part), f32),
                shape((len(kept[1]), *part), bf16),
            ],
            in_specs=[whole()] * 2,
            out_specs=[whole()] * 2,
            compiler_params=params(),
            name="halve",
        )(keep, arrived)
        arrived = over_dp(send, bit)
    if len(spans) > 1:
        crossed[0], keep = lax.optimization_barrier((crossed[0], keep))
    d_gate, d_up = pl.pallas_call(
        gate_kernel,
        out_shape=[shape(gate_stash.shape, bf16)] * 2,
        in_specs=[whole()] * 4,
        out_specs=[whole()] * 2,
        compiler_params=params(),
        name="gates",
    )(gate_stash, up_stash, keep, arrived)

    states = pl.pallas_call(
        functools.partial(store_kernel, spans),
        out_shape=[shape((high, across), f32)] * 3,
        in_specs=[whole()] * len(news),
        out_specs=[hbm] * 3,
        scratch_shapes=[pltpu.SemaphoreType.DMA((len(spans), 3))],
        compiler_params=params(),
        cost_estimate=cost(0, high * across * 24),
        name="store",
    )(*news)

    def join(entries, before):
        return pl.pallas_call(
            functools.partial(join_kernel, high, [entry[:3] for entry in entries]),
            out_shape=shape((pieces * high, across), bf16),
            in_specs=[whole(pl.ANY)] * len(entries) + [hbm] * len(before),
            out_specs=hbm,
            input_output_aliases={len(entries): 0} if before else {},
            scratch_shapes=[pltpu.SemaphoreType.DMA((len(entries),))],
            compiler_params=params(),
            name="join",
        )(*[entry[3] for entry in entries], *before)

    near, *far = spread([(0, 0, high, own_fresh)], top // 2)
    early, late = [near], far
    for (start, stop), piece in zip(spans[:-1], crossed[:-1]):
        near, *far = spread([(top, start, stop, piece)], top // 2)
        early.append(near)
        late += far
    joined = join(early, [])
    crossed[-1], joined, states, arrived = lax.optimization_barrier(
        (crossed[-1], joined, states, arrived)
    )
    joined = join(late + spread([(top, *spans[-1], crossed[-1])], top // 2), [joined])
    return (d_gate, d_up, *states, joined)


def solution(mesh):
    placed = (
        P("dp", "expert", None, None),
        P("dp", "expert", None),
        P("dp", "expert"),
        P("dp", None, "expert"),
        P("dp", None, "expert"),
        P("dp", "expert"),
        P("dp", "expert"),
        P("dp", "expert"),
    )
    return jax.shard_map(
        local,
        mesh=mesh,
        in_specs=placed,
        out_specs=(
            P("dp", None, "expert"),
            P("dp", None, "expert"),
            P("dp", "expert"),
            P("dp", "expert"),
            P("dp", "expert"),
            P(None, "expert"),
        ),
        check_vma=False,
    )
```

```python
import functools

import jax
import jax.numpy as jnp
from jax import lax
from jax.experimental import pallas as pl
from jax.experimental.pallas import tpu as pltpu
from jax.sharding import PartitionSpec as P

learning_rate = 0.01
beta_one = 0.9
beta_two = 0.95
decay_rate = 0.1
epsilon = 1e-08

bf16 = jnp.bfloat16
f32 = jnp.float32
VMEM_LIMIT = 40 * 1024 * 1024
LANES = 128


def params():
    return pltpu.CompilerParams(vmem_limit_bytes=VMEM_LIMIT)


def cost(flops, nbytes):
    return pl.CostEstimate(flops=flops, bytes_accessed=nbytes, transcendentals=0)


def take(refs, count):
    taken = refs[:count]
    del refs[:count]
    return taken


def wide(tiles):
    return tiles[0] if len(tiles) == 1 else jnp.concatenate(tiles, axis=1)


def tall(blocks):
    return blocks[0] if len(blocks) == 1 else jnp.concatenate(blocks, axis=0)


def seat_of(ways):
    return lax.axis_index("dp"), lax.rem(lax.axis_index("expert"), ways)


def scale_kernel(counts_in, router_in, rows_in, gate_in, up_in, out, hidden, *scratch):
    counts, router, rows, gate, up, sems = scratch
    copies = [
        pltpu.make_async_copy(source, target, sems.at[n])
        for n, (source, target) in enumerate(
            [
                (gate_in, gate),
                (up_in, up),
                (counts_in, counts),
                (router_in, router),
                (rows_in, rows),
            ]
        )
    ]
    for copy in copies:
        copy.start()
    flight, slots, width = rows.shape[1:]
    pieces = out.shape[0]
    piece = width // pieces
    ways = hidden.shape[0]
    copies[0].wait()
    copies[1].wait()
    g = gate[0].astype(f32)
    value = (g * jax.nn.sigmoid(g) * up[0].astype(f32)).astype(bf16)
    for f in range(flight):
        for v in range(ways):
            at = (f * ways + v) * slots
            hidden[v, f] = value[at : at + slots]
    for copy in copies[2:]:
        copy.wait()
    diagonal = lax.broadcasted_iota(jnp.int32, (slots, slots), 0) == lax.broadcasted_iota(
        jnp.int32, (slots, slots), 1
    )
    row = lax.broadcasted_iota(jnp.int32, (slots, 1), 0)
    for f in range(flight):
        weight = jnp.sum(
            jnp.where(diagonal, jnp.broadcast_to(router[0, f : f + 1, :], (slots, slots)), 0.0),
            axis=1,
            keepdims=True,
        )
        live = row < counts[0, f]
        scaled = jnp.where(live, weight * rows[0, f].astype(f32), 0.0).astype(bf16)
        for i in range(pieces):
            out[i, f] = scaled[:, i * piece : (i + 1) * piece]


def fetch_kernel(after, *refs):
    del after
    sems = refs[6]
    copies = [pltpu.make_async_copy(refs[n], refs[3 + n], sems.at[n]) for n in range(3)]
    for copy in copies:
        copy.start()
    for copy in copies:
        copy.wait()


def order_kernel(*refs):
    hiddens, right = refs[:-1], refs[-1]
    ways = right.shape[0]
    me, lane = seat_of(ways)
    for dj, hidden in enumerate(hiddens):
        for d in range(ways):
            right[d, me ^ dj] = hidden[lane ^ d]


def update_kernel(start, stop, *refs):
    refs = list(refs)
    rows = refs[:-9]
    right, master, first, second, fresh, new_master, new_first, new_second, gradient = refs[-9:]
    hidden = right[...].reshape(-1, right.shape[-1])
    left = tall([block[...].reshape(-1, stop - start) for block in rows])
    gradient[...] = lax.dot_general(
        left, hidden, (((0,), (0,)), ((), ())), preferred_element_type=f32
    )
    for low in range(start, stop, 128):
        end = min(low + 128, stop)
        here = pl.ds(low, end - low)
        there = pl.ds(low - start, end - low)
        grad = gradient[there]
        old = master[here]
        moment_a = beta_one * first[here] + (1.0 - beta_one) * grad
        moment_b = beta_two * second[here] + (1.0 - beta_two) * grad * grad
        step_size = (moment_a * (1.0 / (1.0 - beta_one**5))) / (
            jnp.sqrt(moment_b * (1.0 / (1.0 - beta_two**5))) + epsilon
        )
        updated = old - learning_rate * (step_size + decay_rate * old)
        fresh[there] = updated.astype(bf16)
        new_master[there] = updated
        new_first[there] = moment_a
        new_second[there] = moment_b


def partial_kernel(spans, kept, *refs):
    refs = list(refs)
    chunks = len(spans)
    master, keep, send, own_fresh, held = refs[-5:]
    fresh = refs[-5 - chunks : -5]
    rows = refs[: -5 - chunks]
    ways = held.shape[0]
    me, lane = seat_of(ways)
    left = wide(
        [
            tall([block[...].reshape(-1, stop - start) for block in rows[c * ways : (c + 1) * ways]])
            for c, (start, stop) in enumerate(spans)
        ]
    )
    share = jnp.dot(left, master[...].astype(bf16), preferred_element_type=f32)
    held[...] = share.reshape(held.shape)
    for out, chosen in ((keep, kept[0]), (send, kept[1])):
        for n, dj in enumerate(chosen):
            for d in range(ways):
                out[n, lane ^ d] = held[d, me ^ dj].astype(out.dtype)
    for c, (start, stop) in enumerate(spans):
        own_fresh[start:stop] = fresh[c][...]


def finish_kernel(spans, kept, *refs):
    refs = list(refs)
    gradient, held = refs[-2:]
    ways = held.shape[0]
    rows = take(refs, ways * len(spans))
    right, *state = take(refs, 4)
    earlier = take(refs, len(spans) - 1)
    fresh, *news = take(refs, 4)
    keep, send, own_fresh = take(refs, 3)
    update_kernel(*spans[-1], *rows[-ways:], right, *state, fresh, *news, gradient)
    partial_kernel(
        spans, kept, *rows, *earlier, fresh, state[0], keep, send, own_fresh, held
    )


def halve_kernel(kept, held, arrived, keep, send):
    for out, chosen in ((keep, kept[0]), (send, kept[1])):
        for n, m in enumerate(chosen):
            out[n] = (held[m] + arrived[m].astype(f32)).astype(out.dtype)


def store_kernel(spans, *refs):
    refs = list(refs)
    news = take(refs, 3 * len(spans))
    outs = take(refs, 3)
    (sems,) = refs
    copies = []
    for c, (start, stop) in enumerate(spans):
        for n in range(3):
            copy = pltpu.make_async_copy(
                news[3 * c + n], outs[n].at[pl.ds(start, stop - start)], sems.at[c, n]
            )
            copy.start()
            copies.append(copy)
    for copy in copies:
        copy.wait()


def gate_kernel(gate, up, held, arrived, d_gate, d_up):
    ways, flight, slots = held.shape[1:4]
    for f in range(flight):
        for v in range(ways):
            at = pl.ds((f * ways + v) * slots, slots)
            grad = held[0, v, f] + arrived[0, v, f].astype(f32)
            g = gate[0, at].astype(f32)
            u = up[0, at].astype(f32)
            sig = jax.nn.sigmoid(g)
            d_gate[0, at] = (grad * u * sig * (1.0 + g * (1.0 - sig))).astype(bf16)
            d_up[0, at] = (grad * (g * sig)).astype(bf16)


def join_kernel(high, entries, *refs):
    out, sems = refs[-2], refs[-1]
    me = lax.axis_index("dp")
    copies = []
    for n, (d, start, stop) in enumerate(entries):
        at = pl.multiple_of((me ^ d) * high + start, 16)
        copy = pltpu.make_async_copy(refs[n], out.at[pl.ds(at, stop - start)], sems.at[n])
        copy.start()
        copies.append(copy)
    for copy in copies:
        copy.wait()


def whole(memory=pltpu.VMEM):
    return pl.BlockSpec(memory_space=memory)


def shape(dims, kind):
    return jax.ShapeDtypeStruct(dims, kind)


def pinned(x):
    return pltpu.with_memory_space_constraint(x, pltpu.HBM)


def local(
    grad_rows,
    router_weight,
    send_counts,
    gate_stash,
    up_stash,
    master_weight,
    first_moment,
    second_moment,
):
    _, flight, slots, width = grad_rows.shape
    pieces = lax.axis_size("dp")
    sources = lax.axis_size("expert")
    ways = sources // flight
    high, across = master_weight.shape
    hbm = whole(pltpu.HBM)
    count = pieces * flight * slots

    def over_dp(x, d):
        return lax.ppermute(x, "dp", [(i, i ^ d) for i in range(pieces)])

    cut, hidden = pl.pallas_call(
        scale_kernel,
        out_shape=(
            shape((pieces, flight, slots, high), bf16),
            shape((ways, flight, slots, across), bf16),
        ),
        in_specs=[hbm] * 5,
        out_specs=[whole()] * 2,
        scratch_shapes=[
            pltpu.SMEM(send_counts.shape, jnp.int32),
            pltpu.VMEM(router_weight.shape, f32),
            pltpu.VMEM(grad_rows.shape, bf16),
            pltpu.VMEM(gate_stash.shape, bf16),
            pltpu.VMEM(up_stash.shape, bf16),
            pltpu.SemaphoreType.DMA((5,)),
        ],
        compiler_params=params(),
        name="scale",
    )(
        pinned(send_counts),
        pinned(router_weight),
        pinned(grad_rows),
        pinned(gate_stash),
        pinned(up_stash),
    )
    groups = [
        [i * sources + g * ways + v for i in range(pieces) for g in range(flight)]
        for v in range(ways)
    ]
    mine = lax.all_to_all(
        cut.reshape(pieces * flight, slots, high),
        ("dp", "expert"),
        split_axis=0,
        concat_axis=0,
        axis_index_groups=groups,
        tiled=True,
    )
    mine, hidden = lax.optimization_barrier((mine, hidden))
    top = pieces // 2

    def spread(entries, first):
        step = first
        while step:
            entries = entries + [(d ^ step, *span, over_dp(x, step)) for d, *span, x in entries]
            step //= 2
        return entries

    hiddens = [entry[1] for entry in sorted(spread([(0, hidden)], top), key=lambda e: e[0])]
    right = pl.pallas_call(
        order_kernel,
        out_shape=shape((ways, pieces, flight, slots, across), bf16),
        in_specs=[whole()] * pieces,
        out_specs=whole(),
        compiler_params=params(),
        name="order",
    )(*hiddens)
    state = pl.pallas_call(
        fetch_kernel,
        out_shape=[shape((high, across), f32)] * 3,
        in_specs=[whole(pl.ANY)] + [hbm] * 3,
        out_specs=[whole()] * 3,
        scratch_shapes=[pltpu.SemaphoreType.DMA((3,))],
        compiler_params=params(),
        cost_estimate=cost(0, high * across * 24),
        name="fetch",
    )(hidden, pinned(master_weight), pinned(first_moment), pinned(second_moment))

    tiles = -(-high // LANES)
    middle = (tiles + 1) // 2 * LANES
    spans = [(0, middle), (middle, high)] if middle < high else [(0, high)]
    def square(piece):
        return [piece] + [
            lax.ppermute(piece, "expert", [(k, k ^ d) for k in range(sources)])
            for d in range(1, ways)
        ]

    part = (ways, flight, slots, across)
    bit = 1
    kept = [[d for d in range(pieces) if not d & bit], [d for d in range(pieces) if d & bit]]
    rows, fresh, news = [], [], []
    for c, (start, stop) in enumerate(spans):
        piece = mine[:, :, start:stop]
        if c:
            piece, _ = lax.optimization_barrier((piece, fresh[-1]))
        rows.append(square(piece))
        tall_shape = (stop - start, across)
        results = [shape(tall_shape, bf16)] + [shape(tall_shape, f32)] * 3
        scratch = [pltpu.VMEM(tall_shape, f32)]
        operands = rows[c] + [right, *state]
        body = functools.partial(update_kernel, start, stop)
        if stop == high:
            operands = [block for chunk in rows for block in chunk] + [right, *state, *fresh]
            body = functools.partial(finish_kernel, spans, kept)
            results += [
                shape((pieces // 2, *part), f32),
                shape((pieces // 2, *part), bf16),
                shape((high, across), bf16),
            ]
            scratch += [pltpu.VMEM((ways, pieces, flight, slots, across), f32)]
        out = pl.pallas_call(
            body,
            out_shape=results,
            in_specs=[whole()] * len(operands),
            out_specs=[whole()] * len(results),
            scratch_shapes=scratch,
            compiler_params=params(),
            cost_estimate=cost(2 * ways * count * (stop - start) * across, high * across * 26),
            name="update",
        )(*operands)
        fresh.append(out[0])
        news += out[1:4]
    keep, send, own_fresh = out[4:]
    crossed = [over_dp(piece, top) for piece in fresh]
    if len(spans) > 1:
        send, crossed[0] = lax.optimization_barrier((send, crossed[0]))
    arrived = over_dp(send, bit)
    while bit < top:
        bit *= 2
        left = kept[0]
        kept = [[d for d in left if not d & bit], [d for d in left if d & bit]]
        chosen = [[left.index(d) for d in half] for half in kept]
        keep, send = pl.pallas_call(
            functools.partial(halve_kernel, chosen),
            out_shape=[
                shape((len(kept[0]), *part), f32),
                shape((len(kept[1]), *part), bf16),
            ],
            in_specs=[whole()] * 2,
            out_specs=[whole()] * 2,
            compiler_params=params(),
            name="halve",
        )(keep, arrived)
        arrived = over_dp(send, bit)
    d_gate, d_up = pl.pallas_call(
        gate_kernel,
        out_shape=[shape(gate_stash.shape, bf16)] * 2,
        in_specs=[whole()] * 4,
        out_specs=[whole()] * 2,
        compiler_params=params(),
        name="gates",
    )(gate_stash, up_stash, keep, arrived)

    states = pl.pallas_call(
        functools.partial(store_kernel, spans),
        out_shape=[shape((high, across), f32)] * 3,
        in_specs=[whole()] * len(news),
        out_specs=[hbm] * 3,
        scratch_shapes=[pltpu.SemaphoreType.DMA((len(spans), 3))],
        compiler_params=params(),
        cost_estimate=cost(0, high * across * 24),
        name="store",
    )(*news)

    def join(entries, before):
        return pl.pallas_call(
            functools.partial(join_kernel, high, [entry[:3] for entry in entries]),
            out_shape=shape((pieces * high, across), bf16),
            in_specs=[whole(pl.ANY)] * len(entries) + [hbm] * len(before),
            out_specs=hbm,
            input_output_aliases={len(entries): 0} if before else {},
            scratch_shapes=[pltpu.SemaphoreType.DMA((len(entries),))],
            compiler_params=params(),
            name="join",
        )(*[entry[3] for entry in entries], *before)

    near, *far = spread([(0, 0, high, own_fresh)], top // 2)
    early, late = [near], far
    for (start, stop), piece in zip(spans[:-1], crossed[:-1]):
        near, *far = spread([(top, start, stop, piece)], top // 2)
        early.append(near)
        late += far
    joined = join(early, [])
    crossed[-1], joined, states, arrived = lax.optimization_barrier(
        (crossed[-1], joined, states, arrived)
    )
    joined = join(late + spread([(top, *spans[-1], crossed[-1])], top // 2), [joined])
    return (d_gate, d_up, *states, joined)


def solution(mesh):
    placed = (
        P("dp", "expert", None, None),
        P("dp", "expert", None),
        P("dp", "expert"),
        P("dp", None, "expert"),
        P("dp", None, "expert"),
        P("dp", "expert"),
        P("dp", "expert"),
        P("dp", "expert"),
    )
    return jax.shard_map(
        local,
        mesh=mesh,
        in_specs=placed,
        out_specs=(
            P("dp", None, "expert"),
            P("dp", None, "expert"),
            P("dp", "expert"),
            P("dp", "expert"),
            P("dp", "expert"),
            P(None, "expert"),
        ),
        check_vma=False,
    )
```

```python
import functools

import jax
import jax.numpy as jnp
from jax import lax
from jax.experimental import pallas as pl
from jax.experimental.pallas import tpu as pltpu
from jax.sharding import PartitionSpec as P

learning_rate = 0.01
beta_one = 0.9
beta_two = 0.95
decay_rate = 0.1
epsilon = 1e-08

bf16 = jnp.bfloat16
f32 = jnp.float32
VMEM_LIMIT = 40 * 1024 * 1024
LANES = 128


def params():
    return pltpu.CompilerParams(vmem_limit_bytes=VMEM_LIMIT)


def cost(flops, nbytes):
    return pl.CostEstimate(flops=flops, bytes_accessed=nbytes, transcendentals=0)


def take(refs, count):
    taken = refs[:count]
    del refs[:count]
    return taken


def wide(tiles):
    return tiles[0] if len(tiles) == 1 else jnp.concatenate(tiles, axis=1)


def tall(blocks):
    return blocks[0] if len(blocks) == 1 else jnp.concatenate(blocks, axis=0)


def seat_of(ways):
    return lax.axis_index("dp"), lax.rem(lax.axis_index("expert"), ways)


def fetch(state, targets, start, sems):
    copies = []
    for n in range(3):
        rows = pl.ds(start, targets[n].shape[0])
        copies.append(pltpu.make_async_copy(state[n].at[rows], targets[n], sems.at[n]))
        copies[-1].start()
    return copies


def scale_kernel(counts_in, router_in, rows_in, gate_in, up_in, *refs):
    state, (out, hidden), fetched = refs[:3], refs[3:5], refs[5:8]
    counts, router, rows, gate, up, sems, fetch_sems = refs[8:]
    copies = [
        pltpu.make_async_copy(source, target, sems.at[n])
        for n, (source, target) in enumerate(
            [
                (gate_in, gate),
                (up_in, up),
                (counts_in, counts),
                (router_in, router),
                (rows_in, rows),
            ]
        )
    ]
    for copy in copies:
        copy.start()
    fetches = fetch(state, fetched, 0, fetch_sems)
    flight, slots, width = rows.shape[1:]
    pieces = out.shape[0]
    piece = width // pieces
    ways = hidden.shape[0]
    copies[0].wait()
    copies[1].wait()
    g = gate[0].astype(f32)
    value = (g * jax.nn.sigmoid(g) * up[0].astype(f32)).astype(bf16)
    for f in range(flight):
        for v in range(ways):
            at = (f * ways + v) * slots
            hidden[v, f] = value[at : at + slots]
    for copy in copies[2:]:
        copy.wait()
    diagonal = lax.broadcasted_iota(jnp.int32, (slots, slots), 0) == lax.broadcasted_iota(
        jnp.int32, (slots, slots), 1
    )
    row = lax.broadcasted_iota(jnp.int32, (slots, 1), 0)
    for f in range(flight):
        weight = jnp.sum(
            jnp.where(diagonal, jnp.broadcast_to(router[0, f : f + 1, :], (slots, slots)), 0.0),
            axis=1,
            keepdims=True,
        )
        live = row < counts[0, f]
        scaled = jnp.where(live, weight * rows[0, f].astype(f32), 0.0).astype(bf16)
        for i in range(pieces):
            out[i, f] = scaled[:, i * piece : (i + 1) * piece]
    for copy in fetches:
        copy.wait()


def fetch_kernel(start, after, *refs):
    del after
    for copy in fetch(refs[:3], refs[3:6], start, refs[6]):
        copy.wait()


def order_kernel(*refs):
    hiddens, right = refs[:-1], refs[-1]
    ways = right.shape[0]
    me, lane = seat_of(ways)
    for dj, hidden in enumerate(hiddens):
        for d in range(ways):
            right[d, me ^ dj] = hidden[lane ^ d]


def update_kernel(start, stop, *refs):
    refs = list(refs)
    rows = refs[:-9]
    right, master, first, second, fresh, new_master, new_first, new_second, gradient = refs[-9:]
    hidden = right[...].reshape(-1, right.shape[-1])
    left = tall([block[...].reshape(-1, stop - start) for block in rows])
    gradient[...] = lax.dot_general(
        left, hidden, (((0,), (0,)), ((), ())), preferred_element_type=f32
    )
    for low in range(start, stop, 128):
        end = min(low + 128, stop)
        there = pl.ds(low - start, end - low)
        grad = gradient[there]
        old = master[there]
        moment_a = beta_one * first[there] + (1.0 - beta_one) * grad
        moment_b = beta_two * second[there] + (1.0 - beta_two) * grad * grad
        step_size = (moment_a * (1.0 / (1.0 - beta_one**5))) / (
            jnp.sqrt(moment_b * (1.0 / (1.0 - beta_two**5))) + epsilon
        )
        updated = old - learning_rate * (step_size + decay_rate * old)
        fresh[there] = updated.astype(bf16)
        new_master[there] = updated
        new_first[there] = moment_a
        new_second[there] = moment_b


def partial_kernel(spans, kept, *refs):
    refs = list(refs)
    chunks = len(spans)
    keep, send, own_fresh, held = refs[-4:]
    ways = held.shape[0]
    rows, fresh, master = take(refs, ways * chunks), take(refs, chunks), take(refs, chunks)
    me, lane = seat_of(ways)
    left = wide(
        [
            tall([block[...].reshape(-1, stop - start) for block in rows[c * ways : (c + 1) * ways]])
            for c, (start, stop) in enumerate(spans)
        ]
    )
    current = tall([block[...].astype(bf16) for block in master])
    share = jnp.dot(left, current, preferred_element_type=f32)
    held[...] = share.reshape(held.shape)
    for out, chosen in ((keep, kept[0]), (send, kept[1])):
        for n, dj in enumerate(chosen):
            for d in range(ways):
                out[n, lane ^ d] = held[d, me ^ dj].astype(out.dtype)
    for c, (start, stop) in enumerate(spans):
        own_fresh[start:stop] = fresh[c][...]


def halve_kernel(kept, held, arrived, keep, send):
    for out, chosen in ((keep, kept[0]), (send, kept[1])):
        for n, m in enumerate(chosen):
            out[n] = (held[m] + arrived[m].astype(f32)).astype(out.dtype)


def store_kernel(spans, *refs):
    refs = list(refs)
    news = take(refs, 3 * len(spans))
    outs = take(refs, 3)
    (sems,) = refs
    copies = []
    for c, (start, stop) in enumerate(spans):
        for n in range(3):
            copy = pltpu.make_async_copy(
                news[3 * c + n], outs[n].at[pl.ds(start, stop - start)], sems.at[c, n]
            )
            copy.start()
            copies.append(copy)
    for copy in copies:
        copy.wait()


def gate_kernel(gate, up, held, arrived, d_gate, d_up):
    ways, flight, slots = held.shape[1:4]
    for f in range(flight):
        for v in range(ways):
            at = pl.ds((f * ways + v) * slots, slots)
            grad = held[0, v, f] + arrived[0, v, f].astype(f32)
            g = gate[0, at].astype(f32)
            u = up[0, at].astype(f32)
            sig = jax.nn.sigmoid(g)
            d_gate[0, at] = (grad * u * sig * (1.0 + g * (1.0 - sig))).astype(bf16)
            d_up[0, at] = (grad * (g * sig)).astype(bf16)


def join_kernel(high, entries, *refs):
    out, sems = refs[-2], refs[-1]
    me = lax.axis_index("dp")
    copies = []
    for n, (d, start, stop) in enumerate(entries):
        at = pl.multiple_of((me ^ d) * high + start, 16)
        copy = pltpu.make_async_copy(refs[n], out.at[pl.ds(at, stop - start)], sems.at[n])
        copy.start()
        copies.append(copy)
    for copy in copies:
        copy.wait()


def whole(memory=pltpu.VMEM):
    return pl.BlockSpec(memory_space=memory)


def shape(dims, kind):
    return jax.ShapeDtypeStruct(dims, kind)


def pinned(x):
    return pltpu.with_memory_space_constraint(x, pltpu.HBM)


def local(
    grad_rows,
    router_weight,
    send_counts,
    gate_stash,
    up_stash,
    master_weight,
    first_moment,
    second_moment,
):
    _, flight, slots, width = grad_rows.shape
    pieces = lax.axis_size("dp")
    sources = lax.axis_size("expert")
    ways = sources // flight
    high, across = master_weight.shape
    hbm = whole(pltpu.HBM)
    count = pieces * flight * slots

    def over_dp(x, d):
        return lax.ppermute(x, "dp", [(i, i ^ d) for i in range(pieces)])

    tiles = -(-high // LANES)
    middle = (tiles + 1) // 2 * LANES
    spans = [(0, middle), (middle, high)] if middle < high else [(0, high)]
    state = [pinned(master_weight), pinned(first_moment), pinned(second_moment)]
    cut, hidden, *fetched = pl.pallas_call(
        scale_kernel,
        out_shape=(
            shape((pieces, flight, slots, high), bf16),
            shape((ways, flight, slots, across), bf16),
        )
        + (shape((spans[0][1], across), f32),) * 3,
        in_specs=[hbm] * 8,
        out_specs=[whole()] * 5,
        scratch_shapes=[
            pltpu.SMEM(send_counts.shape, jnp.int32),
            pltpu.VMEM(router_weight.shape, f32),
            pltpu.VMEM(grad_rows.shape, bf16),
            pltpu.VMEM(gate_stash.shape, bf16),
            pltpu.VMEM(up_stash.shape, bf16),
            pltpu.SemaphoreType.DMA((5,)),
            pltpu.SemaphoreType.DMA((3,)),
        ],
        compiler_params=params(),
        name="scale",
    )(
        pinned(send_counts),
        pinned(router_weight),
        pinned(grad_rows),
        pinned(gate_stash),
        pinned(up_stash),
        *state,
    )
    groups = [
        [i * sources + g * ways + v for i in range(pieces) for g in range(flight)]
        for v in range(ways)
    ]
    mine = lax.all_to_all(
        cut.reshape(pieces * flight, slots, high),
        ("dp", "expert"),
        split_axis=0,
        concat_axis=0,
        axis_index_groups=groups,
        tiled=True,
    )
    mine, hidden = lax.optimization_barrier((mine, hidden))
    top = pieces // 2

    def spread(entries, first):
        step = first
        while step:
            entries = entries + [(d ^ step, *span, over_dp(x, step)) for d, *span, x in entries]
            step //= 2
        return entries

    hiddens = [entry[1] for entry in sorted(spread([(0, hidden)], top), key=lambda e: e[0])]
    right = pl.pallas_call(
        order_kernel,
        out_shape=shape((ways, pieces, flight, slots, across), bf16),
        in_specs=[whole()] * pieces,
        out_specs=whole(),
        compiler_params=params(),
        name="order",
    )(*hiddens)
    rows = []
    for start, stop in spans:
        piece = mine[:, :, start:stop]
        rows.append(
            [piece]
            + [
                lax.ppermute(piece, "expert", [(k, k ^ d) for k in range(sources)])
                for d in range(1, ways)
            ]
        )

    fresh, news, masters = [], [], []
    for c, (start, stop) in enumerate(spans):
        if c:
            fetched = pl.pallas_call(
                functools.partial(fetch_kernel, start),
                out_shape=[shape((stop - start, across), f32)] * 3,
                in_specs=[whole(pl.ANY)] + [hbm] * 3,
                out_specs=[whole()] * 3,
                scratch_shapes=[pltpu.SemaphoreType.DMA((3,))],
                compiler_params=params(),
                name="fetch",
            )(fresh[-1], *state)
        masters.append(fetched[0])
        out = pl.pallas_call(
            functools.partial(update_kernel, start, stop),
            out_shape=[shape((stop - start, across), bf16)]
            + [shape((stop - start, across), f32)] * 3,
            in_specs=[whole()] * (ways + 4),
            out_specs=[whole()] * 4,
            scratch_shapes=[pltpu.VMEM((stop - start, across), f32)],
            compiler_params=params(),
            cost_estimate=cost(2 * ways * count * (stop - start) * across, high * across * 26),
            name="update",
        )(*rows[c], right, *fetched)
        fresh.append(out[0])
        news += out[1:]
    crossed = [over_dp(piece, top) for piece in fresh]

    part = (ways, flight, slots, across)
    bit = 1
    kept = [[d for d in range(pieces) if not d & bit], [d for d in range(pieces) if d & bit]]
    keep, send, own_fresh = pl.pallas_call(
        functools.partial(partial_kernel, spans, kept),
        out_shape=[
            shape((pieces // 2, *part), f32),
            shape((pieces // 2, *part), bf16),
            shape((high, across), bf16),
        ],
        in_specs=[whole()] * ((ways + 2) * len(spans)),
        out_specs=[whole()] * 3,
        scratch_shapes=[pltpu.VMEM((ways, pieces, flight, slots, across), f32)],
        compiler_params=params(),
        cost_estimate=cost(2 * ways * count * high * across, high * across * 12),
        name="partial",
    )(*[block for chunk in rows for block in chunk], *fresh, *masters)
    arrived = over_dp(send, bit)
    while bit < top:
        bit *= 2
        left = kept[0]
        kept = [[d for d in left if not d & bit], [d for d in left if d & bit]]
        chosen = [[left.index(d) for d in half] for half in kept]
        keep, send = pl.pallas_call(
            functools.partial(halve_kernel, chosen),
            out_shape=[
                shape((len(kept[0]), *part), f32),
                shape((len(kept[1]), *part), bf16),
            ],
            in_specs=[whole()] * 2,
            out_specs=[whole()] * 2,
            compiler_params=params(),
            name="halve",
        )(keep, arrived)
        arrived = over_dp(send, bit)
    if len(spans) > 1:
        crossed[0], keep = lax.optimization_barrier((crossed[0], keep))
    d_gate, d_up = pl.pallas_call(
        gate_kernel,
        out_shape=[shape(gate_stash.shape, bf16)] * 2,
        in_specs=[whole()] * 4,
        out_specs=[whole()] * 2,
        compiler_params=params(),
        name="gates",
    )(gate_stash, up_stash, keep, arrived)

    states = pl.pallas_call(
        functools.partial(store_kernel, spans),
        out_shape=[shape((high, across), f32)] * 3,
        in_specs=[whole()] * len(news),
        out_specs=[hbm] * 3,
        scratch_shapes=[pltpu.SemaphoreType.DMA((len(spans), 3))],
        compiler_params=params(),
        cost_estimate=cost(0, high * across * 24),
        name="store",
    )(*news)

    def join(entries, before):
        return pl.pallas_call(
            functools.partial(join_kernel, high, [entry[:3] for entry in entries]),
            out_shape=shape((pieces * high, across), bf16),
            in_specs=[whole(pl.ANY)] * len(entries) + [hbm] * len(before),
            out_specs=hbm,
            input_output_aliases={len(entries): 0} if before else {},
            scratch_shapes=[pltpu.SemaphoreType.DMA((len(entries),))],
            compiler_params=params(),
            name="join",
        )(*[entry[3] for entry in entries], *before)

    near, *far = spread([(0, 0, high, own_fresh)], top // 2)
    early, late = [near], far
    for (start, stop), piece in zip(spans[:-1], crossed[:-1]):
        near, *far = spread([(top, start, stop, piece)], top // 2)
        early.append(near)
        late += far
    joined = join(early, [])
    crossed[-1], joined, states, arrived = lax.optimization_barrier(
        (crossed[-1], joined, states, arrived)
    )
    joined = join(late + spread([(top, *spans[-1], crossed[-1])], top // 2), [joined])
    return (d_gate, d_up, *states, joined)


def solution(mesh):
    placed = (
        P("dp", "expert", None, None),
        P("dp", "expert", None),
        P("dp", "expert"),
        P("dp", None, "expert"),
        P("dp", None, "expert"),
        P("dp", "expert"),
        P("dp", "expert"),
        P("dp", "expert"),
    )
    return jax.shard_map(
        local,
        mesh=mesh,
        in_specs=placed,
        out_specs=(
            P("dp", None, "expert"),
            P("dp", None, "expert"),
            P("dp", "expert"),
            P("dp", "expert"),
            P("dp", "expert"),
            P(None, "expert"),
        ),
        check_vma=False,
    )
```

```python
import functools

import jax
import jax.numpy as jnp
from jax import lax
from jax.experimental import pallas as pl
from jax.experimental.pallas import tpu as pltpu
from jax.sharding import PartitionSpec as P

learning_rate = 0.01
beta_one = 0.9
beta_two = 0.95
decay_rate = 0.1
epsilon = 1e-08

bf16 = jnp.bfloat16
f32 = jnp.float32
VMEM_LIMIT = 40 * 1024 * 1024
LANES = 128


def params():
    return pltpu.CompilerParams(vmem_limit_bytes=VMEM_LIMIT)


def cost(flops, nbytes):
    return pl.CostEstimate(flops=flops, bytes_accessed=nbytes, transcendentals=0)


def take(refs, count):
    taken = refs[:count]
    del refs[:count]
    return taken


def wide(tiles):
    return tiles[0] if len(tiles) == 1 else jnp.concatenate(tiles, axis=1)


def tall(blocks):
    return blocks[0] if len(blocks) == 1 else jnp.concatenate(blocks, axis=0)


def seat_of(ways):
    seat = lax.axis_index("expert")
    return lax.axis_index("dp"), lax.rem(seat, ways), lax.div(seat, ways)


def fetch(state, targets, start, sems):
    copies = []
    for n in range(3):
        rows = pl.ds(start, targets[n].shape[0])
        copies.append(pltpu.make_async_copy(state[n].at[rows], targets[n], sems.at[n]))
        copies[-1].start()
    return copies


def scale_kernel(counts_in, router_in, rows_in, gate_in, up_in, *refs):
    state, fetched, hidden = refs[:3], refs[3:6], refs[6]
    outs, scratch = refs[7:-8], refs[-8:]
    counts, router, rows, gate, up, cut, sems, fetch_sems = scratch
    copies = [
        pltpu.make_async_copy(source, target, sems.at[n])
        for n, (source, target) in enumerate(
            [
                (gate_in, gate),
                (up_in, up),
                (counts_in, counts),
                (router_in, router),
                (rows_in, rows),
            ]
        )
    ]
    for copy in copies:
        copy.start()
    fetches = fetch(state, fetched, 0, fetch_sems)
    flight, slots, width = rows.shape[1:]
    pieces = cut.shape[0]
    piece = width // pieces
    ways = hidden.shape[0]
    me, _, own = seat_of(ways)
    copies[0].wait()
    copies[1].wait()
    g = gate[0].astype(f32)
    value = (g * jax.nn.sigmoid(g) * up[0].astype(f32)).astype(bf16)
    for f in range(flight):
        for v in range(ways):
            at = (f * ways + v) * slots
            hidden[v, f] = value[at : at + slots]
    for copy in copies[2:]:
        copy.wait()
    diagonal = lax.broadcasted_iota(jnp.int32, (slots, slots), 0) == lax.broadcasted_iota(
        jnp.int32, (slots, slots), 1
    )
    row = lax.broadcasted_iota(jnp.int32, (slots, 1), 0)
    for f in range(flight):
        weight = jnp.sum(
            jnp.where(diagonal, jnp.broadcast_to(router[0, f : f + 1, :], (slots, slots)), 0.0),
            axis=1,
            keepdims=True,
        )
        live = row < counts[0, f]
        scaled = jnp.where(live, weight * rows[0, f].astype(f32), 0.0).astype(bf16)
        for i in range(pieces):
            cut[i, f] = scaled[:, i * piece : (i + 1) * piece]
    for n, out in enumerate(outs):
        out[...] = cut[me ^ (n % pieces), own ^ (n // pieces)]
    for copy in fetches:
        copy.wait()


def fetch_kernel(start, after, *refs):
    del after
    for copy in fetch(refs[:3], refs[3:6], start, refs[6]):
        copy.wait()


def pack_kernel(spans, *refs):
    blocks, outs = refs[: -len(spans)], refs[-len(spans) :]
    for (start, stop), out in zip(spans, outs):
        for n, block in enumerate(blocks[::-1]):
            out[n] = block[:, start:stop]


def order_kernel(*refs):
    hiddens, right = refs[:-1], refs[-1]
    ways, flight = right.shape[:2]
    _, lane, own = seat_of(ways)
    for dj, hidden in enumerate(hiddens):
        for d in range(ways):
            for dg in range(flight):
                right[d, dg, dj] = hidden[lane ^ d, own ^ dg]


def update_kernel(start, stop, *refs):
    refs = list(refs)
    rows = refs[:-9]
    right, master, first, second, fresh, new_master, new_first, new_second, gradient = refs[-9:]
    hidden = right[...].reshape(-1, right.shape[-1])
    left = tall([block[...].reshape(-1, stop - start) for block in rows])
    gradient[...] = lax.dot_general(
        left, hidden, (((0,), (0,)), ((), ())), preferred_element_type=f32
    )
    for low in range(start, stop, 128):
        end = min(low + 128, stop)
        there = pl.ds(low - start, end - low)
        grad = gradient[there]
        old = master[there]
        moment_a = beta_one * first[there] + (1.0 - beta_one) * grad
        moment_b = beta_two * second[there] + (1.0 - beta_two) * grad * grad
        step_size = (moment_a * (1.0 / (1.0 - beta_one**5))) / (
            jnp.sqrt(moment_b * (1.0 / (1.0 - beta_two**5))) + epsilon
        )
        updated = old - learning_rate * (step_size + decay_rate * old)
        fresh[there] = updated.astype(bf16)
        new_master[there] = updated
        new_first[there] = moment_a
        new_second[there] = moment_b


def partial_kernel(spans, kept, *refs):
    refs = list(refs)
    chunks = len(spans)
    keep, send, own_fresh, held = refs[-4:]
    ways = held.shape[0]
    rows, fresh, master = take(refs, ways * chunks), take(refs, chunks), take(refs, chunks)
    flight = held.shape[1]
    _, lane, own = seat_of(ways)
    left = wide(
        [
            tall([block[...].reshape(-1, stop - start) for block in rows[c * ways : (c + 1) * ways]])
            for c, (start, stop) in enumerate(spans)
        ]
    )
    current = tall([block[...].astype(bf16) for block in master])
    share = jnp.dot(left, current, preferred_element_type=f32)
    held[...] = share.reshape(held.shape)
    for out, chosen in ((keep, kept[0]), (send, kept[1])):
        for n, dj in enumerate(chosen):
            for d in range(ways):
                for dg in range(flight):
                    out[n, lane ^ d, own ^ dg] = held[d, dg, dj].astype(out.dtype)
    for c, (start, stop) in enumerate(spans):
        own_fresh[start:stop] = fresh[c][...]


def halve_kernel(kept, held, arrived, keep, send):
    for out, chosen in ((keep, kept[0]), (send, kept[1])):
        for n, m in enumerate(chosen):
            out[n] = (held[m] + arrived[m].astype(f32)).astype(out.dtype)


def store_kernel(spans, *refs):
    refs = list(refs)
    news = take(refs, 3 * len(spans))
    outs = take(refs, 3)
    (sems,) = refs
    copies = []
    for c, (start, stop) in enumerate(spans):
        for n in range(3):
            copy = pltpu.make_async_copy(
                news[3 * c + n], outs[n].at[pl.ds(start, stop - start)], sems.at[c, n]
            )
            copy.start()
            copies.append(copy)
    for copy in copies:
        copy.wait()


def gate_kernel(gate, up, held, arrived, d_gate, d_up):
    ways, flight, slots = held.shape[1:4]
    for f in range(flight):
        for v in range(ways):
            at = pl.ds((f * ways + v) * slots, slots)
            grad = held[0, v, f] + arrived[0, v, f].astype(f32)
            g = gate[0, at].astype(f32)
            u = up[0, at].astype(f32)
            sig = jax.nn.sigmoid(g)
            d_gate[0, at] = (grad * u * sig * (1.0 + g * (1.0 - sig))).astype(bf16)
            d_up[0, at] = (grad * (g * sig)).astype(bf16)


def join_kernel(high, entries, *refs):
    out, sems = refs[-2], refs[-1]
    me = lax.axis_index("dp")
    copies = []
    for n, (d, start, stop) in enumerate(entries):
        at = pl.multiple_of((me ^ d) * high + start, 16)
        copy = pltpu.make_async_copy(refs[n], out.at[pl.ds(at, stop - start)], sems.at[n])
        copy.start()
        copies.append(copy)
    for copy in copies:
        copy.wait()


def whole(memory=pltpu.VMEM):
    return pl.BlockSpec(memory_space=memory)


def shape(dims, kind):
    return jax.ShapeDtypeStruct(dims, kind)


def pinned(x):
    return pltpu.with_memory_space_constraint(x, pltpu.HBM)


def local(
    grad_rows,
    router_weight,
    send_counts,
    gate_stash,
    up_stash,
    master_weight,
    first_moment,
    second_moment,
):
    _, flight, slots, width = grad_rows.shape
    pieces = lax.axis_size("dp")
    sources = lax.axis_size("expert")
    ways = sources // flight
    high, across = master_weight.shape
    hbm = whole(pltpu.HBM)
    count = pieces * flight * slots

    def over_dp(x, d):
        return lax.ppermute(x, "dp", [(i, i ^ d) for i in range(pieces)])

    tiles = -(-high // LANES)
    middle = (tiles + 1) // 2 * LANES
    spans = [(0, middle), (middle, high)] if middle < high else [(0, high)]
    state = [pinned(master_weight), pinned(first_moment), pinned(second_moment)]
    offsets = [(dj, dg) for dg in range(flight) for dj in range(pieces)]
    results = pl.pallas_call(
        scale_kernel,
        out_shape=[shape((spans[0][1], across), f32)] * 3
        + [shape((ways, flight, slots, across), bf16)]
        + [shape((slots, high), bf16)] * len(offsets),
        in_specs=[hbm] * 8,
        out_specs=[whole()] * (4 + len(offsets)),
        scratch_shapes=[
            pltpu.SMEM(send_counts.shape, jnp.int32),
            pltpu.VMEM(router_weight.shape, f32),
            pltpu.VMEM(grad_rows.shape, bf16),
            pltpu.VMEM(gate_stash.shape, bf16),
            pltpu.VMEM(up_stash.shape, bf16),
            pltpu.VMEM((pieces, flight, slots, high), bf16),
            pltpu.SemaphoreType.DMA((5,)),
            pltpu.SemaphoreType.DMA((3,)),
        ],
        compiler_params=params(),
        name="scale",
    )(
        pinned(send_counts),
        pinned(router_weight),
        pinned(grad_rows),
        pinned(gate_stash),
        pinned(up_stash),
        *state,
    )
    fetched, hidden, blocks = results[:3], results[3], list(results[4:])
    for n, (dj, dg) in reversed(list(enumerate(offsets))):
        if n:
            pairs = [
                (i * sources + k, (i ^ dj) * sources + (k ^ (dg * ways)))
                for i in range(pieces)
                for k in range(sources)
            ]
            blocks[n] = lax.ppermute(blocks[n], ("dp", "expert"), pairs)
    mine = pl.pallas_call(
        functools.partial(pack_kernel, spans),
        out_shape=[shape((len(offsets), slots, stop - start), bf16) for start, stop in spans],
        in_specs=[whole()] * len(offsets),
        out_specs=[whole()] * len(spans),
        compiler_params=params(),
        name="pack",
    )(*blocks[::-1])
    mine, hidden = lax.optimization_barrier((mine, hidden))
    top = pieces // 2

    def spread(entries, first):
        step = first
        while step:
            entries = entries + [(d ^ step, *span, over_dp(x, step)) for d, *span, x in entries]
            step //= 2
        return entries

    hiddens = [entry[1] for entry in sorted(spread([(0, hidden)], top), key=lambda e: e[0])]
    right = pl.pallas_call(
        order_kernel,
        out_shape=shape((ways, flight, pieces, slots, across), bf16),
        in_specs=[whole()] * pieces,
        out_specs=whole(),
        compiler_params=params(),
        name="order",
    )(*hiddens)
    rows = []
    for piece in mine:
        rows.append(
            [piece]
            + [
                lax.ppermute(piece, "expert", [(k, k ^ d) for k in range(sources)])
                for d in range(1, ways)
            ]
        )

    fresh, news, masters = [], [], []
    for c, (start, stop) in enumerate(spans):
        if c:
            fetched = pl.pallas_call(
                functools.partial(fetch_kernel, start),
                out_shape=[shape((stop - start, across), f32)] * 3,
                in_specs=[whole(pl.ANY)] + [hbm] * 3,
                out_specs=[whole()] * 3,
                scratch_shapes=[pltpu.SemaphoreType.DMA((3,))],
                compiler_params=params(),
                name="fetch",
            )(fresh[-1], *state)
        masters.append(fetched[0])
        out = pl.pallas_call(
            functools.partial(update_kernel, start, stop),
            out_shape=[shape((stop - start, across), bf16)]
            + [shape((stop - start, across), f32)] * 3,
            in_specs=[whole()] * (ways + 4),
            out_specs=[whole()] * 4,
            scratch_shapes=[pltpu.VMEM((stop - start, across), f32)],
            compiler_params=params(),
            cost_estimate=cost(2 * ways * count * (stop - start) * across, high * across * 26),
            name="update",
        )(*rows[c], right, *fetched)
        fresh.append(out[0])
        news += out[1:]
    crossed = [over_dp(piece, top) for piece in fresh]

    part = (ways, flight, slots, across)
    bit = 1
    kept = [[d for d in range(pieces) if not d & bit], [d for d in range(pieces) if d & bit]]
    keep, send, own_fresh = pl.pallas_call(
        functools.partial(partial_kernel, spans, kept),
        out_shape=[
            shape((pieces // 2, *part), f32),
            shape((pieces // 2, *part), bf16),
            shape((high, across), bf16),
        ],
        in_specs=[whole()] * ((ways + 2) * len(spans)),
        out_specs=[whole()] * 3,
        scratch_shapes=[pltpu.VMEM((ways, flight, pieces, slots, across), f32)],
        compiler_params=params(),
        cost_estimate=cost(2 * ways * count * high * across, high * across * 12),
        name="partial",
    )(*[block for chunk in rows for block in chunk], *fresh, *masters)
    arrived = over_dp(send, bit)
    while bit < top:
        bit *= 2
        left = kept[0]
        kept = [[d for d in left if not d & bit], [d for d in left if d & bit]]
        chosen = [[left.index(d) for d in half] for half in kept]
        keep, send = pl.pallas_call(
            functools.partial(halve_kernel, chosen),
            out_shape=[
                shape((len(kept[0]), *part), f32),
                shape((len(kept[1]), *part), bf16),
            ],
            in_specs=[whole()] * 2,
            out_specs=[whole()] * 2,
            compiler_params=params(),
            name="halve",
        )(keep, arrived)
        arrived = over_dp(send, bit)
    if len(spans) > 1:
        crossed[0], keep = lax.optimization_barrier((crossed[0], keep))
    d_gate, d_up = pl.pallas_call(
        gate_kernel,
        out_shape=[shape(gate_stash.shape, bf16)] * 2,
        in_specs=[whole()] * 4,
        out_specs=[whole()] * 2,
        compiler_params=params(),
        name="gates",
    )(gate_stash, up_stash, keep, arrived)

    states = pl.pallas_call(
        functools.partial(store_kernel, spans),
        out_shape=[shape((high, across), f32)] * 3,
        in_specs=[whole()] * len(news),
        out_specs=[hbm] * 3,
        scratch_shapes=[pltpu.SemaphoreType.DMA((len(spans), 3))],
        compiler_params=params(),
        cost_estimate=cost(0, high * across * 24),
        name="store",
    )(*news)

    def join(entries, before):
        return pl.pallas_call(
            functools.partial(join_kernel, high, [entry[:3] for entry in entries]),
            out_shape=shape((pieces * high, across), bf16),
            in_specs=[whole(pl.ANY)] * len(entries) + [hbm] * len(before),
            out_specs=hbm,
            input_output_aliases={len(entries): 0} if before else {},
            scratch_shapes=[pltpu.SemaphoreType.DMA((len(entries),))],
            compiler_params=params(),
            name="join",
        )(*[entry[3] for entry in entries], *before)

    near, *far = spread([(0, 0, high, own_fresh)], top // 2)
    early, late = [near], far
    for (start, stop), piece in zip(spans[:-1], crossed[:-1]):
        near, *far = spread([(top, start, stop, piece)], top // 2)
        early.append(near)
        late += far
    joined = join(early, [])
    crossed[-1], joined, states, arrived = lax.optimization_barrier(
        (crossed[-1], joined, states, arrived)
    )
    joined = join(late + spread([(top, *spans[-1], crossed[-1])], top // 2), [joined])
    return (d_gate, d_up, *states, joined)


def solution(mesh):
    placed = (
        P("dp", "expert", None, None),
        P("dp", "expert", None),
        P("dp", "expert"),
        P("dp", None, "expert"),
        P("dp", None, "expert"),
        P("dp", "expert"),
        P("dp", "expert"),
        P("dp", "expert"),
    )
    return jax.shard_map(
        local,
        mesh=mesh,
        in_specs=placed,
        out_specs=(
            P("dp", None, "expert"),
            P("dp", None, "expert"),
            P("dp", "expert"),
            P("dp", "expert"),
            P("dp", "expert"),
            P(None, "expert"),
        ),
        check_vma=False,
    )
```

```python
import functools

import jax
import jax.numpy as jnp
from jax import lax
from jax.experimental import pallas as pl
from jax.experimental.pallas import tpu as pltpu
from jax.sharding import PartitionSpec as P

learning_rate = 0.01
beta_one = 0.9
beta_two = 0.95
decay_rate = 0.1
epsilon = 1e-08

bf16 = jnp.bfloat16
f32 = jnp.float32
VMEM_LIMIT = 40 * 1024 * 1024
LANES = 128


def params():
    return pltpu.CompilerParams(vmem_limit_bytes=VMEM_LIMIT)


def cost(flops, nbytes):
    return pl.CostEstimate(flops=flops, bytes_accessed=nbytes, transcendentals=0)


def take(refs, count):
    taken = refs[:count]
    del refs[:count]
    return taken


def wide(tiles):
    return tiles[0] if len(tiles) == 1 else jnp.concatenate(tiles, axis=1)


def tall(blocks):
    return blocks[0] if len(blocks) == 1 else jnp.concatenate(blocks, axis=0)


def seat_of(ways):
    seat = lax.axis_index("expert")
    return lax.axis_index("dp"), lax.rem(seat, ways), lax.div(seat, ways)


def fetch(state, targets, start, sems):
    copies = []
    for n in range(3):
        rows = pl.ds(start, targets[n].shape[0])
        copies.append(pltpu.make_async_copy(state[n].at[rows], targets[n], sems.at[n]))
        copies[-1].start()
    return copies


def scale_kernel(counts_in, router_in, rows_in, gate_in, up_in, *refs):
    state, fetched, hidden = refs[:3], refs[3:6], refs[6]
    outs, scratch = refs[7:-8], refs[-8:]
    counts, router, rows, gate, up, cut, sems, fetch_sems = scratch
    copies = [
        pltpu.make_async_copy(source, target, sems.at[n])
        for n, (source, target) in enumerate(
            [
                (gate_in, gate),
                (up_in, up),
                (counts_in, counts),
                (router_in, router),
                (rows_in, rows),
            ]
        )
    ]
    for copy in copies:
        copy.start()
    fetches = fetch(state, fetched, 0, fetch_sems)
    flight, slots, width = rows.shape[1:]
    pieces = cut.shape[0]
    piece = width // pieces
    ways = hidden.shape[0]
    me, _, own = seat_of(ways)
    copies[0].wait()
    copies[1].wait()
    g = gate[0].astype(f32)
    value = (g * jax.nn.sigmoid(g) * up[0].astype(f32)).astype(bf16)
    for f in range(flight):
        for v in range(ways):
            at = (f * ways + v) * slots
            hidden[v, f] = value[at : at + slots]
    for copy in copies[2:]:
        copy.wait()
    diagonal = lax.broadcasted_iota(jnp.int32, (slots, slots), 0) == lax.broadcasted_iota(
        jnp.int32, (slots, slots), 1
    )
    row = lax.broadcasted_iota(jnp.int32, (slots, 1), 0)
    for f in range(flight):
        weight = jnp.sum(
            jnp.where(diagonal, jnp.broadcast_to(router[0, f : f + 1, :], (slots, slots)), 0.0),
            axis=1,
            keepdims=True,
        )
        live = row < counts[0, f]
        scaled = jnp.where(live, weight * rows[0, f].astype(f32), 0.0).astype(bf16)
        for i in range(pieces):
            cut[i, f] = scaled[:, i * piece : (i + 1) * piece]
    for n, out in enumerate(outs):
        out[...] = cut[me ^ (n % pieces), own ^ (n // pieces)]
    for copy in fetches:
        copy.wait()


def fetch_kernel(start, after, *refs):
    del after
    for copy in fetch(refs[:3], refs[3:6], start, refs[6]):
        copy.wait()


def pack_kernel(spans, order, *refs):
    blocks, outs = refs[: -len(spans)], refs[-len(spans) :]
    for (start, stop), out in zip(spans, outs):
        for n, block in zip(order, blocks):
            out[n] = block[:, start:stop]


def order_kernel(*refs):
    hiddens, right = refs[:-1], refs[-1]
    ways, flight = right.shape[:2]
    _, lane, own = seat_of(ways)
    for dj, hidden in enumerate(hiddens):
        for d in range(ways):
            for dg in range(flight):
                right[d, dg, dj] = hidden[lane ^ d, own ^ dg]


def update_kernel(start, stop, *refs):
    refs = list(refs)
    rows = refs[:-9]
    right, master, first, second, fresh, new_master, new_first, new_second, gradient = refs[-9:]
    hidden = right[...].reshape(-1, right.shape[-1])
    left = tall([block[...].reshape(-1, stop - start) for block in rows])
    gradient[...] = lax.dot_general(
        left, hidden, (((0,), (0,)), ((), ())), preferred_element_type=f32
    )
    for low in range(start, stop, 128):
        end = min(low + 128, stop)
        there = pl.ds(low - start, end - low)
        grad = gradient[there]
        old = master[there]
        moment_a = beta_one * first[there] + (1.0 - beta_one) * grad
        moment_b = beta_two * second[there] + (1.0 - beta_two) * grad * grad
        step_size = (moment_a * (1.0 / (1.0 - beta_one**5))) / (
            jnp.sqrt(moment_b * (1.0 / (1.0 - beta_two**5))) + epsilon
        )
        updated = old - learning_rate * (step_size + decay_rate * old)
        fresh[there] = updated.astype(bf16)
        new_master[there] = updated
        new_first[there] = moment_a
        new_second[there] = moment_b


def partial_kernel(spans, kept, *refs):
    refs = list(refs)
    chunks = len(spans)
    keep, send, own_fresh, held = refs[-4:]
    ways = held.shape[0]
    rows, fresh, master = take(refs, ways * chunks), take(refs, chunks), take(refs, chunks)
    flight = held.shape[1]
    _, lane, own = seat_of(ways)
    left = wide(
        [
            tall([block[...].reshape(-1, stop - start) for block in rows[c * ways : (c + 1) * ways]])
            for c, (start, stop) in enumerate(spans)
        ]
    )
    current = tall([block[...].astype(bf16) for block in master])
    share = jnp.dot(left, current, preferred_element_type=f32)
    held[...] = share.reshape(held.shape)
    for out, chosen in ((keep, kept[0]), (send, kept[1])):
        for n, dj in enumerate(chosen):
            for d in range(ways):
                for dg in range(flight):
                    out[n, lane ^ d, own ^ dg] = held[d, dg, dj].astype(out.dtype)
    for c, (start, stop) in enumerate(spans):
        own_fresh[start:stop] = fresh[c][...]


def halve_kernel(kept, held, arrived, keep, send):
    for out, chosen in ((keep, kept[0]), (send, kept[1])):
        for n, m in enumerate(chosen):
            out[n] = (held[m] + arrived[m].astype(f32)).astype(out.dtype)


def store_kernel(spans, *refs):
    refs = list(refs)
    news = take(refs, 3 * len(spans))
    outs = take(refs, 3)
    (sems,) = refs
    copies = []
    for c, (start, stop) in enumerate(spans):
        for n in range(3):
            copy = pltpu.make_async_copy(
                news[3 * c + n], outs[n].at[pl.ds(start, stop - start)], sems.at[c, n]
            )
            copy.start()
            copies.append(copy)
    for copy in copies:
        copy.wait()


def gate_kernel(gate, up, held, arrived, d_gate, d_up):
    ways, flight, slots = held.shape[1:4]
    for f in range(flight):
        for v in range(ways):
            at = pl.ds((f * ways + v) * slots, slots)
            grad = held[0, v, f] + arrived[0, v, f].astype(f32)
            g = gate[0, at].astype(f32)
            u = up[0, at].astype(f32)
            sig = jax.nn.sigmoid(g)
            d_gate[0, at] = (grad * u * sig * (1.0 + g * (1.0 - sig))).astype(bf16)
            d_up[0, at] = (grad * (g * sig)).astype(bf16)


def join_kernel(high, entries, *refs):
    out, sems = refs[-2], refs[-1]
    me = lax.axis_index("dp")
    copies = []
    for n, (d, start, stop) in enumerate(entries):
        at = pl.multiple_of((me ^ d) * high + start, 16)
        copy = pltpu.make_async_copy(refs[n], out.at[pl.ds(at, stop - start)], sems.at[n])
        copy.start()
        copies.append(copy)
    for copy in copies:
        copy.wait()


def whole(memory=pltpu.VMEM):
    return pl.BlockSpec(memory_space=memory)


def shape(dims, kind):
    return jax.ShapeDtypeStruct(dims, kind)


def pinned(x):
    return pltpu.with_memory_space_constraint(x, pltpu.HBM)


def local(
    grad_rows,
    router_weight,
    send_counts,
    gate_stash,
    up_stash,
    master_weight,
    first_moment,
    second_moment,
):
    _, flight, slots, width = grad_rows.shape
    pieces = lax.axis_size("dp")
    sources = lax.axis_size("expert")
    ways = sources // flight
    high, across = master_weight.shape
    hbm = whole(pltpu.HBM)
    count = pieces * flight * slots

    def over_dp(x, d):
        return lax.ppermute(x, "dp", [(i, i ^ d) for i in range(pieces)])

    tiles = -(-high // LANES)
    middle = (tiles + 1) // 2 * LANES
    spans = [(0, middle), (middle, high)] if middle < high else [(0, high)]
    state = [pinned(master_weight), pinned(first_moment), pinned(second_moment)]
    offsets = [(dj, dg) for dg in range(flight) for dj in range(pieces)]
    results = pl.pallas_call(
        scale_kernel,
        out_shape=[shape((spans[0][1], across), f32)] * 3
        + [shape((ways, flight, slots, across), bf16)]
        + [shape((slots, high), bf16)] * len(offsets),
        in_specs=[hbm] * 8,
        out_specs=[whole()] * (4 + len(offsets)),
        scratch_shapes=[
            pltpu.SMEM(send_counts.shape, jnp.int32),
            pltpu.VMEM(router_weight.shape, f32),
            pltpu.VMEM(grad_rows.shape, bf16),
            pltpu.VMEM(gate_stash.shape, bf16),
            pltpu.VMEM(up_stash.shape, bf16),
            pltpu.VMEM((pieces, flight, slots, high), bf16),
            pltpu.SemaphoreType.DMA((5,)),
            pltpu.SemaphoreType.DMA((3,)),
        ],
        compiler_params=params(),
        name="scale",
    )(
        pinned(send_counts),
        pinned(router_weight),
        pinned(grad_rows),
        pinned(gate_stash),
        pinned(up_stash),
        *state,
    )
    fetched, hidden, blocks = results[:3], results[3], list(results[4:])
    for n, (dj, dg) in reversed(list(enumerate(offsets))):
        if n:
            pairs = [
                (i * sources + k, (i ^ dj) * sources + (k ^ (dg * ways)))
                for i in range(pieces)
                for k in range(sources)
            ]
            blocks[n] = lax.ppermute(blocks[n], ("dp", "expert"), pairs)
    near, far = list(range(1, pieces)), list(range(len(offsets) - 1, pieces - 1, -1))
    order = [far.pop(0)]
    while near or far:
        order += near[:2] + far[:2]
        near, far = near[2:], far[2:]
    order.append(0)
    mine = pl.pallas_call(
        functools.partial(pack_kernel, spans, order),
        out_shape=[shape((len(offsets), slots, stop - start), bf16) for start, stop in spans],
        in_specs=[whole()] * len(offsets),
        out_specs=[whole()] * len(spans),
        compiler_params=params(),
        name="pack",
    )(*[blocks[n] for n in order])
    top = pieces // 2

    def spread(entries, first):
        step = first
        while step:
            entries = entries + [(d ^ step, *span, over_dp(x, step)) for d, *span, x in entries]
            step //= 2
        return entries

    hiddens = [entry[1] for entry in sorted(spread([(0, hidden)], top), key=lambda e: e[0])]
    right = pl.pallas_call(
        order_kernel,
        out_shape=shape((ways, flight, pieces, slots, across), bf16),
        in_specs=[whole()] * pieces,
        out_specs=whole(),
        compiler_params=params(),
        name="order",
    )(*hiddens)
    rows = []
    for piece in mine:
        rows.append(
            [piece]
            + [
                lax.ppermute(piece, "expert", [(k, k ^ d) for k in range(sources)])
                for d in range(1, ways)
            ]
        )

    fresh, news, masters = [], [], []
    for c, (start, stop) in enumerate(spans):
        if c:
            fetched = pl.pallas_call(
                functools.partial(fetch_kernel, start),
                out_shape=[shape((stop - start, across), f32)] * 3,
                in_specs=[whole(pl.ANY)] + [hbm] * 3,
                out_specs=[whole()] * 3,
                scratch_shapes=[pltpu.SemaphoreType.DMA((3,))],
                compiler_params=params(),
                name="fetch",
            )(fresh[-1], *state)
        masters.append(fetched[0])
        out = pl.pallas_call(
            functools.partial(update_kernel, start, stop),
            out_shape=[shape((stop - start, across), bf16)]
            + [shape((stop - start, across), f32)] * 3,
            in_specs=[whole()] * (ways + 4),
            out_specs=[whole()] * 4,
            scratch_shapes=[pltpu.VMEM((stop - start, across), f32)],
            compiler_params=params(),
            cost_estimate=cost(2 * ways * count * (stop - start) * across, high * across * 26),
            name="update",
        )(*rows[c], right, *fetched)
        fresh.append(out[0])
        news += out[1:]
    crossed = [over_dp(piece, top) for piece in fresh]

    part = (ways, flight, slots, across)
    bit = 1
    kept = [[d for d in range(pieces) if not d & bit], [d for d in range(pieces) if d & bit]]
    keep, send, own_fresh = pl.pallas_call(
        functools.partial(partial_kernel, spans, kept),
        out_shape=[
            shape((pieces // 2, *part), f32),
            shape((pieces // 2, *part), bf16),
            shape((high, across), bf16),
        ],
        in_specs=[whole()] * ((ways + 2) * len(spans)),
        out_specs=[whole()] * 3,
        scratch_shapes=[pltpu.VMEM((ways, flight, pieces, slots, across), f32)],
        compiler_params=params(),
        cost_estimate=cost(2 * ways * count * high * across, high * across * 12),
        name="partial",
    )(*[block for chunk in rows for block in chunk], *fresh, *masters)
    arrived = over_dp(send, bit)
    while bit < top:
        bit *= 2
        left = kept[0]
        kept = [[d for d in left if not d & bit], [d for d in left if d & bit]]
        chosen = [[left.index(d) for d in half] for half in kept]
        keep, send = pl.pallas_call(
            functools.partial(halve_kernel, chosen),
            out_shape=[
                shape((len(kept[0]), *part), f32),
                shape((len(kept[1]), *part), bf16),
            ],
            in_specs=[whole()] * 2,
            out_specs=[whole()] * 2,
            compiler_params=params(),
            name="halve",
        )(keep, arrived)
        arrived = over_dp(send, bit)
    if len(spans) > 1:
        crossed[0], keep = lax.optimization_barrier((crossed[0], keep))
    d_gate, d_up = pl.pallas_call(
        gate_kernel,
        out_shape=[shape(gate_stash.shape, bf16)] * 2,
        in_specs=[whole()] * 4,
        out_specs=[whole()] * 2,
        compiler_params=params(),
        name="gates",
    )(gate_stash, up_stash, keep, arrived)

    states = pl.pallas_call(
        functools.partial(store_kernel, spans),
        out_shape=[shape((high, across), f32)] * 3,
        in_specs=[whole()] * len(news),
        out_specs=[hbm] * 3,
        scratch_shapes=[pltpu.SemaphoreType.DMA((len(spans), 3))],
        compiler_params=params(),
        cost_estimate=cost(0, high * across * 24),
        name="store",
    )(*news)

    def join(entries, before):
        return pl.pallas_call(
            functools.partial(join_kernel, high, [entry[:3] for entry in entries]),
            out_shape=shape((pieces * high, across), bf16),
            in_specs=[whole(pl.ANY)] * len(entries) + [hbm] * len(before),
            out_specs=hbm,
            input_output_aliases={len(entries): 0} if before else {},
            scratch_shapes=[pltpu.SemaphoreType.DMA((len(entries),))],
            compiler_params=params(),
            name="join",
        )(*[entry[3] for entry in entries], *before)

    near, *far = spread([(0, 0, high, own_fresh)], top // 2)
    early, late = [near], far
    for (start, stop), piece in zip(spans[:-1], crossed[:-1]):
        near, *far = spread([(top, start, stop, piece)], top // 2)
        early.append(near)
        late += far
    joined = join(early, [])
    crossed[-1], joined, states, arrived = lax.optimization_barrier(
        (crossed[-1], joined, states, arrived)
    )
    joined = join(late + spread([(top, *spans[-1], crossed[-1])], top // 2), [joined])
    return (d_gate, d_up, *states, joined)


def solution(mesh):
    placed = (
        P("dp", "expert", None, None),
        P("dp", "expert", None),
        P("dp", "expert"),
        P("dp", None, "expert"),
        P("dp", None, "expert"),
        P("dp", "expert"),
        P("dp", "expert"),
        P("dp", "expert"),
    )
    return jax.shard_map(
        local,
        mesh=mesh,
        in_specs=placed,
        out_specs=(
            P("dp", None, "expert"),
            P("dp", None, "expert"),
            P("dp", "expert"),
            P("dp", "expert"),
            P("dp", "expert"),
            P(None, "expert"),
        ),
        check_vma=False,
    )
```

```python
import functools

import jax
import jax.numpy as jnp
from jax import lax
from jax.experimental import pallas as pl
from jax.experimental.pallas import tpu as pltpu
from jax.sharding import PartitionSpec as P

learning_rate = 0.01
beta_one = 0.9
beta_two = 0.95
decay_rate = 0.1
epsilon = 1e-08

bf16 = jnp.bfloat16
f32 = jnp.float32
VMEM_LIMIT = 40 * 1024 * 1024
LANES = 128


def params():
    return pltpu.CompilerParams(vmem_limit_bytes=VMEM_LIMIT)


def cost(flops, nbytes):
    return pl.CostEstimate(flops=flops, bytes_accessed=nbytes, transcendentals=0)


def take(refs, count):
    taken = refs[:count]
    del refs[:count]
    return taken


def wide(tiles):
    return tiles[0] if len(tiles) == 1 else jnp.concatenate(tiles, axis=1)


def tall(blocks):
    return blocks[0] if len(blocks) == 1 else jnp.concatenate(blocks, axis=0)


def seat_of(ways):
    seat = lax.axis_index("expert")
    return lax.axis_index("dp"), lax.rem(seat, ways), lax.div(seat, ways)


def scale_kernel(counts_in, router_in, rows_in, gate_in, up_in, *refs):
    hidden, outs = refs[0], refs[1:-7]
    counts, router, rows, gate, up, cut, sems = refs[-7:]
    copies = [
        pltpu.make_async_copy(source, target, sems.at[n])
        for n, (source, target) in enumerate(
            [
                (gate_in, gate),
                (up_in, up),
                (counts_in, counts),
                (router_in, router),
                (rows_in, rows),
            ]
        )
    ]
    for copy in copies:
        copy.start()
    flight, slots, width = rows.shape[1:]
    pieces = cut.shape[0]
    piece = width // pieces
    ways = hidden.shape[0]
    me, _, own = seat_of(ways)
    copies[0].wait()
    copies[1].wait()
    g = gate[0].astype(f32)
    value = (g * jax.nn.sigmoid(g) * up[0].astype(f32)).astype(bf16)
    for f in range(flight):
        for v in range(ways):
            at = (f * ways + v) * slots
            hidden[v, f] = value[at : at + slots]
    for copy in copies[2:]:
        copy.wait()
    diagonal = lax.broadcasted_iota(jnp.int32, (slots, slots), 0) == lax.broadcasted_iota(
        jnp.int32, (slots, slots), 1
    )
    row = lax.broadcasted_iota(jnp.int32, (slots, 1), 0)
    for f in range(flight):
        weight = jnp.sum(
            jnp.where(diagonal, jnp.broadcast_to(router[0, f : f + 1, :], (slots, slots)), 0.0),
            axis=1,
            keepdims=True,
        )
        live = row < counts[0, f]
        scaled = jnp.where(live, weight * rows[0, f].astype(f32), 0.0).astype(bf16)
        for i in range(pieces):
            cut[i, f] = scaled[:, i * piece : (i + 1) * piece]
    for dj in range(pieces):
        outs[dj][...] = cut[me ^ dj, own]
        for dg in range(1, flight):
            outs[pieces + dg - 1][dj] = cut[me ^ dj, own ^ dg]


def fetch_kernel(after, *refs):
    del after
    sems = refs[6]
    copies = [pltpu.make_async_copy(refs[n], refs[3 + n], sems.at[n]) for n in range(3)]
    for copy in copies:
        copy.start()
    for copy in copies:
        copy.wait()


def pack_kernel(spans, *refs):
    blocks, outs = refs[: -len(spans)], refs[-len(spans) :]
    for (start, stop), out in zip(spans, outs):
        for n, block in enumerate(blocks):
            out[n] = block[:, start:stop]


def order_kernel(*refs):
    hiddens, right = refs[:-1], refs[-1]
    ways, flight = right.shape[:2]
    _, lane, own = seat_of(ways)
    for dj, hidden in enumerate(hiddens):
        for d in range(ways):
            for dg in range(flight):
                right[d, dg, dj] = hidden[lane ^ d, own ^ dg]


def update_kernel(start, stop, *refs):
    refs = list(refs)
    rows = refs[:-9]
    right, master, first, second, fresh, new_master, new_first, new_second, gradient = refs[-9:]
    hidden = right[...].reshape(-1, right.shape[-1])
    left = tall([block[...].reshape(-1, stop - start) for block in rows])
    gradient[...] = lax.dot_general(
        left, hidden, (((0,), (0,)), ((), ())), preferred_element_type=f32
    )
    for low in range(start, stop, 128):
        end = min(low + 128, stop)
        here = pl.ds(low, end - low)
        there = pl.ds(low - start, end - low)
        grad = gradient[there]
        old = master[here]
        moment_a = beta_one * first[here] + (1.0 - beta_one) * grad
        moment_b = beta_two * second[here] + (1.0 - beta_two) * grad * grad
        step_size = (moment_a * (1.0 / (1.0 - beta_one**5))) / (
            jnp.sqrt(moment_b * (1.0 / (1.0 - beta_two**5))) + epsilon
        )
        updated = old - learning_rate * (step_size + decay_rate * old)
        fresh[there] = updated.astype(bf16)
        new_master[there] = updated
        new_first[there] = moment_a
        new_second[there] = moment_b


def partial_kernel(spans, kept, *refs):
    refs = list(refs)
    chunks = len(spans)
    keep, send, own_fresh, held = refs[-4:]
    ways = held.shape[0]
    rows, fresh, (master,) = take(refs, ways * chunks), take(refs, chunks), take(refs, 1)
    flight = held.shape[1]
    _, lane, own = seat_of(ways)
    left = wide(
        [
            tall([block[...].reshape(-1, stop - start) for block in rows[c * ways : (c + 1) * ways]])
            for c, (start, stop) in enumerate(spans)
        ]
    )
    share = jnp.dot(left, master[...].astype(bf16), preferred_element_type=f32)
    held[...] = share.reshape(held.shape)
    for out, chosen in ((keep, kept[0]), (send, kept[1])):
        for n, dj in enumerate(chosen):
            for d in range(ways):
                for dg in range(flight):
                    out[n, lane ^ d, own ^ dg] = held[d, dg, dj].astype(out.dtype)
    for c, (start, stop) in enumerate(spans):
        own_fresh[start:stop] = fresh[c][...]


def halve_kernel(kept, held, arrived, keep, send):
    for out, chosen in ((keep, kept[0]), (send, kept[1])):
        for n, m in enumerate(chosen):
            out[n] = (held[m] + arrived[m].astype(f32)).astype(out.dtype)


def store_kernel(spans, *refs):
    refs = list(refs)
    news = take(refs, 3 * len(spans))
    outs = take(refs, 3)
    (sems,) = refs
    copies = []
    for c, (start, stop) in enumerate(spans):
        for n in range(3):
            copy = pltpu.make_async_copy(
                news[3 * c + n], outs[n].at[pl.ds(start, stop - start)], sems.at[c, n]
            )
            copy.start()
            copies.append(copy)
    for copy in copies:
        copy.wait()


def gate_kernel(gate, up, held, arrived, d_gate, d_up):
    ways, flight, slots = held.shape[1:4]
    for f in range(flight):
        for v in range(ways):
            at = pl.ds((f * ways + v) * slots, slots)
            grad = held[0, v, f] + arrived[0, v, f].astype(f32)
            g = gate[0, at].astype(f32)
            u = up[0, at].astype(f32)
            sig = jax.nn.sigmoid(g)
            d_gate[0, at] = (grad * u * sig * (1.0 + g * (1.0 - sig))).astype(bf16)
            d_up[0, at] = (grad * (g * sig)).astype(bf16)


def join_kernel(high, entries, *refs):
    out, sems = refs[-2], refs[-1]
    me = lax.axis_index("dp")
    copies = []
    for n, (d, start, stop) in enumerate(entries):
        at = pl.multiple_of((me ^ d) * high + start, 16)
        copy = pltpu.make_async_copy(refs[n], out.at[pl.ds(at, stop - start)], sems.at[n])
        copy.start()
        copies.append(copy)
    for copy in copies:
        copy.wait()


def whole(memory=pltpu.VMEM):
    return pl.BlockSpec(memory_space=memory)


def shape(dims, kind):
    return jax.ShapeDtypeStruct(dims, kind)


def pinned(x):
    return pltpu.with_memory_space_constraint(x, pltpu.HBM)


def local(
    grad_rows,
    router_weight,
    send_counts,
    gate_stash,
    up_stash,
    master_weight,
    first_moment,
    second_moment,
):
    _, flight, slots, width = grad_rows.shape
    pieces = lax.axis_size("dp")
    sources = lax.axis_size("expert")
    ways = sources // flight
    high, across = master_weight.shape
    hbm = whole(pltpu.HBM)
    count = pieces * flight * slots

    def over_dp(x, d):
        return lax.ppermute(x, "dp", [(i, i ^ d) for i in range(pieces)])

    tiles = -(-high // LANES)
    middle = (tiles + 1) // 2 * LANES
    spans = [(0, middle), (middle, high)] if middle < high else [(0, high)]
    hidden, *blocks = pl.pallas_call(
        scale_kernel,
        out_shape=[shape((ways, flight, slots, across), bf16)]
        + [shape((slots, high), bf16)] * pieces
        + [shape((pieces, slots, high), bf16)] * (flight - 1),
        in_specs=[hbm] * 5,
        out_specs=[whole()] * (pieces + flight),
        scratch_shapes=[
            pltpu.SMEM(send_counts.shape, jnp.int32),
            pltpu.VMEM(router_weight.shape, f32),
            pltpu.VMEM(grad_rows.shape, bf16),
            pltpu.VMEM(gate_stash.shape, bf16),
            pltpu.VMEM(up_stash.shape, bf16),
            pltpu.VMEM((pieces, flight, slots, high), bf16),
            pltpu.SemaphoreType.DMA((5,)),
        ],
        compiler_params=params(),
        name="scale",
    )(
        pinned(send_counts),
        pinned(router_weight),
        pinned(grad_rows),
        pinned(gate_stash),
        pinned(up_stash),
    )
    far = [
        lax.ppermute(
            blocks[pieces + dg - 1], "expert", [(k, k ^ (dg * ways)) for k in range(sources)]
        )
        for dg in range(1, flight)
    ]
    blocks = [blocks[0]] + [over_dp(blocks[dj], dj) for dj in range(1, pieces)]
    top = pieces // 2

    def spread(entries, first):
        step = first
        while step:
            entries = entries + [(d ^ step, *span, over_dp(x, step)) for d, *span, x in entries]
            step //= 2
        return entries

    hiddens = [entry[1] for entry in sorted(spread([(0, hidden)], top), key=lambda e: e[0])]
    right = pl.pallas_call(
        order_kernel,
        out_shape=shape((ways, flight, pieces, slots, across), bf16),
        in_specs=[whole()] * pieces,
        out_specs=whole(),
        compiler_params=params(),
        name="order",
    )(*hiddens)
    state = pl.pallas_call(
        fetch_kernel,
        out_shape=[shape((high, across), f32)] * 3,
        in_specs=[whole(pl.ANY)] + [hbm] * 3,
        out_specs=[whole()] * 3,
        scratch_shapes=[pltpu.SemaphoreType.DMA((3,))],
        compiler_params=params(),
        cost_estimate=cost(0, high * across * 24),
        name="fetch",
    )(hidden, pinned(master_weight), pinned(first_moment), pinned(second_moment))
    far, right, state = lax.optimization_barrier((far, right, state))
    for block in far:
        blocks += [block[0]] + [over_dp(block[dj], dj) for dj in range(1, pieces)]
    mine = pl.pallas_call(
        functools.partial(pack_kernel, spans),
        out_shape=[shape((len(blocks), slots, stop - start), bf16) for start, stop in spans],
        in_specs=[whole()] * len(blocks),
        out_specs=[whole()] * len(spans),
        compiler_params=params(),
        name="pack",
    )(*blocks)

    rows = []
    for piece in mine:
        rows.append(
            [piece]
            + [
                lax.ppermute(piece, "expert", [(k, k ^ d) for k in range(sources)])
                for d in range(1, ways)
            ]
        )

    fresh, news = [], []
    for c, (start, stop) in enumerate(spans):
        out = pl.pallas_call(
            functools.partial(update_kernel, start, stop),
            out_shape=[shape((stop - start, across), bf16)]
            + [shape((stop - start, across), f32)] * 3,
            in_specs=[whole()] * (ways + 4),
            out_specs=[whole()] * 4,
            scratch_shapes=[pltpu.VMEM((stop - start, across), f32)],
            compiler_params=params(),
            cost_estimate=cost(2 * ways * count * (stop - start) * across, high * across * 26),
            name="update",
        )(*rows[c], right, *state)
        fresh.append(out[0])
        news += out[1:]
    crossed = [over_dp(piece, top) for piece in fresh]

    part = (ways, flight, slots, across)
    bit = 1
    kept = [[d for d in range(pieces) if not d & bit], [d for d in range(pieces) if d & bit]]
    keep, send, own_fresh = pl.pallas_call(
        functools.partial(partial_kernel, spans, kept),
        out_shape=[
            shape((pieces // 2, *part), f32),
            shape((pieces // 2, *part), bf16),
            shape((high, across), bf16),
        ],
        in_specs=[whole()] * ((ways + 1) * len(spans) + 1),
        out_specs=[whole()] * 3,
        scratch_shapes=[pltpu.VMEM((ways, flight, pieces, slots, across), f32)],
        compiler_params=params(),
        cost_estimate=cost(2 * ways * count * high * across, high * across * 12),
        name="partial",
    )(*[block for chunk in rows for block in chunk], *fresh, state[0])
    arrived = over_dp(send, bit)
    while bit < top:
        bit *= 2
        left = kept[0]
        kept = [[d for d in left if not d & bit], [d for d in left if d & bit]]
        chosen = [[left.index(d) for d in half] for half in kept]
        keep, send = pl.pallas_call(
            functools.partial(halve_kernel, chosen),
            out_shape=[
                shape((len(kept[0]), *part), f32),
                shape((len(kept[1]), *part), bf16),
            ],
            in_specs=[whole()] * 2,
            out_specs=[whole()] * 2,
            compiler_params=params(),
            name="halve",
        )(keep, arrived)
        arrived = over_dp(send, bit)
    if len(spans) > 1:
        crossed[0], keep = lax.optimization_barrier((crossed[0], keep))
    d_gate, d_up = pl.pallas_call(
        gate_kernel,
        out_shape=[shape(gate_stash.shape, bf16)] * 2,
        in_specs=[whole()] * 4,
        out_specs=[whole()] * 2,
        compiler_params=params(),
        name="gates",
    )(gate_stash, up_stash, keep, arrived)

    states = pl.pallas_call(
        functools.partial(store_kernel, spans),
        out_shape=[shape((high, across), f32)] * 3,
        in_specs=[whole()] * len(news),
        out_specs=[hbm] * 3,
        scratch_shapes=[pltpu.SemaphoreType.DMA((len(spans), 3))],
        compiler_params=params(),
        cost_estimate=cost(0, high * across * 24),
        name="store",
    )(*news)

    def join(entries, before):
        return pl.pallas_call(
            functools.partial(join_kernel, high, [entry[:3] for entry in entries]),
            out_shape=shape((pieces * high, across), bf16),
            in_specs=[whole(pl.ANY)] * len(entries) + [hbm] * len(before),
            out_specs=hbm,
            input_output_aliases={len(entries): 0} if before else {},
            scratch_shapes=[pltpu.SemaphoreType.DMA((len(entries),))],
            compiler_params=params(),
            name="join",
        )(*[entry[3] for entry in entries], *before)

    near, *far = spread([(0, 0, high, own_fresh)], top // 2)
    early, late = [near], far
    for (start, stop), piece in zip(spans[:-1], crossed[:-1]):
        near, *far = spread([(top, start, stop, piece)], top // 2)
        early.append(near)
        late += far
    joined = join(early, [])
    crossed[-1], joined, states, arrived = lax.optimization_barrier(
        (crossed[-1], joined, states, arrived)
    )
    joined = join(late + spread([(top, *spans[-1], crossed[-1])], top // 2), [joined])
    return (d_gate, d_up, *states, joined)


def solution(mesh):
    placed = (
        P("dp", "expert", None, None),
        P("dp", "expert", None),
        P("dp", "expert"),
        P("dp", None, "expert"),
        P("dp", None, "expert"),
        P("dp", "expert"),
        P("dp", "expert"),
        P("dp", "expert"),
    )
    return jax.shard_map(
        local,
        mesh=mesh,
        in_specs=placed,
        out_specs=(
            P("dp", None, "expert"),
            P("dp", None, "expert"),
            P("dp", "expert"),
            P("dp", "expert"),
            P("dp", "expert"),
            P(None, "expert"),
        ),
        check_vma=False,
    )
```

```python
import functools

import jax
import jax.numpy as jnp
from jax import lax
from jax.experimental import pallas as pl
from jax.experimental.pallas import tpu as pltpu
from jax.sharding import PartitionSpec as P

learning_rate = 0.01
beta_one = 0.9
beta_two = 0.95
decay_rate = 0.1
epsilon = 1e-08

bf16 = jnp.bfloat16
f32 = jnp.float32
VMEM_LIMIT = 40 * 1024 * 1024
LANES = 128


def params():
    return pltpu.CompilerParams(vmem_limit_bytes=VMEM_LIMIT)


def cost(flops, nbytes):
    return pl.CostEstimate(flops=flops, bytes_accessed=nbytes, transcendentals=0)


def take(refs, count):
    taken = refs[:count]
    del refs[:count]
    return taken


def wide(tiles):
    return tiles[0] if len(tiles) == 1 else jnp.concatenate(tiles, axis=1)


def tall(blocks):
    return blocks[0] if len(blocks) == 1 else jnp.concatenate(blocks, axis=0)


def seat_of(ways):
    seat = lax.axis_index("expert")
    return lax.axis_index("dp"), lax.rem(seat, ways), lax.div(seat, ways)


def fetch(state, targets, start, sems):
    copies = []
    for n in range(3):
        rows = pl.ds(start, targets[n].shape[0])
        copies.append(pltpu.make_async_copy(state[n].at[rows], targets[n], sems.at[n]))
        copies[-1].start()
    return copies


def scale_kernel(counts_in, router_in, rows_in, gate_in, up_in, *refs):
    state, fetched, hidden = refs[:3], refs[3:6], refs[6]
    outs, scratch = refs[7:-8], refs[-8:]
    counts, router, rows, gate, up, cut, sems, fetch_sems = scratch
    copies = [
        pltpu.make_async_copy(source, target, sems.at[n])
        for n, (source, target) in enumerate(
            [
                (gate_in, gate),
                (up_in, up),
                (counts_in, counts),
                (router_in, router),
                (rows_in, rows),
            ]
        )
    ]
    for copy in copies:
        copy.start()
    fetches = fetch(state, fetched, 0, fetch_sems)
    flight, slots, width = rows.shape[1:]
    pieces = cut.shape[0]
    piece = width // pieces
    ways = hidden.shape[0]
    me, _, own = seat_of(ways)
    copies[0].wait()
    copies[1].wait()
    g = gate[0].astype(f32)
    value = (g * jax.nn.sigmoid(g) * up[0].astype(f32)).astype(bf16)
    for f in range(flight):
        for v in range(ways):
            at = (f * ways + v) * slots
            hidden[v, f] = value[at : at + slots]
    for copy in copies[2:]:
        copy.wait()
    diagonal = lax.broadcasted_iota(jnp.int32, (slots, slots), 0) == lax.broadcasted_iota(
        jnp.int32, (slots, slots), 1
    )
    row = lax.broadcasted_iota(jnp.int32, (slots, 1), 0)
    for f in range(flight):
        weight = jnp.sum(
            jnp.where(diagonal, jnp.broadcast_to(router[0, f : f + 1, :], (slots, slots)), 0.0),
            axis=1,
            keepdims=True,
        )
        live = row < counts[0, f]
        scaled = jnp.where(live, weight * rows[0, f].astype(f32), 0.0).astype(bf16)
        for i in range(pieces):
            cut[i, f] = scaled[:, i * piece : (i + 1) * piece]
    for n, out in enumerate(outs):
        for dc in range(2):
            out[dc] = cut[me ^ (n % (pieces // 2) * 2 + dc), own ^ (n // (pieces // 2))]
    for copy in fetches:
        copy.wait()


def fetch_kernel(start, after, *refs):
    del after
    for copy in fetch(refs[:3], refs[3:6], start, refs[6]):
        copy.wait()


def share_kernel(order, *refs):
    for n, block in zip(order, refs):
        refs[-1][n] = block[1]


def pack_kernel(spans, other, *refs):
    blocks, outs = refs[: -len(spans)], refs[-len(spans) :]
    for (start, stop), out in zip(spans, outs):
        for n, block in enumerate(blocks):
            out[2 * n] = block[0, :, start:stop]
            out[2 * n + 1] = other[n, :, start:stop]


def order_kernel(*refs):
    hiddens, right = refs[:-1], refs[-1]
    ways, flight = right.shape[:2]
    _, lane, own = seat_of(ways)
    for dj, hidden in enumerate(hiddens):
        for d in range(ways):
            for dg in range(flight):
                right[d, dg, dj] = hidden[lane ^ d, own ^ dg]


def update_kernel(start, stop, *refs):
    refs = list(refs)
    rows = refs[:-9]
    right, master, first, second, fresh, new_master, new_first, new_second, gradient = refs[-9:]
    hidden = right[...].reshape(-1, right.shape[-1])
    left = tall([block[...].reshape(-1, stop - start) for block in rows])
    gradient[...] = lax.dot_general(
        left, hidden, (((0,), (0,)), ((), ())), preferred_element_type=f32
    )
    for low in range(start, stop, 128):
        end = min(low + 128, stop)
        there = pl.ds(low - start, end - low)
        grad = gradient[there]
        old = master[there]
        moment_a = beta_one * first[there] + (1.0 - beta_one) * grad
        moment_b = beta_two * second[there] + (1.0 - beta_two) * grad * grad
        step_size = (moment_a * (1.0 / (1.0 - beta_one**5))) / (
            jnp.sqrt(moment_b * (1.0 / (1.0 - beta_two**5))) + epsilon
        )
        updated = old - learning_rate * (step_size + decay_rate * old)
        fresh[there] = updated.astype(bf16)
        new_master[there] = updated
        new_first[there] = moment_a
        new_second[there] = moment_b


def partial_kernel(spans, kept, *refs):
    refs = list(refs)
    chunks = len(spans)
    keep, send, own_fresh, held = refs[-4:]
    ways = held.shape[0]
    rows, fresh, master = take(refs, ways * chunks), take(refs, chunks), take(refs, chunks)
    flight = held.shape[1]
    _, lane, own = seat_of(ways)
    left = wide(
        [
            tall([block[...].reshape(-1, stop - start) for block in rows[c * ways : (c + 1) * ways]])
            for c, (start, stop) in enumerate(spans)
        ]
    )
    current = tall([block[...].astype(bf16) for block in master])
    share = jnp.dot(left, current, preferred_element_type=f32)
    held[...] = share.reshape(held.shape)
    for out, chosen in ((keep, kept[0]), (send, kept[1])):
        for n, dj in enumerate(chosen):
            for d in range(ways):
                for dg in range(flight):
                    out[n, lane ^ d, own ^ dg] = held[d, dg, dj].astype(out.dtype)
    for c, (start, stop) in enumerate(spans):
        own_fresh[start:stop] = fresh[c][...]


def halve_kernel(kept, held, arrived, keep, send):
    for out, chosen in ((keep, kept[0]), (send, kept[1])):
        for n, m in enumerate(chosen):
            out[n] = (held[m] + arrived[m].astype(f32)).astype(out.dtype)


def store_kernel(spans, *refs):
    refs = list(refs)
    news = take(refs, 3 * len(spans))
    outs = take(refs, 3)
    (sems,) = refs
    copies = []
    for c, (start, stop) in enumerate(spans):
        for n in range(3):
            copy = pltpu.make_async_copy(
                news[3 * c + n], outs[n].at[pl.ds(start, stop - start)], sems.at[c, n]
            )
            copy.start()
            copies.append(copy)
    for copy in copies:
        copy.wait()


def gate_kernel(gate, up, held, arrived, d_gate, d_up):
    ways, flight, slots = held.shape[1:4]
    for f in range(flight):
        for v in range(ways):
            at = pl.ds((f * ways + v) * slots, slots)
            grad = held[0, v, f] + arrived[0, v, f].astype(f32)
            g = gate[0, at].astype(f32)
            u = up[0, at].astype(f32)
            sig = jax.nn.sigmoid(g)
            d_gate[0, at] = (grad * u * sig * (1.0 + g * (1.0 - sig))).astype(bf16)
            d_up[0, at] = (grad * (g * sig)).astype(bf16)


def join_kernel(high, entries, *refs):
    out, sems = refs[-2], refs[-1]
    me = lax.axis_index("dp")
    copies = []
    for n, (d, start, stop) in enumerate(entries):
        at = pl.multiple_of((me ^ d) * high + start, 16)
        copy = pltpu.make_async_copy(refs[n], out.at[pl.ds(at, stop - start)], sems.at[n])
        copy.start()
        copies.append(copy)
    for copy in copies:
        copy.wait()


def whole(memory=pltpu.VMEM):
    return pl.BlockSpec(memory_space=memory)


def shape(dims, kind):
    return jax.ShapeDtypeStruct(dims, kind)


def pinned(x):
    return pltpu.with_memory_space_constraint(x, pltpu.HBM)


def local(
    grad_rows,
    router_weight,
    send_counts,
    gate_stash,
    up_stash,
    master_weight,
    first_moment,
    second_moment,
):
    _, flight, slots, width = grad_rows.shape
    pieces = lax.axis_size("dp")
    sources = lax.axis_size("expert")
    ways = sources // flight
    high, across = master_weight.shape
    hbm = whole(pltpu.HBM)
    count = pieces * flight * slots

    def over_dp(x, d):
        return lax.ppermute(x, "dp", [(i, i ^ d) for i in range(pieces)])

    tiles = -(-high // LANES)
    middle = (tiles + 1) // 2 * LANES
    spans = [(0, middle), (middle, high)] if middle < high else [(0, high)]
    state = [pinned(master_weight), pinned(first_moment), pinned(second_moment)]
    offsets = [(dj, dg) for dg in range(flight) for dj in range(0, pieces, 2)]
    results = pl.pallas_call(
        scale_kernel,
        out_shape=[shape((spans[0][1], across), f32)] * 3
        + [shape((ways, flight, slots, across), bf16)]
        + [shape((2, slots, high), bf16)] * len(offsets),
        in_specs=[hbm] * 8,
        out_specs=[whole()] * (4 + len(offsets)),
        scratch_shapes=[
            pltpu.SMEM(send_counts.shape, jnp.int32),
            pltpu.VMEM(router_weight.shape, f32),
            pltpu.VMEM(grad_rows.shape, bf16),
            pltpu.VMEM(gate_stash.shape, bf16),
            pltpu.VMEM(up_stash.shape, bf16),
            pltpu.VMEM((pieces, flight, slots, high), bf16),
            pltpu.SemaphoreType.DMA((5,)),
            pltpu.SemaphoreType.DMA((3,)),
        ],
        compiler_params=params(),
        name="scale",
    )(
        pinned(send_counts),
        pinned(router_weight),
        pinned(grad_rows),
        pinned(gate_stash),
        pinned(up_stash),
        *state,
    )
    fetched, hidden, blocks = results[:3], results[3], list(results[4:])
    for n, (dj, dg) in reversed(list(enumerate(offsets))):
        if n:
            pairs = [
                (i * sources + k, (i ^ dj) * sources + (k ^ (dg * ways)))
                for i in range(pieces)
                for k in range(sources)
            ]
            blocks[n] = lax.ppermute(blocks[n], ("dp", "expert"), pairs)
    order = [*range(pieces // 2, len(offsets)), *range(1, pieces // 2), 0]
    other = pl.pallas_call(
        functools.partial(share_kernel, order),
        out_shape=shape((len(offsets), slots, high), bf16),
        in_specs=[whole()] * len(offsets),
        out_specs=whole(),
        compiler_params=params(),
        name="share",
    )(*[blocks[n] for n in order])
    mine = pl.pallas_call(
        functools.partial(pack_kernel, spans),
        out_shape=[shape((2 * len(offsets), slots, stop - start), bf16) for start, stop in spans],
        in_specs=[whole()] * (1 + len(offsets)),
        out_specs=[whole()] * len(spans),
        compiler_params=params(),
        name="pack",
    )(over_dp(other, 1), *blocks)
    top = pieces // 2

    def spread(entries, first):
        step = first
        while step:
            entries = entries + [(d ^ step, *span, over_dp(x, step)) for d, *span, x in entries]
            step //= 2
        return entries

    hiddens = [entry[1] for entry in sorted(spread([(0, hidden)], top), key=lambda e: e[0])]
    right = pl.pallas_call(
        order_kernel,
        out_shape=shape((ways, flight, pieces, slots, across), bf16),
        in_specs=[whole()] * pieces,
        out_specs=whole(),
        compiler_params=params(),
        name="order",
    )(*hiddens)
    rows = []
    for piece in mine:
        rows.append(
            [piece]
            + [
                lax.ppermute(piece, "expert", [(k, k ^ d) for k in range(sources)])
                for d in range(1, ways)
            ]
        )

    fresh, news, masters = [], [], []
    for c, (start, stop) in enumerate(spans):
        if c:
            fetched = pl.pallas_call(
                functools.partial(fetch_kernel, start),
                out_shape=[shape((stop - start, across), f32)] * 3,
                in_specs=[whole(pl.ANY)] + [hbm] * 3,
                out_specs=[whole()] * 3,
                scratch_shapes=[pltpu.SemaphoreType.DMA((3,))],
                compiler_params=params(),
                name="fetch",
            )(fresh[-1], *state)
        masters.append(fetched[0])
        out = pl.pallas_call(
            functools.partial(update_kernel, start, stop),
            out_shape=[shape((stop - start, across), bf16)]
            + [shape((stop - start, across), f32)] * 3,
            in_specs=[whole()] * (ways + 4),
            out_specs=[whole()] * 4,
            scratch_shapes=[pltpu.VMEM((stop - start, across), f32)],
            compiler_params=params(),
            cost_estimate=cost(2 * ways * count * (stop - start) * across, high * across * 26),
            name="update",
        )(*rows[c], right, *fetched)
        fresh.append(out[0])
        news += out[1:]
    crossed = [over_dp(piece, top) for piece in fresh]

    part = (ways, flight, slots, across)
    bit = 1
    kept = [[d for d in range(pieces) if not d & bit], [d for d in range(pieces) if d & bit]]
    keep, send, own_fresh = pl.pallas_call(
        functools.partial(partial_kernel, spans, kept),
        out_shape=[
            shape((pieces // 2, *part), f32),
            shape((pieces // 2, *part), bf16),
            shape((high, across), bf16),
        ],
        in_specs=[whole()] * ((ways + 2) * len(spans)),
        out_specs=[whole()] * 3,
        scratch_shapes=[pltpu.VMEM((ways, flight, pieces, slots, across), f32)],
        compiler_params=params(),
        cost_estimate=cost(2 * ways * count * high * across, high * across * 12),
        name="partial",
    )(*[block for chunk in rows for block in chunk], *fresh, *masters)
    arrived = over_dp(send, bit)
    while bit < top:
        bit *= 2
        left = kept[0]
        kept = [[d for d in left if not d & bit], [d for d in left if d & bit]]
        chosen = [[left.index(d) for d in half] for half in kept]
        keep, send = pl.pallas_call(
            functools.partial(halve_kernel, chosen),
            out_shape=[
                shape((len(kept[0]), *part), f32),
                shape((len(kept[1]), *part), bf16),
            ],
            in_specs=[whole()] * 2,
            out_specs=[whole()] * 2,
            compiler_params=params(),
            name="halve",
        )(keep, arrived)
        arrived = over_dp(send, bit)
    if len(spans) > 1:
        crossed[0], keep = lax.optimization_barrier((crossed[0], keep))
    d_gate, d_up = pl.pallas_call(
        gate_kernel,
        out_shape=[shape(gate_stash.shape, bf16)] * 2,
        in_specs=[whole()] * 4,
        out_specs=[whole()] * 2,
        compiler_params=params(),
        name="gates",
    )(gate_stash, up_stash, keep, arrived)

    states = pl.pallas_call(
        functools.partial(store_kernel, spans),
        out_shape=[shape((high, across), f32)] * 3,
        in_specs=[whole()] * len(news),
        out_specs=[hbm] * 3,
        scratch_shapes=[pltpu.SemaphoreType.DMA((len(spans), 3))],
        compiler_params=params(),
        cost_estimate=cost(0, high * across * 24),
        name="store",
    )(*news)

    def join(entries, before):
        return pl.pallas_call(
            functools.partial(join_kernel, high, [entry[:3] for entry in entries]),
            out_shape=shape((pieces * high, across), bf16),
            in_specs=[whole(pl.ANY)] * len(entries) + [hbm] * len(before),
            out_specs=hbm,
            input_output_aliases={len(entries): 0} if before else {},
            scratch_shapes=[pltpu.SemaphoreType.DMA((len(entries),))],
            compiler_params=params(),
            name="join",
        )(*[entry[3] for entry in entries], *before)

    near, *far = spread([(0, 0, high, own_fresh)], top // 2)
    early, late = [near], far
    for (start, stop), piece in zip(spans[:-1], crossed[:-1]):
        near, *far = spread([(top, start, stop, piece)], top // 2)
        early.append(near)
        late += far
    joined = join(early, [])
    crossed[-1], joined, states, arrived = lax.optimization_barrier(
        (crossed[-1], joined, states, arrived)
    )
    joined = join(late + spread([(top, *spans[-1], crossed[-1])], top // 2), [joined])
    return (d_gate, d_up, *states, joined)


def solution(mesh):
    placed = (
        P("dp", "expert", None, None),
        P("dp", "expert", None),
        P("dp", "expert"),
        P("dp", None, "expert"),
        P("dp", None, "expert"),
        P("dp", "expert"),
        P("dp", "expert"),
        P("dp", "expert"),
    )
    return jax.shard_map(
        local,
        mesh=mesh,
        in_specs=placed,
        out_specs=(
            P("dp", None, "expert"),
            P("dp", None, "expert"),
            P("dp", "expert"),
            P("dp", "expert"),
            P("dp", "expert"),
            P(None, "expert"),
        ),
        check_vma=False,
    )
```

```python
import functools

import jax
import jax.numpy as jnp
from jax import lax
from jax.experimental import pallas as pl
from jax.experimental.pallas import tpu as pltpu
from jax.sharding import PartitionSpec as P

learning_rate = 0.01
beta_one = 0.9
beta_two = 0.95
decay_rate = 0.1
epsilon = 1e-08

bf16 = jnp.bfloat16
f32 = jnp.float32
VMEM_LIMIT = 40 * 1024 * 1024
LANES = 128


def params():
    return pltpu.CompilerParams(vmem_limit_bytes=VMEM_LIMIT)


def cost(flops, nbytes):
    return pl.CostEstimate(flops=flops, bytes_accessed=nbytes, transcendentals=0)


def take(refs, count):
    taken = refs[:count]
    del refs[:count]
    return taken


def wide(tiles):
    return tiles[0] if len(tiles) == 1 else jnp.concatenate(tiles, axis=1)


def tall(blocks):
    return blocks[0] if len(blocks) == 1 else jnp.concatenate(blocks, axis=0)


def seat_of(ways):
    seat = lax.axis_index("expert")
    return lax.axis_index("dp"), lax.rem(seat, ways), lax.div(seat, ways)


def scale_kernel(counts_in, router_in, rows_in, gate_in, up_in, *refs):
    hidden, outs = refs[0], refs[1:-7]
    counts, router, rows, gate, up, cut, sems = refs[-7:]
    copies = [
        pltpu.make_async_copy(source, target, sems.at[n])
        for n, (source, target) in enumerate(
            [
                (gate_in, gate),
                (up_in, up),
                (counts_in, counts),
                (router_in, router),
                (rows_in, rows),
            ]
        )
    ]
    for copy in copies:
        copy.start()
    flight, slots, width = rows.shape[1:]
    pieces = cut.shape[0]
    piece = width // pieces
    ways = hidden.shape[0]
    me, _, own = seat_of(ways)
    copies[0].wait()
    copies[1].wait()
    g = gate[0].astype(f32)
    value = (g * jax.nn.sigmoid(g) * up[0].astype(f32)).astype(bf16)
    for f in range(flight):
        for v in range(ways):
            at = (f * ways + v) * slots
            hidden[v, f] = value[at : at + slots]
    for copy in copies[2:]:
        copy.wait()
    diagonal = lax.broadcasted_iota(jnp.int32, (slots, slots), 0) == lax.broadcasted_iota(
        jnp.int32, (slots, slots), 1
    )
    row = lax.broadcasted_iota(jnp.int32, (slots, 1), 0)
    for f in range(flight):
        weight = jnp.sum(
            jnp.where(diagonal, jnp.broadcast_to(router[0, f : f + 1, :], (slots, slots)), 0.0),
            axis=1,
            keepdims=True,
        )
        live = row < counts[0, f]
        scaled = jnp.where(live, weight * rows[0, f].astype(f32), 0.0).astype(bf16)
        for i in range(pieces):
            cut[i, f] = scaled[:, i * piece : (i + 1) * piece]
    for n, out in enumerate(outs):
        for dc in range(2):
            out[dc] = cut[me ^ (n % (pieces // 2) * 2 + dc), own ^ (n // (pieces // 2))]


def fetch_kernel(after, *refs):
    del after
    sems = refs[6]
    copies = [pltpu.make_async_copy(refs[n], refs[3 + n], sems.at[n]) for n in range(3)]
    for copy in copies:
        copy.start()
    for copy in copies:
        copy.wait()


def share_kernel(order, *refs):
    for n, block in zip(order, refs):
        refs[-1][n] = block[1]


def pack_kernel(spans, other, *refs):
    blocks, outs = refs[: -len(spans)], refs[-len(spans) :]
    for (start, stop), out in zip(spans, outs):
        for n, block in enumerate(blocks):
            out[2 * n] = block[0, :, start:stop]
            out[2 * n + 1] = other[n, :, start:stop]


def order_kernel(*refs):
    hiddens, right = refs[:-1], refs[-1]
    ways, flight = right.shape[:2]
    _, lane, own = seat_of(ways)
    for dj, hidden in enumerate(hiddens):
        for d in range(ways):
            for dg in range(flight):
                right[d, dg, dj] = hidden[lane ^ d, own ^ dg]


def update_kernel(start, stop, *refs):
    refs = list(refs)
    rows = refs[:-9]
    right, master, first, second, fresh, new_master, new_first, new_second, gradient = refs[-9:]
    hidden = right[...].reshape(-1, right.shape[-1])
    left = tall([block[...].reshape(-1, stop - start) for block in rows])
    gradient[...] = lax.dot_general(
        left, hidden, (((0,), (0,)), ((), ())), preferred_element_type=f32
    )
    for low in range(start, stop, 128):
        end = min(low + 128, stop)
        here = pl.ds(low, end - low)
        there = pl.ds(low - start, end - low)
        grad = gradient[there]
        old = master[here]
        moment_a = beta_one * first[here] + (1.0 - beta_one) * grad
        moment_b = beta_two * second[here] + (1.0 - beta_two) * grad * grad
        step_size = (moment_a * (1.0 / (1.0 - beta_one**5))) / (
            jnp.sqrt(moment_b * (1.0 / (1.0 - beta_two**5))) + epsilon
        )
        updated = old - learning_rate * (step_size + decay_rate * old)
        fresh[there] = updated.astype(bf16)
        new_master[there] = updated
        new_first[there] = moment_a
        new_second[there] = moment_b


def partial_kernel(spans, kept, *refs):
    refs = list(refs)
    chunks = len(spans)
    keep, send, own_fresh, held = refs[-4:]
    ways = held.shape[0]
    rows, fresh, (master,) = take(refs, ways * chunks), take(refs, chunks), take(refs, 1)
    flight = held.shape[1]
    _, lane, own = seat_of(ways)
    left = wide(
        [
            tall([block[...].reshape(-1, stop - start) for block in rows[c * ways : (c + 1) * ways]])
            for c, (start, stop) in enumerate(spans)
        ]
    )
    share = jnp.dot(left, master[...].astype(bf16), preferred_element_type=f32)
    held[...] = share.reshape(held.shape)
    for out, chosen in ((keep, kept[0]), (send, kept[1])):
        for n, dj in enumerate(chosen):
            for d in range(ways):
                for dg in range(flight):
                    out[n, lane ^ d, own ^ dg] = held[d, dg, dj].astype(out.dtype)
    for c, (start, stop) in enumerate(spans):
        own_fresh[start:stop] = fresh[c][...]


def halve_kernel(kept, held, arrived, keep, send):
    for out, chosen in ((keep, kept[0]), (send, kept[1])):
        for n, m in enumerate(chosen):
            out[n] = (held[m] + arrived[m].astype(f32)).astype(out.dtype)


def store_kernel(spans, *refs):
    refs = list(refs)
    news = take(refs, 3 * len(spans))
    outs = take(refs, 3)
    (sems,) = refs
    copies = []
    for c, (start, stop) in enumerate(spans):
        for n in range(3):
            copy = pltpu.make_async_copy(
                news[3 * c + n], outs[n].at[pl.ds(start, stop - start)], sems.at[c, n]
            )
            copy.start()
            copies.append(copy)
    for copy in copies:
        copy.wait()


def gate_kernel(gate, up, held, arrived, d_gate, d_up):
    ways, flight, slots = held.shape[1:4]
    for f in range(flight):
        for v in range(ways):
            at = pl.ds((f * ways + v) * slots, slots)
            grad = held[0, v, f] + arrived[0, v, f].astype(f32)
            g = gate[0, at].astype(f32)
            u = up[0, at].astype(f32)
            sig = jax.nn.sigmoid(g)
            d_gate[0, at] = (grad * u * sig * (1.0 + g * (1.0 - sig))).astype(bf16)
            d_up[0, at] = (grad * (g * sig)).astype(bf16)


def join_kernel(high, entries, *refs):
    out, sems = refs[-2], refs[-1]
    me = lax.axis_index("dp")
    copies = []
    for n, (d, start, stop) in enumerate(entries):
        at = pl.multiple_of((me ^ d) * high + start, 16)
        copy = pltpu.make_async_copy(refs[n], out.at[pl.ds(at, stop - start)], sems.at[n])
        copy.start()
        copies.append(copy)
    for copy in copies:
        copy.wait()


def whole(memory=pltpu.VMEM):
    return pl.BlockSpec(memory_space=memory)


def shape(dims, kind):
    return jax.ShapeDtypeStruct(dims, kind)


def pinned(x):
    return pltpu.with_memory_space_constraint(x, pltpu.HBM)


def local(
    grad_rows,
    router_weight,
    send_counts,
    gate_stash,
    up_stash,
    master_weight,
    first_moment,
    second_moment,
):
    _, flight, slots, width = grad_rows.shape
    pieces = lax.axis_size("dp")
    sources = lax.axis_size("expert")
    ways = sources // flight
    high, across = master_weight.shape
    hbm = whole(pltpu.HBM)
    count = pieces * flight * slots

    def over_dp(x, d):
        return lax.ppermute(x, "dp", [(i, i ^ d) for i in range(pieces)])

    tiles = -(-high // LANES)
    middle = (tiles + 1) // 2 * LANES
    spans = [(0, middle), (middle, high)] if middle < high else [(0, high)]
    offsets = [(dj, dg) for dg in range(flight) for dj in range(0, pieces, 2)]
    results = pl.pallas_call(
        scale_kernel,
        out_shape=[shape((ways, flight, slots, across), bf16)]
        + [shape((2, slots, high), bf16)] * len(offsets),
        in_specs=[hbm] * 5,
        out_specs=[whole()] * (1 + len(offsets)),
        scratch_shapes=[
            pltpu.SMEM(send_counts.shape, jnp.int32),
            pltpu.VMEM(router_weight.shape, f32),
            pltpu.VMEM(grad_rows.shape, bf16),
            pltpu.VMEM(gate_stash.shape, bf16),
            pltpu.VMEM(up_stash.shape, bf16),
            pltpu.VMEM((pieces, flight, slots, high), bf16),
            pltpu.SemaphoreType.DMA((5,)),
        ],
        compiler_params=params(),
        name="scale",
    )(
        pinned(send_counts),
        pinned(router_weight),
        pinned(grad_rows),
        pinned(gate_stash),
        pinned(up_stash),
    )
    hidden, blocks = results[0], list(results[1:])
    for n, (dj, dg) in reversed(list(enumerate(offsets))):
        if n:
            pairs = [
                (i * sources + k, (i ^ dj) * sources + (k ^ (dg * ways)))
                for i in range(pieces)
                for k in range(sources)
            ]
            blocks[n] = lax.ppermute(blocks[n], ("dp", "expert"), pairs)
    state = pl.pallas_call(
        fetch_kernel,
        out_shape=[shape((high, across), f32)] * 3,
        in_specs=[whole(pl.ANY)] + [hbm] * 3,
        out_specs=[whole()] * 3,
        scratch_shapes=[pltpu.SemaphoreType.DMA((3,))],
        compiler_params=params(),
        cost_estimate=cost(0, high * across * 24),
        name="fetch",
    )(hidden, pinned(master_weight), pinned(first_moment), pinned(second_moment))
    order = [*range(pieces // 2, len(offsets)), *range(1, pieces // 2), 0]
    turned, state = lax.optimization_barrier(([blocks[n] for n in order], state))
    blocks = [turned[order.index(n)] for n in range(len(offsets))]
    other = pl.pallas_call(
        functools.partial(share_kernel, order),
        out_shape=shape((len(offsets), slots, high), bf16),
        in_specs=[whole()] * len(offsets),
        out_specs=whole(),
        compiler_params=params(),
        name="share",
    )(*[blocks[n] for n in order])
    mine = pl.pallas_call(
        functools.partial(pack_kernel, spans),
        out_shape=[shape((2 * len(offsets), slots, stop - start), bf16) for start, stop in spans],
        in_specs=[whole()] * (1 + len(offsets)),
        out_specs=[whole()] * len(spans),
        compiler_params=params(),
        name="pack",
    )(over_dp(other, 1), *blocks)
    top = pieces // 2

    def spread(entries, first):
        step = first
        while step:
            entries = entries + [(d ^ step, *span, over_dp(x, step)) for d, *span, x in entries]
            step //= 2
        return entries

    hiddens = [entry[1] for entry in sorted(spread([(0, hidden)], top), key=lambda e: e[0])]
    right = pl.pallas_call(
        order_kernel,
        out_shape=shape((ways, flight, pieces, slots, across), bf16),
        in_specs=[whole()] * pieces,
        out_specs=whole(),
        compiler_params=params(),
        name="order",
    )(*hiddens)
    rows = []
    for piece in mine:
        rows.append(
            [piece]
            + [
                lax.ppermute(piece, "expert", [(k, k ^ d) for k in range(sources)])
                for d in range(1, ways)
            ]
        )

    fresh, news = [], []
    for c, (start, stop) in enumerate(spans):
        out = pl.pallas_call(
            functools.partial(update_kernel, start, stop),
            out_shape=[shape((stop - start, across), bf16)]
            + [shape((stop - start, across), f32)] * 3,
            in_specs=[whole()] * (ways + 4),
            out_specs=[whole()] * 4,
            scratch_shapes=[pltpu.VMEM((stop - start, across), f32)],
            compiler_params=params(),
            cost_estimate=cost(2 * ways * count * (stop - start) * across, high * across * 26),
            name="update",
        )(*rows[c], right, *state)
        fresh.append(out[0])
        news += out[1:]
    crossed = [over_dp(piece, top) for piece in fresh]

    part = (ways, flight, slots, across)
    bit = 1
    kept = [[d for d in range(pieces) if not d & bit], [d for d in range(pieces) if d & bit]]
    keep, send, own_fresh = pl.pallas_call(
        functools.partial(partial_kernel, spans, kept),
        out_shape=[
            shape((pieces // 2, *part), f32),
            shape((pieces // 2, *part), bf16),
            shape((high, across), bf16),
        ],
        in_specs=[whole()] * ((ways + 1) * len(spans) + 1),
        out_specs=[whole()] * 3,
        scratch_shapes=[pltpu.VMEM((ways, flight, pieces, slots, across), f32)],
        compiler_params=params(),
        cost_estimate=cost(2 * ways * count * high * across, high * across * 12),
        name="partial",
    )(*[block for chunk in rows for block in chunk], *fresh, state[0])
    arrived = over_dp(send, bit)
    while bit < top:
        bit *= 2
        left = kept[0]
        kept = [[d for d in left if not d & bit], [d for d in left if d & bit]]
        chosen = [[left.index(d) for d in half] for half in kept]
        keep, send = pl.pallas_call(
            functools.partial(halve_kernel, chosen),
            out_shape=[
                shape((len(kept[0]), *part), f32),
                shape((len(kept[1]), *part), bf16),
            ],
            in_specs=[whole()] * 2,
            out_specs=[whole()] * 2,
            compiler_params=params(),
            name="halve",
        )(keep, arrived)
        arrived = over_dp(send, bit)
    if len(spans) > 1:
        crossed[0], keep = lax.optimization_barrier((crossed[0], keep))
    d_gate, d_up = pl.pallas_call(
        gate_kernel,
        out_shape=[shape(gate_stash.shape, bf16)] * 2,
        in_specs=[whole()] * 4,
        out_specs=[whole()] * 2,
        compiler_params=params(),
        name="gates",
    )(gate_stash, up_stash, keep, arrived)

    states = pl.pallas_call(
        functools.partial(store_kernel, spans),
        out_shape=[shape((high, across), f32)] * 3,
        in_specs=[whole()] * len(news),
        out_specs=[hbm] * 3,
        scratch_shapes=[pltpu.SemaphoreType.DMA((len(spans), 3))],
        compiler_params=params(),
        cost_estimate=cost(0, high * across * 24),
        name="store",
    )(*news)

    def join(entries, before):
        return pl.pallas_call(
            functools.partial(join_kernel, high, [entry[:3] for entry in entries]),
            out_shape=shape((pieces * high, across), bf16),
            in_specs=[whole(pl.ANY)] * len(entries) + [hbm] * len(before),
            out_specs=hbm,
            input_output_aliases={len(entries): 0} if before else {},
            scratch_shapes=[pltpu.SemaphoreType.DMA((len(entries),))],
            compiler_params=params(),
            name="join",
        )(*[entry[3] for entry in entries], *before)

    near, *far = spread([(0, 0, high, own_fresh)], top // 2)
    early, late = [near], far
    for (start, stop), piece in zip(spans[:-1], crossed[:-1]):
        near, *far = spread([(top, start, stop, piece)], top // 2)
        early.append(near)
        late += far
    joined = join(early, [])
    crossed[-1], joined, states, arrived = lax.optimization_barrier(
        (crossed[-1], joined, states, arrived)
    )
    joined = join(late + spread([(top, *spans[-1], crossed[-1])], top // 2), [joined])
    return (d_gate, d_up, *states, joined)


def solution(mesh):
    placed = (
        P("dp", "expert", None, None),
        P("dp", "expert", None),
        P("dp", "expert"),
        P("dp", None, "expert"),
        P("dp", None, "expert"),
        P("dp", "expert"),
        P("dp", "expert"),
        P("dp", "expert"),
    )
    return jax.shard_map(
        local,
        mesh=mesh,
        in_specs=placed,
        out_specs=(
            P("dp", None, "expert"),
            P("dp", None, "expert"),
            P("dp", "expert"),
            P("dp", "expert"),
            P("dp", "expert"),
            P(None, "expert"),
        ),
        check_vma=False,
    )
```

```python
import functools

import jax
import jax.numpy as jnp
from jax import lax
from jax.experimental import pallas as pl
from jax.experimental.pallas import tpu as pltpu
from jax.sharding import PartitionSpec as P

learning_rate = 0.01
beta_one = 0.9
beta_two = 0.95
decay_rate = 0.1
epsilon = 1e-08

bf16 = jnp.bfloat16
f32 = jnp.float32
VMEM_LIMIT = 40 * 1024 * 1024
LANES = 128


def params():
    return pltpu.CompilerParams(vmem_limit_bytes=VMEM_LIMIT)


def cost(flops, nbytes):
    return pl.CostEstimate(flops=flops, bytes_accessed=nbytes, transcendentals=0)


def take(refs, count):
    taken = refs[:count]
    del refs[:count]
    return taken


def wide(tiles):
    return tiles[0] if len(tiles) == 1 else jnp.concatenate(tiles, axis=1)


def tall(blocks):
    return blocks[0] if len(blocks) == 1 else jnp.concatenate(blocks, axis=0)


def turns(ways):
    return [0, *range(ways - 1, 0, -1)]


def seat_of(ways):
    seat = lax.axis_index("expert")
    return lax.axis_index("dp"), lax.rem(seat, ways), lax.div(seat, ways)


def scale_kernel(counts_in, router_in, rows_in, gate_in, up_in, *refs):
    hidden, outs = refs[0], refs[1:-7]
    counts, router, rows, gate, up, cut, sems = refs[-7:]
    copies = [
        pltpu.make_async_copy(source, target, sems.at[n])
        for n, (source, target) in enumerate(
            [
                (gate_in, gate),
                (up_in, up),
                (counts_in, counts),
                (router_in, router),
                (rows_in, rows),
            ]
        )
    ]
    for copy in copies:
        copy.start()
    flight, slots, width = rows.shape[1:]
    pieces = cut.shape[0]
    piece = width // pieces
    ways = hidden.shape[0]
    me, _, own = seat_of(ways)
    copies[0].wait()
    copies[1].wait()
    g = gate[0].astype(f32)
    value = (g * jax.nn.sigmoid(g) * up[0].astype(f32)).astype(bf16)
    for f in range(flight):
        for v in range(ways):
            at = (f * ways + v) * slots
            hidden[v, f] = value[at : at + slots]
    for copy in copies[2:]:
        copy.wait()
    diagonal = lax.broadcasted_iota(jnp.int32, (slots, slots), 0) == lax.broadcasted_iota(
        jnp.int32, (slots, slots), 1
    )
    row = lax.broadcasted_iota(jnp.int32, (slots, 1), 0)
    for f in range(flight):
        weight = jnp.sum(
            jnp.where(diagonal, jnp.broadcast_to(router[0, f : f + 1, :], (slots, slots)), 0.0),
            axis=1,
            keepdims=True,
        )
        live = row < counts[0, f]
        scaled = jnp.where(live, weight * rows[0, f].astype(f32), 0.0).astype(bf16)
        for i in range(pieces):
            cut[i, f] = scaled[:, i * piece : (i + 1) * piece]
    for n, out in enumerate(outs):
        for dc in range(2):
            out[dc] = cut[me ^ (n % (pieces // 2) * 2 + dc), own ^ (n // (pieces // 2))]


def fetch_kernel(after, *refs):
    del after
    sems = refs[6]
    copies = [pltpu.make_async_copy(refs[n], refs[3 + n], sems.at[n]) for n in range(3)]
    for copy in copies:
        copy.start()
    for copy in copies:
        copy.wait()


def share_kernel(order, *refs):
    for n, block in zip(order, refs):
        refs[-1][n] = block[1]


def pack_kernel(spans, other, *refs):
    blocks, outs = refs[: -len(spans)], refs[-len(spans) :]
    for (start, stop), out in zip(spans, outs):
        for n, block in enumerate(blocks):
            out[2 * n] = block[0, :, start:stop]
            out[2 * n + 1] = other[n, :, start:stop]


def order_kernel(*refs):
    hiddens, right = refs[:-1], refs[-1]
    ways, flight = right.shape[:2]
    _, lane, own = seat_of(ways)
    for dj, hidden in enumerate(hiddens):
        for n, d in enumerate(turns(ways)):
            for dg in range(flight):
                right[n, dg, dj] = hidden[lane ^ d, own ^ dg]


def update_kernel(start, stop, *refs):
    refs = list(refs)
    rows = refs[:-9]
    right, master, first, second, fresh, new_master, new_first, new_second, gradient = refs[-9:]
    hidden = right[...].reshape(-1, right.shape[-1])
    left = tall([block[...].reshape(-1, stop - start) for block in rows])
    gradient[...] = lax.dot_general(
        left, hidden, (((0,), (0,)), ((), ())), preferred_element_type=f32
    )
    for low in range(start, stop, 128):
        end = min(low + 128, stop)
        here = pl.ds(low, end - low)
        there = pl.ds(low - start, end - low)
        grad = gradient[there]
        old = master[here]
        moment_a = beta_one * first[here] + (1.0 - beta_one) * grad
        moment_b = beta_two * second[here] + (1.0 - beta_two) * grad * grad
        step_size = (moment_a * (1.0 / (1.0 - beta_one**5))) / (
            jnp.sqrt(moment_b * (1.0 / (1.0 - beta_two**5))) + epsilon
        )
        updated = old - learning_rate * (step_size + decay_rate * old)
        fresh[there] = updated.astype(bf16)
        new_master[there] = updated
        new_first[there] = moment_a
        new_second[there] = moment_b


def partial_kernel(spans, kept, *refs):
    refs = list(refs)
    chunks = len(spans)
    keep, send, own_fresh, held = refs[-4:]
    ways = held.shape[0]
    rows, fresh, (master,) = take(refs, ways * chunks), take(refs, chunks), take(refs, 1)
    flight = held.shape[1]
    _, lane, own = seat_of(ways)
    left = wide(
        [
            tall([block[...].reshape(-1, stop - start) for block in rows[c * ways : (c + 1) * ways]])
            for c, (start, stop) in enumerate(spans)
        ]
    )
    share = jnp.dot(left, master[...].astype(bf16), preferred_element_type=f32)
    held[...] = share.reshape(held.shape)
    for out, chosen in ((keep, kept[0]), (send, kept[1])):
        for n, dj in enumerate(chosen):
            for at, d in enumerate(turns(ways)):
                for dg in range(flight):
                    out[n, lane ^ d, own ^ dg] = held[at, dg, dj].astype(out.dtype)
    for c, (start, stop) in enumerate(spans):
        own_fresh[start:stop] = fresh[c][...]


def halve_kernel(kept, held, arrived, keep, send):
    for out, chosen in ((keep, kept[0]), (send, kept[1])):
        for n, m in enumerate(chosen):
            out[n] = (held[m] + arrived[m].astype(f32)).astype(out.dtype)


def store_kernel(spans, *refs):
    refs = list(refs)
    news = take(refs, 3 * len(spans))
    outs = take(refs, 3)
    (sems,) = refs
    copies = []
    for c, (start, stop) in enumerate(spans):
        for n in range(3):
            copy = pltpu.make_async_copy(
                news[3 * c + n], outs[n].at[pl.ds(start, stop - start)], sems.at[c, n]
            )
            copy.start()
            copies.append(copy)
    for copy in copies:
        copy.wait()


def gate_kernel(gate, up, held, arrived, d_gate, d_up):
    ways, flight, slots = held.shape[1:4]
    for f in range(flight):
        for v in range(ways):
            at = pl.ds((f * ways + v) * slots, slots)
            grad = held[0, v, f] + arrived[0, v, f].astype(f32)
            g = gate[0, at].astype(f32)
            u = up[0, at].astype(f32)
            sig = jax.nn.sigmoid(g)
            d_gate[0, at] = (grad * u * sig * (1.0 + g * (1.0 - sig))).astype(bf16)
            d_up[0, at] = (grad * (g * sig)).astype(bf16)


def join_kernel(high, entries, *refs):
    out, sems = refs[-2], refs[-1]
    me = lax.axis_index("dp")
    copies = []
    for n, (d, start, stop) in enumerate(entries):
        at = pl.multiple_of((me ^ d) * high + start, 16)
        copy = pltpu.make_async_copy(refs[n], out.at[pl.ds(at, stop - start)], sems.at[n])
        copy.start()
        copies.append(copy)
    for copy in copies:
        copy.wait()


def whole(memory=pltpu.VMEM):
    return pl.BlockSpec(memory_space=memory)


def shape(dims, kind):
    return jax.ShapeDtypeStruct(dims, kind)


def pinned(x):
    return pltpu.with_memory_space_constraint(x, pltpu.HBM)


def local(
    grad_rows,
    router_weight,
    send_counts,
    gate_stash,
    up_stash,
    master_weight,
    first_moment,
    second_moment,
):
    _, flight, slots, width = grad_rows.shape
    pieces = lax.axis_size("dp")
    sources = lax.axis_size("expert")
    ways = sources // flight
    high, across = master_weight.shape
    hbm = whole(pltpu.HBM)
    count = pieces * flight * slots

    def over_dp(x, d):
        return lax.ppermute(x, "dp", [(i, i ^ d) for i in range(pieces)])

    tiles = -(-high // LANES)
    middle = (tiles + 1) // 2 * LANES
    spans = [(0, middle), (middle, high)] if middle < high else [(0, high)]
    offsets = [(dj, dg) for dg in range(flight) for dj in range(0, pieces, 2)]
    results = pl.pallas_call(
        scale_kernel,
        out_shape=[shape((ways, flight, slots, across), bf16)]
        + [shape((2, slots, high), bf16)] * len(offsets),
        in_specs=[hbm] * 5,
        out_specs=[whole()] * (1 + len(offsets)),
        scratch_shapes=[
            pltpu.SMEM(send_counts.shape, jnp.int32),
            pltpu.VMEM(router_weight.shape, f32),
            pltpu.VMEM(grad_rows.shape, bf16),
            pltpu.VMEM(gate_stash.shape, bf16),
            pltpu.VMEM(up_stash.shape, bf16),
            pltpu.VMEM((pieces, flight, slots, high), bf16),
            pltpu.SemaphoreType.DMA((5,)),
        ],
        compiler_params=params(),
        name="scale",
    )(
        pinned(send_counts),
        pinned(router_weight),
        pinned(grad_rows),
        pinned(gate_stash),
        pinned(up_stash),
    )
    hidden, blocks = results[0], list(results[1:])
    for n, (dj, dg) in reversed(list(enumerate(offsets))):
        if n:
            pairs = [
                (i * sources + k, (i ^ dj) * sources + (k ^ (dg * ways)))
                for i in range(pieces)
                for k in range(sources)
            ]
            blocks[n] = lax.ppermute(blocks[n], ("dp", "expert"), pairs)
    state = pl.pallas_call(
        fetch_kernel,
        out_shape=[shape((high, across), f32)] * 3,
        in_specs=[whole(pl.ANY)] + [hbm] * 3,
        out_specs=[whole()] * 3,
        scratch_shapes=[pltpu.SemaphoreType.DMA((3,))],
        compiler_params=params(),
        cost_estimate=cost(0, high * across * 24),
        name="fetch",
    )(hidden, pinned(master_weight), pinned(first_moment), pinned(second_moment))
    order = [*range(pieces // 2, len(offsets)), *range(1, pieces // 2), 0]
    turned, state = lax.optimization_barrier(([blocks[n] for n in order], state))
    blocks = [turned[order.index(n)] for n in range(len(offsets))]
    other = pl.pallas_call(
        functools.partial(share_kernel, order),
        out_shape=shape((len(offsets), slots, high), bf16),
        in_specs=[whole()] * len(offsets),
        out_specs=whole(),
        compiler_params=params(),
        name="share",
    )(*[blocks[n] for n in order])
    mine = pl.pallas_call(
        functools.partial(pack_kernel, spans),
        out_shape=[shape((2 * len(offsets), slots, stop - start), bf16) for start, stop in spans],
        in_specs=[whole()] * (1 + len(offsets)),
        out_specs=[whole()] * len(spans),
        compiler_params=params(),
        name="pack",
    )(over_dp(other, 1), *blocks)
    top = pieces // 2

    def spread(entries, first):
        step = first
        while step:
            entries = entries + [(d ^ step, *span, over_dp(x, step)) for d, *span, x in entries]
            step //= 2
        return entries

    hiddens = [entry[1] for entry in sorted(spread([(0, hidden)], top), key=lambda e: e[0])]
    right = pl.pallas_call(
        order_kernel,
        out_shape=shape((ways, flight, pieces, slots, across), bf16),
        in_specs=[whole()] * pieces,
        out_specs=whole(),
        compiler_params=params(),
        name="order",
    )(*hiddens)
    rows = []
    for piece in mine:
        rows.append(
            [piece]
            + [
                lax.ppermute(piece, "expert", [(k, k ^ d) for k in range(sources)])
                for d in turns(ways)[1:]
            ]
        )

    fresh, news = [], []
    for c, (start, stop) in enumerate(spans):
        out = pl.pallas_call(
            functools.partial(update_kernel, start, stop),
            out_shape=[shape((stop - start, across), bf16)]
            + [shape((stop - start, across), f32)] * 3,
            in_specs=[whole()] * (ways + 4),
            out_specs=[whole()] * 4,
            scratch_shapes=[pltpu.VMEM((stop - start, across), f32)],
            compiler_params=params(),
            cost_estimate=cost(2 * ways * count * (stop - start) * across, high * across * 26),
            name="update",
        )(*rows[c], right, *state)
        fresh.append(out[0])
        news += out[1:]
    crossed = [over_dp(piece, top) for piece in fresh]

    part = (ways, flight, slots, across)
    bit = 1
    kept = [[d for d in range(pieces) if not d & bit], [d for d in range(pieces) if d & bit]]
    keep, send, own_fresh = pl.pallas_call(
        functools.partial(partial_kernel, spans, kept),
        out_shape=[
            shape((pieces // 2, *part), f32),
            shape((pieces // 2, *part), bf16),
            shape((high, across), bf16),
        ],
        in_specs=[whole()] * ((ways + 1) * len(spans) + 1),
        out_specs=[whole()] * 3,
        scratch_shapes=[pltpu.VMEM((ways, flight, pieces, slots, across), f32)],
        compiler_params=params(),
        cost_estimate=cost(2 * ways * count * high * across, high * across * 12),
        name="partial",
    )(*[block for chunk in rows for block in chunk], *fresh, state[0])
    arrived = over_dp(send, bit)
    while bit < top:
        bit *= 2
        left = kept[0]
        kept = [[d for d in left if not d & bit], [d for d in left if d & bit]]
        chosen = [[left.index(d) for d in half] for half in kept]
        keep, send = pl.pallas_call(
            functools.partial(halve_kernel, chosen),
            out_shape=[
                shape((len(kept[0]), *part), f32),
                shape((len(kept[1]), *part), bf16),
            ],
            in_specs=[whole()] * 2,
            out_specs=[whole()] * 2,
            compiler_params=params(),
            name="halve",
        )(keep, arrived)
        arrived = over_dp(send, bit)
    if len(spans) > 1:
        crossed[0], keep = lax.optimization_barrier((crossed[0], keep))
    d_gate, d_up = pl.pallas_call(
        gate_kernel,
        out_shape=[shape(gate_stash.shape, bf16)] * 2,
        in_specs=[whole()] * 4,
        out_specs=[whole()] * 2,
        compiler_params=params(),
        name="gates",
    )(gate_stash, up_stash, keep, arrived)

    states = pl.pallas_call(
        functools.partial(store_kernel, spans),
        out_shape=[shape((high, across), f32)] * 3,
        in_specs=[whole()] * len(news),
        out_specs=[hbm] * 3,
        scratch_shapes=[pltpu.SemaphoreType.DMA((len(spans), 3))],
        compiler_params=params(),
        cost_estimate=cost(0, high * across * 24),
        name="store",
    )(*news)

    def join(entries, before):
        return pl.pallas_call(
            functools.partial(join_kernel, high, [entry[:3] for entry in entries]),
            out_shape=shape((pieces * high, across), bf16),
            in_specs=[whole(pl.ANY)] * len(entries) + [hbm] * len(before),
            out_specs=hbm,
            input_output_aliases={len(entries): 0} if before else {},
            scratch_shapes=[pltpu.SemaphoreType.DMA((len(entries),))],
            compiler_params=params(),
            name="join",
        )(*[entry[3] for entry in entries], *before)

    near, *far = spread([(0, 0, high, own_fresh)], top // 2)
    early, late = [near], far
    for (start, stop), piece in zip(spans[:-1], crossed[:-1]):
        near, *far = spread([(top, start, stop, piece)], top // 2)
        early.append(near)
        late += far
    joined = join(early, [])
    crossed[-1], joined, states, arrived = lax.optimization_barrier(
        (crossed[-1], joined, states, arrived)
    )
    joined = join(late + spread([(top, *spans[-1], crossed[-1])], top // 2), [joined])
    return (d_gate, d_up, *states, joined)


def solution(mesh):
    placed = (
        P("dp", "expert", None, None),
        P("dp", "expert", None),
        P("dp", "expert"),
        P("dp", None, "expert"),
        P("dp", None, "expert"),
        P("dp", "expert"),
        P("dp", "expert"),
        P("dp", "expert"),
    )
    return jax.shard_map(
        local,
        mesh=mesh,
        in_specs=placed,
        out_specs=(
            P("dp", None, "expert"),
            P("dp", None, "expert"),
            P("dp", "expert"),
            P("dp", "expert"),
            P("dp", "expert"),
            P(None, "expert"),
        ),
        check_vma=False,
    )
```

```python
import functools

import jax
import jax.numpy as jnp
from jax import lax
from jax.experimental import pallas as pl
from jax.experimental.pallas import tpu as pltpu
from jax.sharding import PartitionSpec as P

learning_rate = 0.01
beta_one = 0.9
beta_two = 0.95
decay_rate = 0.1
epsilon = 1e-08

bf16 = jnp.bfloat16
f32 = jnp.float32
VMEM_LIMIT = 40 * 1024 * 1024
LANES = 128


def params():
    return pltpu.CompilerParams(vmem_limit_bytes=VMEM_LIMIT)


def cost(flops, nbytes):
    return pl.CostEstimate(flops=flops, bytes_accessed=nbytes, transcendentals=0)


def take(refs, count):
    taken = refs[:count]
    del refs[:count]
    return taken


def wide(tiles):
    return tiles[0] if len(tiles) == 1 else jnp.concatenate(tiles, axis=1)


def tall(blocks):
    return blocks[0] if len(blocks) == 1 else jnp.concatenate(blocks, axis=0)


def turns(ways):
    near = [d for d in range(1, ways) if d & (d - 1) == 0]
    far = [d for d in range(1, ways) if d & (d - 1)]
    return [0, *near[1:], *far, *near[:1]]


def seat_of(ways):
    seat = lax.axis_index("expert")
    return lax.axis_index("dp"), lax.rem(seat, ways), lax.div(seat, ways)


def scale_kernel(counts_in, router_in, rows_in, gate_in, up_in, *refs):
    hidden, outs = refs[0], refs[1:-7]
    counts, router, rows, gate, up, cut, sems = refs[-7:]
    copies = [
        pltpu.make_async_copy(source, target, sems.at[n])
        for n, (source, target) in enumerate(
            [
                (gate_in, gate),
                (up_in, up),
                (counts_in, counts),
                (router_in, router),
                (rows_in, rows),
            ]
        )
    ]
    for copy in copies:
        copy.start()
    flight, slots, width = rows.shape[1:]
    pieces = cut.shape[0]
    piece = width // pieces
    ways = hidden.shape[0]
    me, _, own = seat_of(ways)
    copies[0].wait()
    copies[1].wait()
    g = gate[0].astype(f32)
    value = (g * jax.nn.sigmoid(g) * up[0].astype(f32)).astype(bf16)
    for f in range(flight):
        for v in range(ways):
            at = (f * ways + v) * slots
            hidden[v, f] = value[at : at + slots]
    for copy in copies[2:]:
        copy.wait()
    diagonal = lax.broadcasted_iota(jnp.int32, (slots, slots), 0) == lax.broadcasted_iota(
        jnp.int32, (slots, slots), 1
    )
    row = lax.broadcasted_iota(jnp.int32, (slots, 1), 0)
    for f in range(flight):
        weight = jnp.sum(
            jnp.where(diagonal, jnp.broadcast_to(router[0, f : f + 1, :], (slots, slots)), 0.0),
            axis=1,
            keepdims=True,
        )
        live = row < counts[0, f]
        scaled = jnp.where(live, weight * rows[0, f].astype(f32), 0.0).astype(bf16)
        for i in range(pieces):
            cut[i, f] = scaled[:, i * piece : (i + 1) * piece]
    for n, out in enumerate(outs):
        for dc in range(2):
            out[dc] = cut[me ^ (n % (pieces // 2) * 2 + dc), own ^ (n // (pieces // 2))]


def fetch_kernel(after, *refs):
    del after
    sems = refs[6]
    copies = [pltpu.make_async_copy(refs[n], refs[3 + n], sems.at[n]) for n in range(3)]
    for copy in copies:
        copy.start()
    for copy in copies:
        copy.wait()


def share_kernel(order, *refs):
    for n, block in zip(order, refs):
        refs[-1][n] = block[1]


def pack_kernel(spans, other, *refs):
    blocks, outs = refs[: -len(spans)], refs[-len(spans) :]
    for (start, stop), out in zip(spans, outs):
        for n, block in enumerate(blocks):
            out[2 * n] = block[0, :, start:stop]
            out[2 * n + 1] = other[n, :, start:stop]


def order_kernel(*refs):
    hiddens, right = refs[:-1], refs[-1]
    ways, flight = right.shape[:2]
    _, lane, own = seat_of(ways)
    for dj, hidden in enumerate(hiddens):
        for n, d in enumerate(turns(ways)):
            for dg in range(flight):
                right[n, dg, dj] = hidden[lane ^ d, own ^ dg]


def update_kernel(start, stop, *refs):
    refs = list(refs)
    rows = refs[:-9]
    right, master, first, second, fresh, new_master, new_first, new_second, gradient = refs[-9:]
    hidden = right[...].reshape(-1, right.shape[-1])
    left = tall([block[...].reshape(-1, stop - start) for block in rows])
    gradient[...] = lax.dot_general(
        left, hidden, (((0,), (0,)), ((), ())), preferred_element_type=f32
    )
    for low in range(start, stop, 128):
        end = min(low + 128, stop)
        here = pl.ds(low, end - low)
        there = pl.ds(low - start, end - low)
        grad = gradient[there]
        old = master[here]
        moment_a = beta_one * first[here] + (1.0 - beta_one) * grad
        moment_b = beta_two * second[here] + (1.0 - beta_two) * grad * grad
        step_size = (moment_a * (1.0 / (1.0 - beta_one**5))) / (
            jnp.sqrt(moment_b * (1.0 / (1.0 - beta_two**5))) + epsilon
        )
        updated = old - learning_rate * (step_size + decay_rate * old)
        fresh[there] = updated.astype(bf16)
        new_master[there] = updated
        new_first[there] = moment_a
        new_second[there] = moment_b


def partial_kernel(spans, kept, *refs):
    refs = list(refs)
    chunks = len(spans)
    keep, send, own_fresh, held = refs[-4:]
    ways = held.shape[0]
    rows, fresh, (master,) = take(refs, ways * chunks), take(refs, chunks), take(refs, 1)
    flight = held.shape[1]
    _, lane, own = seat_of(ways)
    left = wide(
        [
            tall([block[...].reshape(-1, stop - start) for block in rows[c * ways : (c + 1) * ways]])
            for c, (start, stop) in enumerate(spans)
        ]
    )
    share = jnp.dot(left, master[...].astype(bf16), preferred_element_type=f32)
    held[...] = share.reshape(held.shape)
    for out, chosen in ((keep, kept[0]), (send, kept[1])):
        for n, dj in enumerate(chosen):
            for at, d in enumerate(turns(ways)):
                for dg in range(flight):
                    out[n, lane ^ d, own ^ dg] = held[at, dg, dj].astype(out.dtype)
    for c, (start, stop) in enumerate(spans):
        own_fresh[start:stop] = fresh[c][...]


def halve_kernel(kept, held, arrived, keep, send):
    for out, chosen in ((keep, kept[0]), (send, kept[1])):
        for n, m in enumerate(chosen):
            out[n] = (held[m] + arrived[m].astype(f32)).astype(out.dtype)


def store_kernel(spans, *refs):
    refs = list(refs)
    news = take(refs, 3 * len(spans))
    outs = take(refs, 3)
    (sems,) = refs
    copies = []
    for c, (start, stop) in enumerate(spans):
        for n in range(3):
            copy = pltpu.make_async_copy(
                news[3 * c + n], outs[n].at[pl.ds(start, stop - start)], sems.at[c, n]
            )
            copy.start()
            copies.append(copy)
    for copy in copies:
        copy.wait()


def gate_kernel(gate, up, held, arrived, d_gate, d_up):
    ways, flight, slots = held.shape[1:4]
    for f in range(flight):
        for v in range(ways):
            at = pl.ds((f * ways + v) * slots, slots)
            grad = held[0, v, f] + arrived[0, v, f].astype(f32)
            g = gate[0, at].astype(f32)
            u = up[0, at].astype(f32)
            sig = jax.nn.sigmoid(g)
            d_gate[0, at] = (grad * u * sig * (1.0 + g * (1.0 - sig))).astype(bf16)
            d_up[0, at] = (grad * (g * sig)).astype(bf16)


def join_kernel(high, entries, *refs):
    out, sems = refs[-2], refs[-1]
    me = lax.axis_index("dp")
    copies = []
    for n, (d, start, stop) in enumerate(entries):
        at = pl.multiple_of((me ^ d) * high + start, 16)
        copy = pltpu.make_async_copy(refs[n], out.at[pl.ds(at, stop - start)], sems.at[n])
        copy.start()
        copies.append(copy)
    for copy in copies:
        copy.wait()


def whole(memory=pltpu.VMEM):
    return pl.BlockSpec(memory_space=memory)


def shape(dims, kind):
    return jax.ShapeDtypeStruct(dims, kind)


def pinned(x):
    return pltpu.with_memory_space_constraint(x, pltpu.HBM)


def local(
    grad_rows,
    router_weight,
    send_counts,
    gate_stash,
    up_stash,
    master_weight,
    first_moment,
    second_moment,
):
    _, flight, slots, width = grad_rows.shape
    pieces = lax.axis_size("dp")
    sources = lax.axis_size("expert")
    ways = sources // flight
    high, across = master_weight.shape
    hbm = whole(pltpu.HBM)
    count = pieces * flight * slots

    def over_dp(x, d):
        return lax.ppermute(x, "dp", [(i, i ^ d) for i in range(pieces)])

    tiles = -(-high // LANES)
    middle = (tiles + 1) // 2 * LANES
    spans = [(0, middle), (middle, high)] if middle < high else [(0, high)]
    offsets = [(dj, dg) for dg in range(flight) for dj in range(0, pieces, 2)]
    results = pl.pallas_call(
        scale_kernel,
        out_shape=[shape((ways, flight, slots, across), bf16)]
        + [shape((2, slots, high), bf16)] * len(offsets),
        in_specs=[hbm] * 5,
        out_specs=[whole()] * (1 + len(offsets)),
        scratch_shapes=[
            pltpu.SMEM(send_counts.shape, jnp.int32),
            pltpu.VMEM(router_weight.shape, f32),
            pltpu.VMEM(grad_rows.shape, bf16),
            pltpu.VMEM(gate_stash.shape, bf16),
            pltpu.VMEM(up_stash.shape, bf16),
            pltpu.VMEM((pieces, flight, slots, high), bf16),
            pltpu.SemaphoreType.DMA((5,)),
        ],
        compiler_params=params(),
        name="scale",
    )(
        pinned(send_counts),
        pinned(router_weight),
        pinned(grad_rows),
        pinned(gate_stash),
        pinned(up_stash),
    )
    hidden, blocks = results[0], list(results[1:])
    for n, (dj, dg) in reversed(list(enumerate(offsets))):
        if n:
            pairs = [
                (i * sources + k, (i ^ dj) * sources + (k ^ (dg * ways)))
                for i in range(pieces)
                for k in range(sources)
            ]
            blocks[n] = lax.ppermute(blocks[n], ("dp", "expert"), pairs)
    state = pl.pallas_call(
        fetch_kernel,
        out_shape=[shape((high, across), f32)] * 3,
        in_specs=[whole(pl.ANY)] + [hbm] * 3,
        out_specs=[whole()] * 3,
        scratch_shapes=[pltpu.SemaphoreType.DMA((3,))],
        compiler_params=params(),
        cost_estimate=cost(0, high * across * 24),
        name="fetch",
    )(hidden, pinned(master_weight), pinned(first_moment), pinned(second_moment))
    order = [*range(pieces // 2, len(offsets)), *range(1, pieces // 2), 0]
    turned, state = lax.optimization_barrier(([blocks[n] for n in order], state))
    blocks = [turned[order.index(n)] for n in range(len(offsets))]
    other = pl.pallas_call(
        functools.partial(share_kernel, order),
        out_shape=shape((len(offsets), slots, high), bf16),
        in_specs=[whole()] * len(offsets),
        out_specs=whole(),
        compiler_params=params(),
        name="share",
    )(*[blocks[n] for n in order])
    mine = pl.pallas_call(
        functools.partial(pack_kernel, spans),
        out_shape=[shape((2 * len(offsets), slots, stop - start), bf16) for start, stop in spans],
        in_specs=[whole()] * (1 + len(offsets)),
        out_specs=[whole()] * len(spans),
        compiler_params=params(),
        name="pack",
    )(over_dp(other, 1), *blocks)
    top = pieces // 2

    def spread(entries, first):
        step = first
        while step:
            entries = entries + [(d ^ step, *span, over_dp(x, step)) for d, *span, x in entries]
            step //= 2
        return entries

    hiddens = [entry[1] for entry in sorted(spread([(0, hidden)], top), key=lambda e: e[0])]
    right = pl.pallas_call(
        order_kernel,
        out_shape=shape((ways, flight, pieces, slots, across), bf16),
        in_specs=[whole()] * pieces,
        out_specs=whole(),
        compiler_params=params(),
        name="order",
    )(*hiddens)
    rows = []
    for piece in mine:
        rows.append(
            [piece]
            + [
                lax.ppermute(piece, "expert", [(k, k ^ d) for k in range(sources)])
                for d in turns(ways)[1:]
            ]
        )

    fresh, news = [], []
    for c, (start, stop) in enumerate(spans):
        out = pl.pallas_call(
            functools.partial(update_kernel, start, stop),
            out_shape=[shape((stop - start, across), bf16)]
            + [shape((stop - start, across), f32)] * 3,
            in_specs=[whole()] * (ways + 4),
            out_specs=[whole()] * 4,
            scratch_shapes=[pltpu.VMEM((stop - start, across), f32)],
            compiler_params=params(),
            cost_estimate=cost(2 * ways * count * (stop - start) * across, high * across * 26),
            name="update",
        )(*rows[c], right, *state)
        fresh.append(out[0])
        news += out[1:]
    crossed = [over_dp(piece, top) for piece in fresh]

    part = (ways, flight, slots, across)
    bit = 1
    kept = [[d for d in range(pieces) if not d & bit], [d for d in range(pieces) if d & bit]]
    keep, send, own_fresh = pl.pallas_call(
        functools.partial(partial_kernel, spans, kept),
        out_shape=[
            shape((pieces // 2, *part), f32),
            shape((pieces // 2, *part), bf16),
            shape((high, across), bf16),
        ],
        in_specs=[whole()] * ((ways + 1) * len(spans) + 1),
        out_specs=[whole()] * 3,
        scratch_shapes=[pltpu.VMEM((ways, flight, pieces, slots, across), f32)],
        compiler_params=params(),
        cost_estimate=cost(2 * ways * count * high * across, high * across * 12),
        name="partial",
    )(*[block for chunk in rows for block in chunk], *fresh, state[0])
    arrived = over_dp(send, bit)
    while bit < top:
        bit *= 2
        left = kept[0]
        kept = [[d for d in left if not d & bit], [d for d in left if d & bit]]
        chosen = [[left.index(d) for d in half] for half in kept]
        keep, send = pl.pallas_call(
            functools.partial(halve_kernel, chosen),
            out_shape=[
                shape((len(kept[0]), *part), f32),
                shape((len(kept[1]), *part), bf16),
            ],
            in_specs=[whole()] * 2,
            out_specs=[whole()] * 2,
            compiler_params=params(),
            name="halve",
        )(keep, arrived)
        arrived = over_dp(send, bit)
    if len(spans) > 1:
        crossed[0], keep = lax.optimization_barrier((crossed[0], keep))
    d_gate, d_up = pl.pallas_call(
        gate_kernel,
        out_shape=[shape(gate_stash.shape, bf16)] * 2,
        in_specs=[whole()] * 4,
        out_specs=[whole()] * 2,
        compiler_params=params(),
        name="gates",
    )(gate_stash, up_stash, keep, arrived)

    states = pl.pallas_call(
        functools.partial(store_kernel, spans),
        out_shape=[shape((high, across), f32)] * 3,
        in_specs=[whole()] * len(news),
        out_specs=[hbm] * 3,
        scratch_shapes=[pltpu.SemaphoreType.DMA((len(spans), 3))],
        compiler_params=params(),
        cost_estimate=cost(0, high * across * 24),
        name="store",
    )(*news)

    def join(entries, before):
        return pl.pallas_call(
            functools.partial(join_kernel, high, [entry[:3] for entry in entries]),
            out_shape=shape((pieces * high, across), bf16),
            in_specs=[whole(pl.ANY)] * len(entries) + [hbm] * len(before),
            out_specs=hbm,
            input_output_aliases={len(entries): 0} if before else {},
            scratch_shapes=[pltpu.SemaphoreType.DMA((len(entries),))],
            compiler_params=params(),
            name="join",
        )(*[entry[3] for entry in entries], *before)

    near, *far = spread([(0, 0, high, own_fresh)], top // 2)
    early, late = [near], far
    for (start, stop), piece in zip(spans[:-1], crossed[:-1]):
        near, *far = spread([(top, start, stop, piece)], top // 2)
        early.append(near)
        late += far
    joined = join(early, [])
    crossed[-1], joined, states, arrived = lax.optimization_barrier(
        (crossed[-1], joined, states, arrived)
    )
    joined = join(late + spread([(top, *spans[-1], crossed[-1])], top // 2), [joined])
    return (d_gate, d_up, *states, joined)


def solution(mesh):
    placed = (
        P("dp", "expert", None, None),
        P("dp", "expert", None),
        P("dp", "expert"),
        P("dp", None, "expert"),
        P("dp", None, "expert"),
        P("dp", "expert"),
        P("dp", "expert"),
        P("dp", "expert"),
    )
    return jax.shard_map(
        local,
        mesh=mesh,
        in_specs=placed,
        out_specs=(
            P("dp", None, "expert"),
            P("dp", None, "expert"),
            P("dp", "expert"),
            P("dp", "expert"),
            P("dp", "expert"),
            P(None, "expert"),
        ),
        check_vma=False,
    )
```

```python
import functools

import jax
import jax.numpy as jnp
from jax import lax
from jax.experimental import pallas as pl
from jax.experimental.pallas import tpu as pltpu
from jax.sharding import PartitionSpec as P

learning_rate = 0.01
beta_one = 0.9
beta_two = 0.95
decay_rate = 0.1
epsilon = 1e-08

bf16 = jnp.bfloat16
f32 = jnp.float32
VMEM_LIMIT = 40 * 1024 * 1024
LANES = 128


def params():
    return pltpu.CompilerParams(vmem_limit_bytes=VMEM_LIMIT)


def cost(flops, nbytes):
    return pl.CostEstimate(flops=flops, bytes_accessed=nbytes, transcendentals=0)


def take(refs, count):
    taken = refs[:count]
    del refs[:count]
    return taken


def wide(tiles):
    return tiles[0] if len(tiles) == 1 else jnp.concatenate(tiles, axis=1)


def tall(blocks):
    return blocks[0] if len(blocks) == 1 else jnp.concatenate(blocks, axis=0)


def turns(ways):
    return [0, *range(ways - 1, 0, -1)]


def seat_of(ways):
    seat = lax.axis_index("expert")
    return lax.axis_index("dp"), lax.rem(seat, ways), lax.div(seat, ways)


def scale_kernel(counts_in, router_in, rows_in, gate_in, up_in, *refs):
    hidden, outs = refs[0], refs[1:-7]
    counts, router, rows, gate, up, cut, sems = refs[-7:]
    copies = [
        pltpu.make_async_copy(source, target, sems.at[n])
        for n, (source, target) in enumerate(
            [
                (gate_in, gate),
                (up_in, up),
                (counts_in, counts),
                (router_in, router),
                (rows_in, rows),
            ]
        )
    ]
    for copy in copies:
        copy.start()
    flight, slots, width = rows.shape[1:]
    pieces = cut.shape[0]
    piece = width // pieces
    ways = hidden.shape[0]
    me, _, own = seat_of(ways)
    copies[0].wait()
    copies[1].wait()
    g = gate[0].astype(f32)
    value = (g * jax.nn.sigmoid(g) * up[0].astype(f32)).astype(bf16)
    for f in range(flight):
        for v in range(ways):
            at = (f * ways + v) * slots
            hidden[v, f] = value[at : at + slots]
    for copy in copies[2:]:
        copy.wait()
    diagonal = lax.broadcasted_iota(jnp.int32, (slots, slots), 0) == lax.broadcasted_iota(
        jnp.int32, (slots, slots), 1
    )
    row = lax.broadcasted_iota(jnp.int32, (slots, 1), 0)
    for f in range(flight):
        weight = jnp.sum(
            jnp.where(diagonal, jnp.broadcast_to(router[0, f : f + 1, :], (slots, slots)), 0.0),
            axis=1,
            keepdims=True,
        )
        live = row < counts[0, f]
        scaled = jnp.where(live, weight * rows[0, f].astype(f32), 0.0).astype(bf16)
        for i in range(pieces):
            cut[i, f] = scaled[:, i * piece : (i + 1) * piece]
    for n, out in enumerate(outs):
        for dc in range(2):
            out[dc] = cut[me ^ (n % (pieces // 2) * 2 + dc), own ^ (n // (pieces // 2))]


def fetch_kernel(after, *refs):
    del after
    sems = refs[6]
    copies = [pltpu.make_async_copy(refs[n], refs[3 + n], sems.at[n]) for n in range(3)]
    for copy in copies:
        copy.start()
    for copy in copies:
        copy.wait()


def share_kernel(order, *refs):
    for n, block in zip(order, refs):
        refs[-1][n] = block[1]


def pack_kernel(spans, other, *refs):
    blocks, outs = refs[: -len(spans)], refs[-len(spans) :]
    for (start, stop), out in zip(spans, outs):
        for n, block in enumerate(blocks):
            out[2 * n] = block[0, :, start:stop]
            out[2 * n + 1] = other[n, :, start:stop]


def order_kernel(*refs):
    hiddens, right = refs[:-1], refs[-1]
    ways, flight = right.shape[:2]
    _, lane, own = seat_of(ways)
    for dj, hidden in enumerate(hiddens):
        for n, d in enumerate(turns(ways)):
            for dg in range(flight):
                right[n, dg, dj] = hidden[lane ^ d, own ^ dg]


def update_kernel(start, stop, *refs):
    refs = list(refs)
    rows = refs[:-9]
    right, master, first, second, fresh, new_master, new_first, new_second, gradient = refs[-9:]
    hidden = right[...].reshape(-1, right.shape[-1])
    left = tall([block[...].reshape(-1, stop - start) for block in rows])
    gradient[...] = lax.dot_general(
        left, hidden, (((0,), (0,)), ((), ())), preferred_element_type=f32
    )
    for low in range(start, stop, 128):
        end = min(low + 128, stop)
        here = pl.ds(low, end - low)
        there = pl.ds(low - start, end - low)
        grad = gradient[there]
        old = master[here]
        moment_a = beta_one * first[here] + (1.0 - beta_one) * grad
        moment_b = beta_two * second[here] + (1.0 - beta_two) * grad * grad
        step_size = (moment_a * (1.0 / (1.0 - beta_one**5))) / (
            jnp.sqrt(moment_b * (1.0 / (1.0 - beta_two**5))) + epsilon
        )
        updated = old - learning_rate * (step_size + decay_rate * old)
        fresh[there] = updated.astype(bf16)
        new_master[there] = updated
        new_first[there] = moment_a
        new_second[there] = moment_b


def partial_kernel(spans, kept, *refs):
    refs = list(refs)
    chunks = len(spans)
    keep, send, own_fresh, held = refs[-4:]
    ways = held.shape[0]
    rows, fresh, (master,) = take(refs, ways * chunks), take(refs, chunks), take(refs, 1)
    flight = held.shape[1]
    _, lane, own = seat_of(ways)
    left = wide(
        [
            tall([block[...].reshape(-1, stop - start) for block in rows[c * ways : (c + 1) * ways]])
            for c, (start, stop) in enumerate(spans)
        ]
    )
    share = jnp.dot(left, master[...].astype(bf16), preferred_element_type=f32)
    held[...] = share.reshape(held.shape)
    for out, chosen in ((keep, kept[0]), (send, kept[1])):
        for n, dj in enumerate(chosen):
            for at, d in enumerate(turns(ways)):
                for dg in range(flight):
                    out[n, lane ^ d, own ^ dg] = held[at, dg, dj].astype(out.dtype)
    for c, (start, stop) in enumerate(spans):
        own_fresh[start:stop] = fresh[c][...]


def halve_kernel(kept, held, arrived, keep, send):
    for out, chosen in ((keep, kept[0]), (send, kept[1])):
        for n, m in enumerate(chosen):
            out[n] = (held[m] + arrived[m].astype(f32)).astype(out.dtype)


def store_kernel(spans, *refs):
    refs = list(refs)
    news = take(refs, 3 * len(spans))
    outs = take(refs, 3)
    (sems,) = refs
    copies = []
    for c, (start, stop) in enumerate(spans):
        for n in range(3):
            copy = pltpu.make_async_copy(
                news[3 * c + n], outs[n].at[pl.ds(start, stop - start)], sems.at[c, n]
            )
            copy.start()
            copies.append(copy)
    for copy in copies:
        copy.wait()


def gate_kernel(gate, up, held, arrived, d_gate, d_up):
    ways, flight, slots = held.shape[1:4]
    for f in range(flight):
        for v in range(ways):
            at = pl.ds((f * ways + v) * slots, slots)
            grad = held[0, v, f] + arrived[0, v, f].astype(f32)
            g = gate[0, at].astype(f32)
            u = up[0, at].astype(f32)
            sig = jax.nn.sigmoid(g)
            d_gate[0, at] = (grad * u * sig * (1.0 + g * (1.0 - sig))).astype(bf16)
            d_up[0, at] = (grad * (g * sig)).astype(bf16)


def join_kernel(high, entries, *refs):
    out, sems = refs[-2], refs[-1]
    me = lax.axis_index("dp")
    copies = []
    for n, (d, start, stop) in enumerate(entries):
        at = pl.multiple_of((me ^ d) * high + start, 16)
        copy = pltpu.make_async_copy(refs[n], out.at[pl.ds(at, stop - start)], sems.at[n])
        copy.start()
        copies.append(copy)
    for copy in copies:
        copy.wait()


def whole(memory=pltpu.VMEM):
    return pl.BlockSpec(memory_space=memory)


def shape(dims, kind):
    return jax.ShapeDtypeStruct(dims, kind)


def pinned(x):
    return pltpu.with_memory_space_constraint(x, pltpu.HBM)


def local(
    grad_rows,
    router_weight,
    send_counts,
    gate_stash,
    up_stash,
    master_weight,
    first_moment,
    second_moment,
):
    _, flight, slots, width = grad_rows.shape
    pieces = lax.axis_size("dp")
    sources = lax.axis_size("expert")
    ways = sources // flight
    high, across = master_weight.shape
    hbm = whole(pltpu.HBM)
    count = pieces * flight * slots

    def over_dp(x, d):
        return lax.ppermute(x, "dp", [(i, i ^ d) for i in range(pieces)])

    tiles = -(-high // LANES)
    middle = (tiles + 1) // 2 * LANES
    spans = [(0, middle), (middle, high)] if middle < high else [(0, high)]
    offsets = [(dj, dg) for dg in range(flight) for dj in range(0, pieces, 2)]
    results = pl.pallas_call(
        scale_kernel,
        out_shape=[shape((ways, flight, slots, across), bf16)]
        + [shape((2, slots, high), bf16)] * len(offsets),
        in_specs=[hbm] * 5,
        out_specs=[whole()] * (1 + len(offsets)),
        scratch_shapes=[
            pltpu.SMEM(send_counts.shape, jnp.int32),
            pltpu.VMEM(router_weight.shape, f32),
            pltpu.VMEM(grad_rows.shape, bf16),
            pltpu.VMEM(gate_stash.shape, bf16),
            pltpu.VMEM(up_stash.shape, bf16),
            pltpu.VMEM((pieces, flight, slots, high), bf16),
            pltpu.SemaphoreType.DMA((5,)),
        ],
        compiler_params=params(),
        name="scale",
    )(
        pinned(send_counts),
        pinned(router_weight),
        pinned(grad_rows),
        pinned(gate_stash),
        pinned(up_stash),
    )
    hidden, blocks = results[0], list(results[1:])
    for n, (dj, dg) in reversed(list(enumerate(offsets))):
        if n:
            pairs = [
                (i * sources + k, (i ^ dj) * sources + (k ^ (dg * ways)))
                for i in range(pieces)
                for k in range(sources)
            ]
            blocks[n] = lax.ppermute(blocks[n], ("dp", "expert"), pairs)
    state = pl.pallas_call(
        fetch_kernel,
        out_shape=[shape((high, across), f32)] * 3,
        in_specs=[whole(pl.ANY)] + [hbm] * 3,
        out_specs=[whole()] * 3,
        scratch_shapes=[pltpu.SemaphoreType.DMA((3,))],
        compiler_params=params(),
        cost_estimate=cost(0, high * across * 24),
        name="fetch",
    )(hidden, pinned(master_weight), pinned(first_moment), pinned(second_moment))
    order = [*range(pieces // 2, len(offsets)), *range(1, pieces // 2), 0]
    other = pl.pallas_call(
        functools.partial(share_kernel, order),
        out_shape=shape((len(offsets), slots, high), bf16),
        in_specs=[whole()] * len(offsets),
        out_specs=whole(),
        compiler_params=params(),
        name="share",
    )(*[blocks[n] for n in order])
    mine = pl.pallas_call(
        functools.partial(pack_kernel, spans),
        out_shape=[shape((2 * len(offsets), slots, stop - start), bf16) for start, stop in spans],
        in_specs=[whole()] * (1 + len(offsets)),
        out_specs=[whole()] * len(spans),
        compiler_params=params(),
        name="pack",
    )(over_dp(other, 1), *blocks)
    top = pieces // 2

    def spread(entries, first):
        step = first
        while step:
            entries = entries + [(d ^ step, *span, over_dp(x, step)) for d, *span, x in entries]
            step //= 2
        return entries

    hiddens = [entry[1] for entry in sorted(spread([(0, hidden)], top), key=lambda e: e[0])]
    right = pl.pallas_call(
        order_kernel,
        out_shape=shape((ways, flight, pieces, slots, across), bf16),
        in_specs=[whole()] * pieces,
        out_specs=whole(),
        compiler_params=params(),
        name="order",
    )(*hiddens)
    rows = []
    for c, piece in enumerate(mine):
        if c:
            piece, _ = lax.optimization_barrier((piece, state))
        rows.append(
            [piece]
            + [
                lax.ppermute(piece, "expert", [(k, k ^ d) for k in range(sources)])
                for d in turns(ways)[1:]
            ]
        )

    fresh, news = [], []
    for c, (start, stop) in enumerate(spans):
        out = pl.pallas_call(
            functools.partial(update_kernel, start, stop),
            out_shape=[shape((stop - start, across), bf16)]
            + [shape((stop - start, across), f32)] * 3,
            in_specs=[whole()] * (ways + 4),
            out_specs=[whole()] * 4,
            scratch_shapes=[pltpu.VMEM((stop - start, across), f32)],
            compiler_params=params(),
            cost_estimate=cost(2 * ways * count * (stop - start) * across, high * across * 26),
            name="update",
        )(*rows[c], right, *state)
        fresh.append(out[0])
        news += out[1:]
    crossed = [over_dp(piece, top) for piece in fresh]

    part = (ways, flight, slots, across)
    bit = 1
    kept = [[d for d in range(pieces) if not d & bit], [d for d in range(pieces) if d & bit]]
    keep, send, own_fresh = pl.pallas_call(
        functools.partial(partial_kernel, spans, kept),
        out_shape=[
            shape((pieces // 2, *part), f32),
            shape((pieces // 2, *part), bf16),
            shape((high, across), bf16),
        ],
        in_specs=[whole()] * ((ways + 1) * len(spans) + 1),
        out_specs=[whole()] * 3,
        scratch_shapes=[pltpu.VMEM((ways, flight, pieces, slots, across), f32)],
        compiler_params=params(),
        cost_estimate=cost(2 * ways * count * high * across, high * across * 12),
        name="partial",
    )(*[block for chunk in rows for block in chunk], *fresh, state[0])
    arrived = over_dp(send, bit)
    while bit < top:
        bit *= 2
        left = kept[0]
        kept = [[d for d in left if not d & bit], [d for d in left if d & bit]]
        chosen = [[left.index(d) for d in half] for half in kept]
        keep, send = pl.pallas_call(
            functools.partial(halve_kernel, chosen),
            out_shape=[
                shape((len(kept[0]), *part), f32),
                shape((len(kept[1]), *part), bf16),
            ],
            in_specs=[whole()] * 2,
            out_specs=[whole()] * 2,
            compiler_params=params(),
            name="halve",
        )(keep, arrived)
        arrived = over_dp(send, bit)
    if len(spans) > 1:
        crossed[0], keep = lax.optimization_barrier((crossed[0], keep))
    d_gate, d_up = pl.pallas_call(
        gate_kernel,
        out_shape=[shape(gate_stash.shape, bf16)] * 2,
        in_specs=[whole()] * 4,
        out_specs=[whole()] * 2,
        compiler_params=params(),
        name="gates",
    )(gate_stash, up_stash, keep, arrived)

    states = pl.pallas_call(
        functools.partial(store_kernel, spans),
        out_shape=[shape((high, across), f32)] * 3,
        in_specs=[whole()] * len(news),
        out_specs=[hbm] * 3,
        scratch_shapes=[pltpu.SemaphoreType.DMA((len(spans), 3))],
        compiler_params=params(),
        cost_estimate=cost(0, high * across * 24),
        name="store",
    )(*news)

    def join(entries, before):
        return pl.pallas_call(
            functools.partial(join_kernel, high, [entry[:3] for entry in entries]),
            out_shape=shape((pieces * high, across), bf16),
            in_specs=[whole(pl.ANY)] * len(entries) + [hbm] * len(before),
            out_specs=hbm,
            input_output_aliases={len(entries): 0} if before else {},
            scratch_shapes=[pltpu.SemaphoreType.DMA((len(entries),))],
            compiler_params=params(),
            name="join",
        )(*[entry[3] for entry in entries], *before)

    near, *far = spread([(0, 0, high, own_fresh)], top // 2)
    early, late = [near], far
    for (start, stop), piece in zip(spans[:-1], crossed[:-1]):
        near, *far = spread([(top, start, stop, piece)], top // 2)
        early.append(near)
        late += far
    joined = join(early, [])
    crossed[-1], joined, states, arrived = lax.optimization_barrier(
        (crossed[-1], joined, states, arrived)
    )
    joined = join(late + spread([(top, *spans[-1], crossed[-1])], top // 2), [joined])
    return (d_gate, d_up, *states, joined)


def solution(mesh):
    placed = (
        P("dp", "expert", None, None),
        P("dp", "expert", None),
        P("dp", "expert"),
        P("dp", None, "expert"),
        P("dp", None, "expert"),
        P("dp", "expert"),
        P("dp", "expert"),
        P("dp", "expert"),
    )
    return jax.shard_map(
        local,
        mesh=mesh,
        in_specs=placed,
        out_specs=(
            P("dp", None, "expert"),
            P("dp", None, "expert"),
            P("dp", "expert"),
            P("dp", "expert"),
            P("dp", "expert"),
            P(None, "expert"),
        ),
        check_vma=False,
    )
```

```python
import functools

import jax
import jax.numpy as jnp
from jax import lax
from jax.experimental import pallas as pl
from jax.experimental.pallas import tpu as pltpu
from jax.sharding import PartitionSpec as P

learning_rate = 0.01
beta_one = 0.9
beta_two = 0.95
decay_rate = 0.1
epsilon = 1e-08

bf16 = jnp.bfloat16
f32 = jnp.float32
VMEM_LIMIT = 40 * 1024 * 1024
LANES = 128


def params():
    return pltpu.CompilerParams(vmem_limit_bytes=VMEM_LIMIT)


def cost(flops, nbytes):
    return pl.CostEstimate(flops=flops, bytes_accessed=nbytes, transcendentals=0)


def take(refs, count):
    taken = refs[:count]
    del refs[:count]
    return taken


def wide(tiles):
    return tiles[0] if len(tiles) == 1 else jnp.concatenate(tiles, axis=1)


def tall(blocks):
    return blocks[0] if len(blocks) == 1 else jnp.concatenate(blocks, axis=0)


def turns(ways):
    return [0, *range(ways - 1, 0, -1)]


def seat_of(ways):
    seat = lax.axis_index("expert")
    return lax.axis_index("dp"), lax.rem(seat, ways), lax.div(seat, ways)


def scale_kernel(counts_in, router_in, rows_in, gate_in, up_in, *refs):
    hidden, outs = refs[0], refs[1:-7]
    counts, router, rows, gate, up, cut, sems = refs[-7:]
    copies = [
        pltpu.make_async_copy(source, target, sems.at[n])
        for n, (source, target) in enumerate(
            [
                (gate_in, gate),
                (up_in, up),
                (counts_in, counts),
                (router_in, router),
                (rows_in, rows),
            ]
        )
    ]
    for copy in copies:
        copy.start()
    flight, slots, width = rows.shape[1:]
    pieces = cut.shape[0]
    piece = width // pieces
    ways = hidden.shape[0]
    me, _, own = seat_of(ways)
    copies[0].wait()
    copies[1].wait()
    g = gate[0].astype(f32)
    value = (g * jax.nn.sigmoid(g) * up[0].astype(f32)).astype(bf16)
    for f in range(flight):
        for v in range(ways):
            at = (f * ways + v) * slots
            hidden[v, f] = value[at : at + slots]
    for copy in copies[2:]:
        copy.wait()
    diagonal = lax.broadcasted_iota(jnp.int32, (slots, slots), 0) == lax.broadcasted_iota(
        jnp.int32, (slots, slots), 1
    )
    row = lax.broadcasted_iota(jnp.int32, (slots, 1), 0)
    for f in range(flight):
        weight = jnp.sum(
            jnp.where(diagonal, jnp.broadcast_to(router[0, f : f + 1, :], (slots, slots)), 0.0),
            axis=1,
            keepdims=True,
        )
        live = row < counts[0, f]
        scaled = jnp.where(live, weight * rows[0, f].astype(f32), 0.0).astype(bf16)
        for i in range(pieces):
            cut[i, f] = scaled[:, i * piece : (i + 1) * piece]
    for n, out in enumerate(outs):
        for dc in range(2):
            out[dc] = cut[me ^ (n % (pieces // 2) * 2 + dc), own ^ (n // (pieces // 2))]


def fetch_kernel(after, *refs):
    del after
    sems = refs[6]
    copies = [pltpu.make_async_copy(refs[n], refs[3 + n], sems.at[n]) for n in range(3)]
    for copy in copies:
        copy.start()
    for copy in copies:
        copy.wait()


def share_kernel(order, *refs):
    for n, block in zip(order, refs):
        refs[-1][n] = block[1]


def pack_kernel(spans, other, *refs):
    blocks, outs = refs[: -len(spans)], refs[-len(spans) :]
    for (start, stop), out in zip(spans, outs):
        for n, block in enumerate(blocks):
            out[2 * n] = block[0, :, start:stop]
            out[2 * n + 1] = other[n, :, start:stop]


def order_kernel(*refs):
    hiddens, right = refs[:-1], refs[-1]
    ways, flight = right.shape[:2]
    _, lane, own = seat_of(ways)
    for dj, hidden in enumerate(hiddens):
        for n, d in enumerate(turns(ways)):
            for dg in range(flight):
                right[n, dg, dj] = hidden[lane ^ d, own ^ dg]


def update_kernel(start, stop, *refs):
    refs = list(refs)
    rows = refs[:-9]
    right, master, first, second, fresh, new_master, new_first, new_second, gradient = refs[-9:]
    hidden = right[...].reshape(-1, right.shape[-1])
    left = tall([block[...].reshape(-1, stop - start) for block in rows])
    gradient[...] = lax.dot_general(
        left, hidden, (((0,), (0,)), ((), ())), preferred_element_type=f32
    )
    for low in range(start, stop, 128):
        end = min(low + 128, stop)
        here = pl.ds(low, end - low)
        there = pl.ds(low - start, end - low)
        grad = gradient[there]
        old = master[here]
        moment_a = beta_one * first[here] + (1.0 - beta_one) * grad
        moment_b = beta_two * second[here] + (1.0 - beta_two) * grad * grad
        step_size = (moment_a * (1.0 / (1.0 - beta_one**5))) / (
            jnp.sqrt(moment_b * (1.0 / (1.0 - beta_two**5))) + epsilon
        )
        updated = old - learning_rate * (step_size + decay_rate * old)
        fresh[there] = updated.astype(bf16)
        new_master[there] = updated
        new_first[there] = moment_a
        new_second[there] = moment_b


def partial_kernel(spans, kept, *refs):
    refs = list(refs)
    chunks = len(spans)
    keep, send, own_fresh, held = refs[-4:]
    ways = held.shape[0]
    rows, fresh, (master,) = take(refs, ways * chunks), take(refs, chunks), take(refs, 1)
    flight = held.shape[1]
    _, lane, own = seat_of(ways)
    left = wide(
        [
            tall([block[...].reshape(-1, stop - start) for block in rows[c * ways : (c + 1) * ways]])
            for c, (start, stop) in enumerate(spans)
        ]
    )
    share = jnp.dot(left, master[...].astype(bf16), preferred_element_type=f32)
    held[...] = share.reshape(held.shape)
    for out, chosen in ((keep, kept[0]), (send, kept[1])):
        for n, dj in enumerate(chosen):
            for at, d in enumerate(turns(ways)):
                for dg in range(flight):
                    out[n, lane ^ d, own ^ dg] = held[at, dg, dj].astype(out.dtype)
    for c, (start, stop) in enumerate(spans):
        own_fresh[start:stop] = fresh[c][...]


def halve_kernel(kept, held, arrived, keep, send):
    for out, chosen in ((keep, kept[0]), (send, kept[1])):
        for n, m in enumerate(chosen):
            out[n] = (held[m] + arrived[m].astype(f32)).astype(out.dtype)


def store_kernel(spans, *refs):
    refs = list(refs)
    news = take(refs, 3 * len(spans))
    outs = take(refs, 3)
    (sems,) = refs
    copies = []
    for c, (start, stop) in enumerate(spans):
        for n in range(3):
            copy = pltpu.make_async_copy(
                news[3 * c + n], outs[n].at[pl.ds(start, stop - start)], sems.at[c, n]
            )
            copy.start()
            copies.append(copy)
    for copy in copies:
        copy.wait()


def gate_kernel(gate, up, held, arrived, d_gate, d_up):
    ways, flight, slots = held.shape[1:4]
    for f in range(flight):
        for v in range(ways):
            at = pl.ds((f * ways + v) * slots, slots)
            grad = held[0, v, f] + arrived[0, v, f].astype(f32)
            g = gate[0, at].astype(f32)
            u = up[0, at].astype(f32)
            sig = jax.nn.sigmoid(g)
            d_gate[0, at] = (grad * u * sig * (1.0 + g * (1.0 - sig))).astype(bf16)
            d_up[0, at] = (grad * (g * sig)).astype(bf16)


def join_kernel(high, entries, *refs):
    out, sems = refs[-2], refs[-1]
    me = lax.axis_index("dp")
    copies = []
    for n, (d, start, stop) in enumerate(entries):
        at = pl.multiple_of((me ^ d) * high + start, 16)
        copy = pltpu.make_async_copy(refs[n], out.at[pl.ds(at, stop - start)], sems.at[n])
        copy.start()
        copies.append(copy)
    for copy in copies:
        copy.wait()


def whole(memory=pltpu.VMEM):
    return pl.BlockSpec(memory_space=memory)


def shape(dims, kind):
    return jax.ShapeDtypeStruct(dims, kind)


def pinned(x):
    return pltpu.with_memory_space_constraint(x, pltpu.HBM)


def local(
    grad_rows,
    router_weight,
    send_counts,
    gate_stash,
    up_stash,
    master_weight,
    first_moment,
    second_moment,
):
    _, flight, slots, width = grad_rows.shape
    pieces = lax.axis_size("dp")
    sources = lax.axis_size("expert")
    ways = sources // flight
    high, across = master_weight.shape
    hbm = whole(pltpu.HBM)
    count = pieces * flight * slots

    def over_dp(x, d):
        return lax.ppermute(x, "dp", [(i, i ^ d) for i in range(pieces)])

    tiles = -(-high // LANES)
    middle = (tiles + 1) // 2 * LANES
    spans = [(0, middle), (middle, high)] if middle < high else [(0, high)]
    offsets = [(dj, dg) for dg in range(flight) for dj in range(0, pieces, 2)]
    results = pl.pallas_call(
        scale_kernel,
        out_shape=[shape((ways, flight, slots, across), bf16)]
        + [shape((2, slots, high), bf16)] * len(offsets),
        in_specs=[hbm] * 5,
        out_specs=[whole()] * (1 + len(offsets)),
        scratch_shapes=[
            pltpu.SMEM(send_counts.shape, jnp.int32),
            pltpu.VMEM(router_weight.shape, f32),
            pltpu.VMEM(grad_rows.shape, bf16),
            pltpu.VMEM(gate_stash.shape, bf16),
            pltpu.VMEM(up_stash.shape, bf16),
            pltpu.VMEM((pieces, flight, slots, high), bf16),
            pltpu.SemaphoreType.DMA((5,)),
        ],
        compiler_params=params(),
        name="scale",
    )(
        pinned(send_counts),
        pinned(router_weight),
        pinned(grad_rows),
        pinned(gate_stash),
        pinned(up_stash),
    )
    hidden, blocks = results[0], list(results[1:])
    for n, (dj, dg) in reversed(list(enumerate(offsets))):
        if n:
            pairs = [
                (i * sources + k, (i ^ dj) * sources + (k ^ (dg * ways)))
                for i in range(pieces)
                for k in range(sources)
            ]
            blocks[n] = lax.ppermute(blocks[n], ("dp", "expert"), pairs)
    state = pl.pallas_call(
        fetch_kernel,
        out_shape=[shape((high, across), f32)] * 3,
        in_specs=[whole(pl.ANY)] + [hbm] * 3,
        out_specs=[whole()] * 3,
        scratch_shapes=[pltpu.SemaphoreType.DMA((3,))],
        compiler_params=params(),
        cost_estimate=cost(0, high * across * 24),
        name="fetch",
    )(hidden, pinned(master_weight), pinned(first_moment), pinned(second_moment))
    first, *far = range(pieces // 2, len(offsets))
    order = [first, *range(1, pieces // 2), *far, 0]
    other = pl.pallas_call(
        functools.partial(share_kernel, order),
        out_shape=shape((len(offsets), slots, high), bf16),
        in_specs=[whole()] * len(offsets),
        out_specs=whole(),
        compiler_params=params(),
        name="share",
    )(*[blocks[n] for n in order])
    mine = pl.pallas_call(
        functools.partial(pack_kernel, spans),
        out_shape=[shape((2 * len(offsets), slots, stop - start), bf16) for start, stop in spans],
        in_specs=[whole()] * (1 + len(offsets)),
        out_specs=[whole()] * len(spans),
        compiler_params=params(),
        name="pack",
    )(over_dp(other, 1), *blocks)
    top = pieces // 2

    def spread(entries, first):
        step = first
        while step:
            entries = entries + [(d ^ step, *span, over_dp(x, step)) for d, *span, x in entries]
            step //= 2
        return entries

    hiddens = [entry[1] for entry in sorted(spread([(0, hidden)], top), key=lambda e: e[0])]
    right = pl.pallas_call(
        order_kernel,
        out_shape=shape((ways, flight, pieces, slots, across), bf16),
        in_specs=[whole()] * pieces,
        out_specs=whole(),
        compiler_params=params(),
        name="order",
    )(*hiddens)
    rows = []
    for c, piece in enumerate(mine):
        if c:
            piece, _ = lax.optimization_barrier((piece, state))
        rows.append(
            [piece]
            + [
                lax.ppermute(piece, "expert", [(k, k ^ d) for k in range(sources)])
                for d in turns(ways)[1:]
            ]
        )

    fresh, news = [], []
    for c, (start, stop) in enumerate(spans):
        out = pl.pallas_call(
            functools.partial(update_kernel, start, stop),
            out_shape=[shape((stop - start, across), bf16)]
            + [shape((stop - start, across), f32)] * 3,
            in_specs=[whole()] * (ways + 4),
            out_specs=[whole()] * 4,
            scratch_shapes=[pltpu.VMEM((stop - start, across), f32)],
            compiler_params=params(),
            cost_estimate=cost(2 * ways * count * (stop - start) * across, high * across * 26),
            name="update",
        )(*rows[c], right, *state)
        fresh.append(out[0])
        news += out[1:]
    crossed = [over_dp(piece, top) for piece in fresh]

    part = (ways, flight, slots, across)
    bit = 1
    kept = [[d for d in range(pieces) if not d & bit], [d for d in range(pieces) if d & bit]]
    keep, send, own_fresh = pl.pallas_call(
        functools.partial(partial_kernel, spans, kept),
        out_shape=[
            shape((pieces // 2, *part), f32),
            shape((pieces // 2, *part), bf16),
            shape((high, across), bf16),
        ],
        in_specs=[whole()] * ((ways + 1) * len(spans) + 1),
        out_specs=[whole()] * 3,
        scratch_shapes=[pltpu.VMEM((ways, flight, pieces, slots, across), f32)],
        compiler_params=params(),
        cost_estimate=cost(2 * ways * count * high * across, high * across * 12),
        name="partial",
    )(*[block for chunk in rows for block in chunk], *fresh, state[0])
    arrived = over_dp(send, bit)
    while bit < top:
        bit *= 2
        left = kept[0]
        kept = [[d for d in left if not d & bit], [d for d in left if d & bit]]
        chosen = [[left.index(d) for d in half] for half in kept]
        keep, send = pl.pallas_call(
            functools.partial(halve_kernel, chosen),
            out_shape=[
                shape((len(kept[0]), *part), f32),
                shape((len(kept[1]), *part), bf16),
            ],
            in_specs=[whole()] * 2,
            out_specs=[whole()] * 2,
            compiler_params=params(),
            name="halve",
        )(keep, arrived)
        arrived = over_dp(send, bit)
    if len(spans) > 1:
        crossed[0], keep = lax.optimization_barrier((crossed[0], keep))
    d_gate, d_up = pl.pallas_call(
        gate_kernel,
        out_shape=[shape(gate_stash.shape, bf16)] * 2,
        in_specs=[whole()] * 4,
        out_specs=[whole()] * 2,
        compiler_params=params(),
        name="gates",
    )(gate_stash, up_stash, keep, arrived)

    states = pl.pallas_call(
        functools.partial(store_kernel, spans),
        out_shape=[shape((high, across), f32)] * 3,
        in_specs=[whole()] * len(news),
        out_specs=[hbm] * 3,
        scratch_shapes=[pltpu.SemaphoreType.DMA((len(spans), 3))],
        compiler_params=params(),
        cost_estimate=cost(0, high * across * 24),
        name="store",
    )(*news)

    def join(entries, before):
        return pl.pallas_call(
            functools.partial(join_kernel, high, [entry[:3] for entry in entries]),
            out_shape=shape((pieces * high, across), bf16),
            in_specs=[whole(pl.ANY)] * len(entries) + [hbm] * len(before),
            out_specs=hbm,
            input_output_aliases={len(entries): 0} if before else {},
            scratch_shapes=[pltpu.SemaphoreType.DMA((len(entries),))],
            compiler_params=params(),
            name="join",
        )(*[entry[3] for entry in entries], *before)

    near, *far = spread([(0, 0, high, own_fresh)], top // 2)
    early, late = [near], far
    for (start, stop), piece in zip(spans[:-1], crossed[:-1]):
        near, *far = spread([(top, start, stop, piece)], top // 2)
        early.append(near)
        late += far
    joined = join(early, [])
    crossed[-1], joined, states, arrived = lax.optimization_barrier(
        (crossed[-1], joined, states, arrived)
    )
    joined = join(late + spread([(top, *spans[-1], crossed[-1])], top // 2), [joined])
    return (d_gate, d_up, *states, joined)


def solution(mesh):
    placed = (
        P("dp", "expert", None, None),
        P("dp", "expert", None),
        P("dp", "expert"),
        P("dp", None, "expert"),
        P("dp", None, "expert"),
        P("dp", "expert"),
        P("dp", "expert"),
        P("dp", "expert"),
    )
    return jax.shard_map(
        local,
        mesh=mesh,
        in_specs=placed,
        out_specs=(
            P("dp", None, "expert"),
            P("dp", None, "expert"),
            P("dp", "expert"),
            P("dp", "expert"),
            P("dp", "expert"),
            P(None, "expert"),
        ),
        check_vma=False,
    )
```

```python
import functools

import jax
import jax.numpy as jnp
from jax import lax
from jax.experimental import pallas as pl
from jax.experimental.pallas import tpu as pltpu
from jax.sharding import PartitionSpec as P

learning_rate = 0.01
beta_one = 0.9
beta_two = 0.95
decay_rate = 0.1
epsilon = 1e-08

bf16 = jnp.bfloat16
f32 = jnp.float32
VMEM_LIMIT = 40 * 1024 * 1024
LANES = 128


def params():
    return pltpu.CompilerParams(vmem_limit_bytes=VMEM_LIMIT)


def cost(flops, nbytes):
    return pl.CostEstimate(flops=flops, bytes_accessed=nbytes, transcendentals=0)


def take(refs, count):
    taken = refs[:count]
    del refs[:count]
    return taken


def wide(tiles):
    return tiles[0] if len(tiles) == 1 else jnp.concatenate(tiles, axis=1)


def tall(blocks):
    return blocks[0] if len(blocks) == 1 else jnp.concatenate(blocks, axis=0)


def turns(ways):
    return [0, *range(ways - 1, 0, -1)]


def seat_of(ways):
    seat = lax.axis_index("expert")
    return lax.axis_index("dp"), lax.rem(seat, ways), lax.div(seat, ways)


def scale_kernel(counts_in, router_in, rows_in, gate_in, up_in, *refs):
    hidden, outs = refs[0], refs[1:-7]
    counts, router, rows, gate, up, cut, sems = refs[-7:]
    copies = [
        pltpu.make_async_copy(source, target, sems.at[n])
        for n, (source, target) in enumerate(
            [
                (gate_in, gate),
                (up_in, up),
                (counts_in, counts),
                (router_in, router),
                (rows_in, rows),
            ]
        )
    ]
    for copy in copies:
        copy.start()
    flight, slots, width = rows.shape[1:]
    pieces = cut.shape[0]
    piece = width // pieces
    ways = hidden.shape[0]
    me, _, own = seat_of(ways)
    copies[0].wait()
    copies[1].wait()
    g = gate[0].astype(f32)
    value = (g * jax.nn.sigmoid(g) * up[0].astype(f32)).astype(bf16)
    for f in range(flight):
        for v in range(ways):
            at = (f * ways + v) * slots
            hidden[v, f] = value[at : at + slots]
    for copy in copies[2:]:
        copy.wait()
    diagonal = lax.broadcasted_iota(jnp.int32, (slots, slots), 0) == lax.broadcasted_iota(
        jnp.int32, (slots, slots), 1
    )
    row = lax.broadcasted_iota(jnp.int32, (slots, 1), 0)
    for f in range(flight):
        weight = jnp.sum(
            jnp.where(diagonal, jnp.broadcast_to(router[0, f : f + 1, :], (slots, slots)), 0.0),
            axis=1,
            keepdims=True,
        )
        live = row < counts[0, f]
        scaled = jnp.where(live, weight * rows[0, f].astype(f32), 0.0).astype(bf16)
        for i in range(pieces):
            cut[i, f] = scaled[:, i * piece : (i + 1) * piece]
    for n, out in enumerate(outs):
        for dc in range(2):
            out[dc] = cut[me ^ (n % (pieces // 2) * 2 + dc), own ^ (n // (pieces // 2))]


def fetch_kernel(after, *refs):
    del after
    sems = refs[6]
    copies = [pltpu.make_async_copy(refs[n], refs[3 + n], sems.at[n]) for n in range(3)]
    for copy in copies:
        copy.start()
    for copy in copies:
        copy.wait()


def share_kernel(order, *refs):
    for n, block in zip(order, refs):
        refs[-1][n] = block[1]


def pack_kernel(spans, other, *refs):
    blocks, outs = refs[: -len(spans)], refs[-len(spans) :]
    for (start, stop), out in zip(spans, outs):
        for n, block in enumerate(blocks):
            out[2 * n] = block[0, :, start:stop]
            out[2 * n + 1] = other[n, :, start:stop]


def order_kernel(*refs):
    hiddens, right = refs[:-1], refs[-1]
    ways, flight = right.shape[:2]
    _, lane, own = seat_of(ways)
    for dj, hidden in enumerate(hiddens):
        for n, d in enumerate(turns(ways)):
            for dg in range(flight):
                right[n, dg, dj] = hidden[lane ^ d, own ^ dg]


def update_kernel(start, stop, *refs):
    refs = list(refs)
    rows = refs[:-9]
    right, master, first, second, fresh, new_master, new_first, new_second, gradient = refs[-9:]
    hidden = right[...].reshape(-1, right.shape[-1])
    left = tall([block[...].reshape(-1, stop - start) for block in rows])
    gradient[...] = lax.dot_general(
        left, hidden, (((0,), (0,)), ((), ())), preferred_element_type=f32
    )
    for low in range(start, stop, 128):
        end = min(low + 128, stop)
        here = pl.ds(low, end - low)
        there = pl.ds(low - start, end - low)
        grad = gradient[there]
        old = master[here]
        moment_a = beta_one * first[here] + (1.0 - beta_one) * grad
        moment_b = beta_two * second[here] + (1.0 - beta_two) * grad * grad
        step_size = (moment_a * (1.0 / (1.0 - beta_one**5))) / (
            jnp.sqrt(moment_b * (1.0 / (1.0 - beta_two**5))) + epsilon
        )
        updated = old - learning_rate * (step_size + decay_rate * old)
        fresh[there] = updated.astype(bf16)
        new_master[there] = updated
        new_first[there] = moment_a
        new_second[there] = moment_b


def partial_kernel(spans, kept, *refs):
    refs = list(refs)
    chunks = len(spans)
    keep, send, own_fresh, held = refs[-4:]
    ways = held.shape[0]
    rows, fresh, (master,) = take(refs, ways * chunks), take(refs, chunks), take(refs, 1)
    flight = held.shape[1]
    _, lane, own = seat_of(ways)
    left = wide(
        [
            tall([block[...].reshape(-1, stop - start) for block in rows[c * ways : (c + 1) * ways]])
            for c, (start, stop) in enumerate(spans)
        ]
    )
    share = jnp.dot(left, master[...].astype(bf16), preferred_element_type=f32)
    held[...] = share.reshape(held.shape)
    for out, chosen in ((keep, kept[0]), (send, kept[1])):
        for n, dj in enumerate(chosen):
            for at, d in enumerate(turns(ways)):
                for dg in range(flight):
                    out[n, lane ^ d, own ^ dg] = held[at, dg, dj].astype(out.dtype)
    for c, (start, stop) in enumerate(spans):
        own_fresh[start:stop] = fresh[c][...]


def halve_kernel(kept, held, arrived, keep, send):
    for out, chosen in ((keep, kept[0]), (send, kept[1])):
        for n, m in enumerate(chosen):
            out[n] = (held[m] + arrived[m].astype(f32)).astype(out.dtype)


def store_kernel(spans, *refs):
    refs = list(refs)
    news = take(refs, 3 * len(spans))
    outs = take(refs, 3)
    (sems,) = refs
    copies = []
    for c, (start, stop) in enumerate(spans):
        for n in range(3):
            copy = pltpu.make_async_copy(
                news[3 * c + n], outs[n].at[pl.ds(start, stop - start)], sems.at[c, n]
            )
            copy.start()
            copies.append(copy)
    for copy in copies:
        copy.wait()


def gate_kernel(gate, up, held, arrived, d_gate, d_up):
    ways, flight, slots = held.shape[1:4]
    for f in range(flight):
        for v in range(ways):
            at = pl.ds((f * ways + v) * slots, slots)
            grad = held[0, v, f] + arrived[0, v, f].astype(f32)
            g = gate[0, at].astype(f32)
            u = up[0, at].astype(f32)
            sig = jax.nn.sigmoid(g)
            d_gate[0, at] = (grad * u * sig * (1.0 + g * (1.0 - sig))).astype(bf16)
            d_up[0, at] = (grad * (g * sig)).astype(bf16)


def join_kernel(high, entries, *refs):
    out, sems = refs[-2], refs[-1]
    me = lax.axis_index("dp")
    copies = []
    for n, (d, start, stop) in enumerate(entries):
        at = pl.multiple_of((me ^ d) * high + start, 16)
        copy = pltpu.make_async_copy(refs[n], out.at[pl.ds(at, stop - start)], sems.at[n])
        copy.start()
        copies.append(copy)
    for copy in copies:
        copy.wait()


def whole(memory=pltpu.VMEM):
    return pl.BlockSpec(memory_space=memory)


def shape(dims, kind):
    return jax.ShapeDtypeStruct(dims, kind)


def pinned(x):
    return pltpu.with_memory_space_constraint(x, pltpu.HBM)


def local(
    grad_rows,
    router_weight,
    send_counts,
    gate_stash,
    up_stash,
    master_weight,
    first_moment,
    second_moment,
):
    _, flight, slots, width = grad_rows.shape
    pieces = lax.axis_size("dp")
    sources = lax.axis_size("expert")
    ways = sources // flight
    high, across = master_weight.shape
    hbm = whole(pltpu.HBM)
    count = pieces * flight * slots

    def over_dp(x, d):
        return lax.ppermute(x, "dp", [(i, i ^ d) for i in range(pieces)])

    tiles = -(-high // LANES)
    middle = (tiles + 1) // 2 * LANES
    spans = [(0, middle), (middle, high)] if middle < high else [(0, high)]
    offsets = [(dj, dg) for dg in range(flight) for dj in range(0, pieces, 2)]
    results = pl.pallas_call(
        scale_kernel,
        out_shape=[shape((ways, flight, slots, across), bf16)]
        + [shape((2, slots, high), bf16)] * len(offsets),
        in_specs=[hbm] * 5,
        out_specs=[whole()] * (1 + len(offsets)),
        scratch_shapes=[
            pltpu.SMEM(send_counts.shape, jnp.int32),
            pltpu.VMEM(router_weight.shape, f32),
            pltpu.VMEM(grad_rows.shape, bf16),
            pltpu.VMEM(gate_stash.shape, bf16),
            pltpu.VMEM(up_stash.shape, bf16),
            pltpu.VMEM((pieces, flight, slots, high), bf16),
            pltpu.SemaphoreType.DMA((5,)),
        ],
        compiler_params=params(),
        name="scale",
    )(
        pinned(send_counts),
        pinned(router_weight),
        pinned(grad_rows),
        pinned(gate_stash),
        pinned(up_stash),
    )
    hidden, blocks = results[0], list(results[1:])
    for n, (dj, dg) in reversed(list(enumerate(offsets))):
        if n:
            pairs = [
                (i * sources + k, (i ^ dj) * sources + (k ^ (dg * ways)))
                for i in range(pieces)
                for k in range(sources)
            ]
            blocks[n] = lax.ppermute(blocks[n], ("dp", "expert"), pairs)
    state = pl.pallas_call(
        fetch_kernel,
        out_shape=[shape((high, across), f32)] * 3,
        in_specs=[whole(pl.ANY)] + [hbm] * 3,
        out_specs=[whole()] * 3,
        scratch_shapes=[pltpu.SemaphoreType.DMA((3,))],
        compiler_params=params(),
        cost_estimate=cost(0, high * across * 24),
        name="fetch",
    )(hidden, pinned(master_weight), pinned(first_moment), pinned(second_moment))
    order = [*range(len(offsets) - 1, pieces // 2 - 1, -1), *range(1, pieces // 2), 0]
    turned, state = lax.optimization_barrier(([blocks[n] for n in order], state))
    blocks = [turned[order.index(n)] for n in range(len(offsets))]
    other = pl.pallas_call(
        functools.partial(share_kernel, order),
        out_shape=shape((len(offsets), slots, high), bf16),
        in_specs=[whole()] * len(offsets),
        out_specs=whole(),
        compiler_params=params(),
        name="share",
    )(*[blocks[n] for n in order])
    mine = pl.pallas_call(
        functools.partial(pack_kernel, spans),
        out_shape=[shape((2 * len(offsets), slots, stop - start), bf16) for start, stop in spans],
        in_specs=[whole()] * (1 + len(offsets)),
        out_specs=[whole()] * len(spans),
        compiler_params=params(),
        name="pack",
    )(over_dp(other, 1), *blocks)
    top = pieces // 2

    def spread(entries, first):
        step = first
        while step:
            entries = entries + [(d ^ step, *span, over_dp(x, step)) for d, *span, x in entries]
            step //= 2
        return entries

    hiddens = [entry[1] for entry in sorted(spread([(0, hidden)], top), key=lambda e: e[0])]
    right = pl.pallas_call(
        order_kernel,
        out_shape=shape((ways, flight, pieces, slots, across), bf16),
        in_specs=[whole()] * pieces,
        out_specs=whole(),
        compiler_params=params(),
        name="order",
    )(*hiddens)
    rows = []
    for piece in mine:
        rows.append(
            [piece]
            + [
                lax.ppermute(piece, "expert", [(k, k ^ d) for k in range(sources)])
                for d in turns(ways)[1:]
            ]
        )

    fresh, news = [], []
    for c, (start, stop) in enumerate(spans):
        out = pl.pallas_call(
            functools.partial(update_kernel, start, stop),
            out_shape=[shape((stop - start, across), bf16)]
            + [shape((stop - start, across), f32)] * 3,
            in_specs=[whole()] * (ways + 4),
            out_specs=[whole()] * 4,
            scratch_shapes=[pltpu.VMEM((stop - start, across), f32)],
            compiler_params=params(),
            cost_estimate=cost(2 * ways * count * (stop - start) * across, high * across * 26),
            name="update",
        )(*rows[c], right, *state)
        fresh.append(out[0])
        news += out[1:]
    crossed = [over_dp(piece, top) for piece in fresh]

    part = (ways, flight, slots, across)
    bit = 1
    kept = [[d for d in range(pieces) if not d & bit], [d for d in range(pieces) if d & bit]]
    keep, send, own_fresh = pl.pallas_call(
        functools.partial(partial_kernel, spans, kept),
        out_shape=[
            shape((pieces // 2, *part), f32),
            shape((pieces // 2, *part), bf16),
            shape((high, across), bf16),
        ],
        in_specs=[whole()] * ((ways + 1) * len(spans) + 1),
        out_specs=[whole()] * 3,
        scratch_shapes=[pltpu.VMEM((ways, flight, pieces, slots, across), f32)],
        compiler_params=params(),
        cost_estimate=cost(2 * ways * count * high * across, high * across * 12),
        name="partial",
    )(*[block for chunk in rows for block in chunk], *fresh, state[0])
    arrived = over_dp(send, bit)
    while bit < top:
        bit *= 2
        left = kept[0]
        kept = [[d for d in left if not d & bit], [d for d in left if d & bit]]
        chosen = [[left.index(d) for d in half] for half in kept]
        keep, send = pl.pallas_call(
            functools.partial(halve_kernel, chosen),
            out_shape=[
                shape((len(kept[0]), *part), f32),
                shape((len(kept[1]), *part), bf16),
            ],
            in_specs=[whole()] * 2,
            out_specs=[whole()] * 2,
            compiler_params=params(),
            name="halve",
        )(keep, arrived)
        arrived = over_dp(send, bit)
    if len(spans) > 1:
        crossed[0], keep = lax.optimization_barrier((crossed[0], keep))
    d_gate, d_up = pl.pallas_call(
        gate_kernel,
        out_shape=[shape(gate_stash.shape, bf16)] * 2,
        in_specs=[whole()] * 4,
        out_specs=[whole()] * 2,
        compiler_params=params(),
        name="gates",
    )(gate_stash, up_stash, keep, arrived)

    states = pl.pallas_call(
        functools.partial(store_kernel, spans),
        out_shape=[shape((high, across), f32)] * 3,
        in_specs=[whole()] * len(news),
        out_specs=[hbm] * 3,
        scratch_shapes=[pltpu.SemaphoreType.DMA((len(spans), 3))],
        compiler_params=params(),
        cost_estimate=cost(0, high * across * 24),
        name="store",
    )(*news)

    def join(entries, before):
        return pl.pallas_call(
            functools.partial(join_kernel, high, [entry[:3] for entry in entries]),
            out_shape=shape((pieces * high, across), bf16),
            in_specs=[whole(pl.ANY)] * len(entries) + [hbm] * len(before),
            out_specs=hbm,
            input_output_aliases={len(entries): 0} if before else {},
            scratch_shapes=[pltpu.SemaphoreType.DMA((len(entries),))],
            compiler_params=params(),
            name="join",
        )(*[entry[3] for entry in entries], *before)

    near, *far = spread([(0, 0, high, own_fresh)], top // 2)
    early, late = [near], far
    for (start, stop), piece in zip(spans[:-1], crossed[:-1]):
        near, *far = spread([(top, start, stop, piece)], top // 2)
        early.append(near)
        late += far
    joined = join(early, [])
    crossed[-1], joined, states, arrived = lax.optimization_barrier(
        (crossed[-1], joined, states, arrived)
    )
    joined = join(late + spread([(top, *spans[-1], crossed[-1])], top // 2), [joined])
    return (d_gate, d_up, *states, joined)


def solution(mesh):
    placed = (
        P("dp", "expert", None, None),
        P("dp", "expert", None),
        P("dp", "expert"),
        P("dp", None, "expert"),
        P("dp", None, "expert"),
        P("dp", "expert"),
        P("dp", "expert"),
        P("dp", "expert"),
    )
    return jax.shard_map(
        local,
        mesh=mesh,
        in_specs=placed,
        out_specs=(
            P("dp", None, "expert"),
            P("dp", None, "expert"),
            P("dp", "expert"),
            P("dp", "expert"),
            P("dp", "expert"),
            P(None, "expert"),
        ),
        check_vma=False,
    )
```

```python
import functools

import jax
import jax.numpy as jnp
from jax import lax
from jax.experimental import pallas as pl
from jax.experimental.pallas import tpu as pltpu
from jax.sharding import PartitionSpec as P

learning_rate = 0.01
beta_one = 0.9
beta_two = 0.95
decay_rate = 0.1
epsilon = 1e-08

bf16 = jnp.bfloat16
f32 = jnp.float32
VMEM_LIMIT = 40 * 1024 * 1024
LANES = 128


def params():
    return pltpu.CompilerParams(vmem_limit_bytes=VMEM_LIMIT)


def cost(flops, nbytes):
    return pl.CostEstimate(flops=flops, bytes_accessed=nbytes, transcendentals=0)


def take(refs, count):
    taken = refs[:count]
    del refs[:count]
    return taken


def wide(tiles):
    return tiles[0] if len(tiles) == 1 else jnp.concatenate(tiles, axis=1)


def tall(blocks):
    return blocks[0] if len(blocks) == 1 else jnp.concatenate(blocks, axis=0)


def turns(ways):
    return [0, *range(ways - 1, 0, -1)]


def seat_of(ways):
    seat = lax.axis_index("expert")
    return lax.axis_index("dp"), lax.rem(seat, ways), lax.div(seat, ways)


def scale_kernel(counts_in, router_in, rows_in, gate_in, up_in, *refs):
    hidden, outs = refs[0], refs[1:-7]
    counts, router, rows, gate, up, cut, sems = refs[-7:]
    copies = [
        pltpu.make_async_copy(source, target, sems.at[n])
        for n, (source, target) in enumerate(
            [
                (gate_in, gate),
                (up_in, up),
                (counts_in, counts),
                (router_in, router),
                (rows_in, rows),
            ]
        )
    ]
    for copy in copies:
        copy.start()
    flight, slots, width = rows.shape[1:]
    pieces = cut.shape[0]
    piece = width // pieces
    ways = hidden.shape[0]
    me, _, own = seat_of(ways)
    copies[0].wait()
    copies[1].wait()
    g = gate[0].astype(f32)
    value = (g * jax.nn.sigmoid(g) * up[0].astype(f32)).astype(bf16)
    for f in range(flight):
        for v in range(ways):
            at = (f * ways + v) * slots
            hidden[v, f] = value[at : at + slots]
    for copy in copies[2:]:
        copy.wait()
    diagonal = lax.broadcasted_iota(jnp.int32, (slots, slots), 0) == lax.broadcasted_iota(
        jnp.int32, (slots, slots), 1
    )
    row = lax.broadcasted_iota(jnp.int32, (slots, 1), 0)
    for f in range(flight):
        weight = jnp.sum(
            jnp.where(diagonal, jnp.broadcast_to(router[0, f : f + 1, :], (slots, slots)), 0.0),
            axis=1,
            keepdims=True,
        )
        live = row < counts[0, f]
        scaled = jnp.where(live, weight * rows[0, f].astype(f32), 0.0).astype(bf16)
        for i in range(pieces):
            cut[i, f] = scaled[:, i * piece : (i + 1) * piece]
    for n, out in enumerate(outs):
        for dc in range(2):
            out[dc] = cut[me ^ (n % (pieces // 2) * 2 + dc), own ^ (n // (pieces // 2))]


def fetch_kernel(after, *refs):
    del after
    sems = refs[6]
    copies = [pltpu.make_async_copy(refs[n], refs[3 + n], sems.at[n]) for n in range(3)]
    for copy in copies:
        copy.start()
    for copy in copies:
        copy.wait()


def share_kernel(order, *refs):
    for n, block in zip(order, refs):
        refs[-1][n] = block[1]


def pack_kernel(spans, other, *refs):
    blocks, outs = refs[: -len(spans)], refs[-len(spans) :]
    for (start, stop), out in zip(spans, outs):
        for n, block in enumerate(blocks):
            out[2 * n] = block[0, :, start:stop]
            out[2 * n + 1] = other[n, :, start:stop]


def order_kernel(*refs):
    hiddens, right = refs[:-1], refs[-1]
    ways, flight = right.shape[:2]
    _, lane, own = seat_of(ways)
    for dj, hidden in enumerate(hiddens):
        for n, d in enumerate(turns(ways)):
            for dg in range(flight):
                right[n, dg, dj] = hidden[lane ^ d, own ^ dg]


def update_kernel(start, stop, *refs):
    refs = list(refs)
    rows = refs[:-9]
    right, master, first, second, fresh, new_master, new_first, new_second, gradient = refs[-9:]
    hidden = right[...].reshape(-1, right.shape[-1])
    left = tall([block[...].reshape(-1, stop - start) for block in rows])
    gradient[...] = lax.dot_general(
        left, hidden, (((0,), (0,)), ((), ())), preferred_element_type=f32
    )
    for low in range(start, stop, 128):
        end = min(low + 128, stop)
        here = pl.ds(low, end - low)
        there = pl.ds(low - start, end - low)
        grad = gradient[there]
        old = master[here]
        moment_a = beta_one * first[here] + (1.0 - beta_one) * grad
        moment_b = beta_two * second[here] + (1.0 - beta_two) * grad * grad
        step_size = (moment_a * (1.0 / (1.0 - beta_one**5))) / (
            jnp.sqrt(moment_b * (1.0 / (1.0 - beta_two**5))) + epsilon
        )
        updated = old - learning_rate * (step_size + decay_rate * old)
        fresh[there] = updated.astype(bf16)
        new_master[there] = updated
        new_first[there] = moment_a
        new_second[there] = moment_b


def partial_kernel(spans, kept, *refs):
    refs = list(refs)
    chunks = len(spans)
    keep, send, own_fresh, held = refs[-4:]
    ways = held.shape[0]
    rows, fresh, (master,) = take(refs, ways * chunks), take(refs, chunks), take(refs, 1)
    flight = held.shape[1]
    _, lane, own = seat_of(ways)
    left = wide(
        [
            tall([block[...].reshape(-1, stop - start) for block in rows[c * ways : (c + 1) * ways]])
            for c, (start, stop) in enumerate(spans)
        ]
    )
    share = jnp.dot(left, master[...].astype(bf16), preferred_element_type=f32)
    held[...] = share.reshape(held.shape)
    for out, chosen in ((keep, kept[0]), (send, kept[1])):
        for n, dj in enumerate(chosen):
            for at, d in enumerate(turns(ways)):
                for dg in range(flight):
                    out[n, lane ^ d, own ^ dg] = held[at, dg, dj].astype(out.dtype)
    for c, (start, stop) in enumerate(spans):
        own_fresh[start:stop] = fresh[c][...]


def halve_kernel(kept, held, arrived, keep, send):
    for out, chosen in ((keep, kept[0]), (send, kept[1])):
        for n, m in enumerate(chosen):
            out[n] = (held[m] + arrived[m].astype(f32)).astype(out.dtype)


def store_kernel(spans, *refs):
    refs = list(refs)
    news = take(refs, 3 * len(spans))
    outs = take(refs, 3)
    (sems,) = refs
    copies = []
    for c, (start, stop) in enumerate(spans):
        for n in range(3):
            copy = pltpu.make_async_copy(
                news[3 * c + n], outs[n].at[pl.ds(start, stop - start)], sems.at[c, n]
            )
            copy.start()
            copies.append(copy)
    for copy in copies:
        copy.wait()


def gate_kernel(gate, up, held, arrived, d_gate, d_up):
    ways, flight, slots = held.shape[1:4]
    for f in range(flight):
        for v in range(ways):
            at = pl.ds((f * ways + v) * slots, slots)
            grad = held[0, v, f] + arrived[0, v, f].astype(f32)
            g = gate[0, at].astype(f32)
            u = up[0, at].astype(f32)
            sig = jax.nn.sigmoid(g)
            d_gate[0, at] = (grad * u * sig * (1.0 + g * (1.0 - sig))).astype(bf16)
            d_up[0, at] = (grad * (g * sig)).astype(bf16)


def join_kernel(high, entries, *refs):
    out, sems = refs[-2], refs[-1]
    me = lax.axis_index("dp")
    copies = []
    for n, (d, start, stop) in enumerate(entries):
        at = pl.multiple_of((me ^ d) * high + start, 16)
        copy = pltpu.make_async_copy(refs[n], out.at[pl.ds(at, stop - start)], sems.at[n])
        copy.start()
        copies.append(copy)
    for copy in copies:
        copy.wait()


def whole(memory=pltpu.VMEM):
    return pl.BlockSpec(memory_space=memory)


def shape(dims, kind):
    return jax.ShapeDtypeStruct(dims, kind)


def pinned(x):
    return pltpu.with_memory_space_constraint(x, pltpu.HBM)


def local(
    grad_rows,
    router_weight,
    send_counts,
    gate_stash,
    up_stash,
    master_weight,
    first_moment,
    second_moment,
):
    _, flight, slots, width = grad_rows.shape
    pieces = lax.axis_size("dp")
    sources = lax.axis_size("expert")
    ways = sources // flight
    high, across = master_weight.shape
    hbm = whole(pltpu.HBM)
    count = pieces * flight * slots

    def over_dp(x, d):
        return lax.ppermute(x, "dp", [(i, i ^ d) for i in range(pieces)])

    tiles = -(-high // LANES)
    middle = (tiles + 1) // 2 * LANES
    spans = [(0, middle), (middle, high)] if middle < high else [(0, high)]
    offsets = [(dj, dg) for dg in range(flight) for dj in range(0, pieces, 2)]
    results = pl.pallas_call(
        scale_kernel,
        out_shape=[shape((ways, flight, slots, across), bf16)]
        + [shape((2, slots, high), bf16)] * len(offsets),
        in_specs=[hbm] * 5,
        out_specs=[whole()] * (1 + len(offsets)),
        scratch_shapes=[
            pltpu.SMEM(send_counts.shape, jnp.int32),
            pltpu.VMEM(router_weight.shape, f32),
            pltpu.VMEM(grad_rows.shape, bf16),
            pltpu.VMEM(gate_stash.shape, bf16),
            pltpu.VMEM(up_stash.shape, bf16),
            pltpu.VMEM((pieces, flight, slots, high), bf16),
            pltpu.SemaphoreType.DMA((5,)),
        ],
        compiler_params=params(),
        name="scale",
    )(
        pinned(send_counts),
        pinned(router_weight),
        pinned(grad_rows),
        pinned(gate_stash),
        pinned(up_stash),
    )
    hidden, blocks = results[0], list(results[1:])
    for n, (dj, dg) in reversed(list(enumerate(offsets))):
        if n:
            pairs = [
                (i * sources + k, (i ^ dj) * sources + (k ^ (dg * ways)))
                for i in range(pieces)
                for k in range(sources)
            ]
            blocks[n] = lax.ppermute(blocks[n], ("dp", "expert"), pairs)
    state = pl.pallas_call(
        fetch_kernel,
        out_shape=[shape((high, across), f32)] * 3,
        in_specs=[whole(pl.ANY)] + [hbm] * 3,
        out_specs=[whole()] * 3,
        scratch_shapes=[pltpu.SemaphoreType.DMA((3,))],
        compiler_params=params(),
        cost_estimate=cost(0, high * across * 24),
        name="fetch",
    )(hidden, pinned(master_weight), pinned(first_moment), pinned(second_moment))
    order = [*range(len(offsets) - 1, pieces // 2 - 1, -1), *range(1, pieces // 2), 0]
    other = pl.pallas_call(
        functools.partial(share_kernel, order),
        out_shape=shape((len(offsets), slots, high), bf16),
        in_specs=[whole()] * len(offsets),
        out_specs=whole(),
        compiler_params=params(),
        name="share",
    )(*[blocks[n] for n in order])
    mine = pl.pallas_call(
        functools.partial(pack_kernel, spans),
        out_shape=[shape((2 * len(offsets), slots, stop - start), bf16) for start, stop in spans],
        in_specs=[whole()] * (1 + len(offsets)),
        out_specs=[whole()] * len(spans),
        compiler_params=params(),
        name="pack",
    )(over_dp(other, 1), *blocks)
    top = pieces // 2

    def spread(entries, first):
        step = first
        while step:
            entries = entries + [(d ^ step, *span, over_dp(x, step)) for d, *span, x in entries]
            step //= 2
        return entries

    hiddens = [entry[1] for entry in sorted(spread([(0, hidden)], top), key=lambda e: e[0])]
    right = pl.pallas_call(
        order_kernel,
        out_shape=shape((ways, flight, pieces, slots, across), bf16),
        in_specs=[whole()] * pieces,
        out_specs=whole(),
        compiler_params=params(),
        name="order",
    )(*hiddens)
    rows = []
    for c, piece in enumerate(mine):
        if c:
            piece, _ = lax.optimization_barrier((piece, state))
        rows.append(
            [piece]
            + [
                lax.ppermute(piece, "expert", [(k, k ^ d) for k in range(sources)])
                for d in turns(ways)[1:]
            ]
        )

    fresh, news = [], []
    for c, (start, stop) in enumerate(spans):
        out = pl.pallas_call(
            functools.partial(update_kernel, start, stop),
            out_shape=[shape((stop - start, across), bf16)]
            + [shape((stop - start, across), f32)] * 3,
            in_specs=[whole()] * (ways + 4),
            out_specs=[whole()] * 4,
            scratch_shapes=[pltpu.VMEM((stop - start, across), f32)],
            compiler_params=params(),
            cost_estimate=cost(2 * ways * count * (stop - start) * across, high * across * 26),
            name="update",
        )(*rows[c], right, *state)
        fresh.append(out[0])
        news += out[1:]
    crossed = [over_dp(piece, top) for piece in fresh]

    part = (ways, flight, slots, across)
    bit = 1
    kept = [[d for d in range(pieces) if not d & bit], [d for d in range(pieces) if d & bit]]
    keep, send, own_fresh = pl.pallas_call(
        functools.partial(partial_kernel, spans, kept),
        out_shape=[
            shape((pieces // 2, *part), f32),
            shape((pieces // 2, *part), bf16),
            shape((high, across), bf16),
        ],
        in_specs=[whole()] * ((ways + 1) * len(spans) + 1),
        out_specs=[whole()] * 3,
        scratch_shapes=[pltpu.VMEM((ways, flight, pieces, slots, across), f32)],
        compiler_params=params(),
        cost_estimate=cost(2 * ways * count * high * across, high * across * 12),
        name="partial",
    )(*[block for chunk in rows for block in chunk], *fresh, state[0])
    arrived = over_dp(send, bit)
    while bit < top:
        bit *= 2
        left = kept[0]
        kept = [[d for d in left if not d & bit], [d for d in left if d & bit]]
        chosen = [[left.index(d) for d in half] for half in kept]
        keep, send = pl.pallas_call(
            functools.partial(halve_kernel, chosen),
            out_shape=[
                shape((len(kept[0]), *part), f32),
                shape((len(kept[1]), *part), bf16),
            ],
            in_specs=[whole()] * 2,
            out_specs=[whole()] * 2,
            compiler_params=params(),
            name="halve",
        )(keep, arrived)
        arrived = over_dp(send, bit)
    if len(spans) > 1:
        crossed[0], keep = lax.optimization_barrier((crossed[0], keep))
    d_gate, d_up = pl.pallas_call(
        gate_kernel,
        out_shape=[shape(gate_stash.shape, bf16)] * 2,
        in_specs=[whole()] * 4,
        out_specs=[whole()] * 2,
        compiler_params=params(),
        name="gates",
    )(gate_stash, up_stash, keep, arrived)

    states = pl.pallas_call(
        functools.partial(store_kernel, spans),
        out_shape=[shape((high, across), f32)] * 3,
        in_specs=[whole()] * len(news),
        out_specs=[hbm] * 3,
        scratch_shapes=[pltpu.SemaphoreType.DMA((len(spans), 3))],
        compiler_params=params(),
        cost_estimate=cost(0, high * across * 24),
        name="store",
    )(*news)

    def join(entries, before):
        return pl.pallas_call(
            functools.partial(join_kernel, high, [entry[:3] for entry in entries]),
            out_shape=shape((pieces * high, across), bf16),
            in_specs=[whole(pl.ANY)] * len(entries) + [hbm] * len(before),
            out_specs=hbm,
            input_output_aliases={len(entries): 0} if before else {},
            scratch_shapes=[pltpu.SemaphoreType.DMA((len(entries),))],
            compiler_params=params(),
            name="join",
        )(*[entry[3] for entry in entries], *before)

    near, *far = spread([(0, 0, high, own_fresh)], top // 2)
    early, late = [near], far
    for (start, stop), piece in zip(spans[:-1], crossed[:-1]):
        near, *far = spread([(top, start, stop, piece)], top // 2)
        early.append(near)
        late += far
    joined = join(early, [])
    crossed[-1], joined, states, arrived = lax.optimization_barrier(
        (crossed[-1], joined, states, arrived)
    )
    joined = join(late + spread([(top, *spans[-1], crossed[-1])], top // 2), [joined])
    return (d_gate, d_up, *states, joined)


def solution(mesh):
    placed = (
        P("dp", "expert", None, None),
        P("dp", "expert", None),
        P("dp", "expert"),
        P("dp", None, "expert"),
        P("dp", None, "expert"),
        P("dp", "expert"),
        P("dp", "expert"),
        P("dp", "expert"),
    )
    return jax.shard_map(
        local,
        mesh=mesh,
        in_specs=placed,
        out_specs=(
            P("dp", None, "expert"),
            P("dp", None, "expert"),
            P("dp", "expert"),
            P("dp", "expert"),
            P("dp", "expert"),
            P(None, "expert"),
        ),
        check_vma=False,
    )
```

```python
import functools

import jax
import jax.numpy as jnp
from jax import lax
from jax.experimental import pallas as pl
from jax.experimental.pallas import tpu as pltpu
from jax.sharding import PartitionSpec as P

learning_rate = 0.01
beta_one = 0.9
beta_two = 0.95
decay_rate = 0.1
epsilon = 1e-08

bf16 = jnp.bfloat16
f32 = jnp.float32
VMEM_LIMIT = 40 * 1024 * 1024
LANES = 128


def params():
    return pltpu.CompilerParams(vmem_limit_bytes=VMEM_LIMIT)


def cost(flops, nbytes):
    return pl.CostEstimate(flops=flops, bytes_accessed=nbytes, transcendentals=0)


def take(refs, count):
    taken = refs[:count]
    del refs[:count]
    return taken


def wide(tiles):
    return tiles[0] if len(tiles) == 1 else jnp.concatenate(tiles, axis=1)


def tall(blocks):
    return blocks[0] if len(blocks) == 1 else jnp.concatenate(blocks, axis=0)


def turns(ways):
    return [0, *range(ways - 1, 0, -1)]


def seat_of(ways):
    seat = lax.axis_index("expert")
    return lax.axis_index("dp"), lax.rem(seat, ways), lax.div(seat, ways)


def scale_kernel(counts_in, router_in, rows_in, gate_in, up_in, *refs):
    hidden, outs = refs[0], refs[1:-7]
    counts, router, rows, gate, up, cut, sems = refs[-7:]
    copies = [
        pltpu.make_async_copy(source, target, sems.at[n])
        for n, (source, target) in enumerate(
            [
                (gate_in, gate),
                (up_in, up),
                (counts_in, counts),
                (router_in, router),
            ]
            + [(rows_in.at[0, f], rows.at[0, f]) for f in range(rows.shape[1])]
        )
    ]
    for copy in copies[4:] + copies[:4]:
        copy.start()
    flight, slots, width = rows.shape[1:]
    pieces = cut.shape[0]
    piece = width // pieces
    ways = hidden.shape[0]
    me, _, own = seat_of(ways)
    copies[0].wait()
    copies[1].wait()
    g = gate[0].astype(f32)
    value = (g * jax.nn.sigmoid(g) * up[0].astype(f32)).astype(bf16)
    for f in range(flight):
        for v in range(ways):
            at = (f * ways + v) * slots
            hidden[v, f] = value[at : at + slots]
    copies[2].wait()
    copies[3].wait()
    diagonal = lax.broadcasted_iota(jnp.int32, (slots, slots), 0) == lax.broadcasted_iota(
        jnp.int32, (slots, slots), 1
    )
    row = lax.broadcasted_iota(jnp.int32, (slots, 1), 0)
    for f in range(flight):
        copies[4 + f].wait()
        weight = jnp.sum(
            jnp.where(diagonal, jnp.broadcast_to(router[0, f : f + 1, :], (slots, slots)), 0.0),
            axis=1,
            keepdims=True,
        )
        live = row < counts[0, f]
        scaled = jnp.where(live, weight * rows[0, f].astype(f32), 0.0).astype(bf16)
        for i in range(pieces):
            cut[i, f] = scaled[:, i * piece : (i + 1) * piece]
    for n, out in enumerate(outs):
        for dc in range(2):
            out[dc] = cut[me ^ (n % (pieces // 2) * 2 + dc), own ^ (n // (pieces // 2))]


def fetch_kernel(after, *refs):
    del after
    sems = refs[6]
    copies = [pltpu.make_async_copy(refs[n], refs[3 + n], sems.at[n]) for n in range(3)]
    for copy in copies:
        copy.start()
    for copy in copies:
        copy.wait()


def share_kernel(order, *refs):
    for n, block in zip(order, refs):
        refs[-1][n] = block[1]


def pack_kernel(spans, other, *refs):
    blocks, outs = refs[: -len(spans)], refs[-len(spans) :]
    for (start, stop), out in zip(spans, outs):
        for n, block in enumerate(blocks):
            out[2 * n] = block[0, :, start:stop]
            out[2 * n + 1] = other[n, :, start:stop]


def order_kernel(*refs):
    hiddens, right = refs[:-1], refs[-1]
    ways, flight = right.shape[:2]
    _, lane, own = seat_of(ways)
    for dj, hidden in enumerate(hiddens):
        for n, d in enumerate(turns(ways)):
            for dg in range(flight):
                right[n, dg, dj] = hidden[lane ^ d, own ^ dg]


def update_kernel(start, stop, *refs):
    refs = list(refs)
    rows = refs[:-9]
    right, master, first, second, fresh, new_master, new_first, new_second, gradient = refs[-9:]
    hidden = right[...].reshape(-1, right.shape[-1])
    left = tall([block[...].reshape(-1, stop - start) for block in rows])
    gradient[...] = lax.dot_general(
        left, hidden, (((0,), (0,)), ((), ())), preferred_element_type=f32
    )
    for low in range(start, stop, 128):
        end = min(low + 128, stop)
        here = pl.ds(low, end - low)
        there = pl.ds(low - start, end - low)
        grad = gradient[there]
        old = master[here]
        moment_a = beta_one * first[here] + (1.0 - beta_one) * grad
        moment_b = beta_two * second[here] + (1.0 - beta_two) * grad * grad
        step_size = (moment_a * (1.0 / (1.0 - beta_one**5))) / (
            jnp.sqrt(moment_b * (1.0 / (1.0 - beta_two**5))) + epsilon
        )
        updated = old - learning_rate * (step_size + decay_rate * old)
        fresh[there] = updated.astype(bf16)
        new_master[there] = updated
        new_first[there] = moment_a
        new_second[there] = moment_b


def partial_kernel(spans, kept, *refs):
    refs = list(refs)
    chunks = len(spans)
    keep, send, own_fresh, held = refs[-4:]
    ways = held.shape[0]
    rows, fresh, (master,) = take(refs, ways * chunks), take(refs, chunks), take(refs, 1)
    flight = held.shape[1]
    _, lane, own = seat_of(ways)
    left = wide(
        [
            tall([block[...].reshape(-1, stop - start) for block in rows[c * ways : (c + 1) * ways]])
            for c, (start, stop) in enumerate(spans)
        ]
    )
    share = jnp.dot(left, master[...].astype(bf16), preferred_element_type=f32)
    held[...] = share.reshape(held.shape)
    for out, chosen in ((keep, kept[0]), (send, kept[1])):
        for n, dj in enumerate(chosen):
            for at, d in enumerate(turns(ways)):
                for dg in range(flight):
                    out[n, lane ^ d, own ^ dg] = held[at, dg, dj].astype(out.dtype)
    for c, (start, stop) in enumerate(spans):
        own_fresh[start:stop] = fresh[c][...]


def halve_kernel(kept, held, arrived, keep, send):
    for out, chosen in ((keep, kept[0]), (send, kept[1])):
        for n, m in enumerate(chosen):
            out[n] = (held[m] + arrived[m].astype(f32)).astype(out.dtype)


def store_kernel(spans, *refs):
    refs = list(refs)
    news = take(refs, 3 * len(spans))
    outs = take(refs, 3)
    (sems,) = refs
    copies = []
    for c, (start, stop) in enumerate(spans):
        for n in range(3):
            copy = pltpu.make_async_copy(
                news[3 * c + n], outs[n].at[pl.ds(start, stop - start)], sems.at[c, n]
            )
            copy.start()
            copies.append(copy)
    for copy in copies:
        copy.wait()


def gate_kernel(gate, up, held, arrived, d_gate, d_up):
    ways, flight, slots = held.shape[1:4]
    for f in range(flight):
        for v in range(ways):
            at = pl.ds((f * ways + v) * slots, slots)
            grad = held[0, v, f] + arrived[0, v, f].astype(f32)
            g = gate[0, at].astype(f32)
            u = up[0, at].astype(f32)
            sig = jax.nn.sigmoid(g)
            d_gate[0, at] = (grad * u * sig * (1.0 + g * (1.0 - sig))).astype(bf16)
            d_up[0, at] = (grad * (g * sig)).astype(bf16)


def join_kernel(high, entries, *refs):
    out, sems = refs[-2], refs[-1]
    me = lax.axis_index("dp")
    copies = []
    for n, (d, start, stop) in enumerate(entries):
        at = pl.multiple_of((me ^ d) * high + start, 16)
        copy = pltpu.make_async_copy(refs[n], out.at[pl.ds(at, stop - start)], sems.at[n])
        copy.start()
        copies.append(copy)
    for copy in copies:
        copy.wait()


def whole(memory=pltpu.VMEM):
    return pl.BlockSpec(memory_space=memory)


def shape(dims, kind):
    return jax.ShapeDtypeStruct(dims, kind)


def pinned(x):
    return pltpu.with_memory_space_constraint(x, pltpu.HBM)


def local(
    grad_rows,
    router_weight,
    send_counts,
    gate_stash,
    up_stash,
    master_weight,
    first_moment,
    second_moment,
):
    _, flight, slots, width = grad_rows.shape
    pieces = lax.axis_size("dp")
    sources = lax.axis_size("expert")
    ways = sources // flight
    high, across = master_weight.shape
    hbm = whole(pltpu.HBM)
    count = pieces * flight * slots

    def over_dp(x, d):
        return lax.ppermute(x, "dp", [(i, i ^ d) for i in range(pieces)])

    tiles = -(-high // LANES)
    middle = (tiles + 1) // 2 * LANES
    spans = [(0, middle), (middle, high)] if middle < high else [(0, high)]
    offsets = [(dj, dg) for dg in range(flight) for dj in range(0, pieces, 2)]
    results = pl.pallas_call(
        scale_kernel,
        out_shape=[shape((ways, flight, slots, across), bf16)]
        + [shape((2, slots, high), bf16)] * len(offsets),
        in_specs=[hbm] * 5,
        out_specs=[whole()] * (1 + len(offsets)),
        scratch_shapes=[
            pltpu.SMEM(send_counts.shape, jnp.int32),
            pltpu.VMEM(router_weight.shape, f32),
            pltpu.VMEM(grad_rows.shape, bf16),
            pltpu.VMEM(gate_stash.shape, bf16),
            pltpu.VMEM(up_stash.shape, bf16),
            pltpu.VMEM((pieces, flight, slots, high), bf16),
            pltpu.SemaphoreType.DMA((4 + flight,)),
        ],
        compiler_params=params(),
        name="scale",
    )(
        pinned(send_counts),
        pinned(router_weight),
        pinned(grad_rows),
        pinned(gate_stash),
        pinned(up_stash),
    )
    hidden, blocks = results[0], list(results[1:])
    for n, (dj, dg) in reversed(list(enumerate(offsets))):
        if n:
            pairs = [
                (i * sources + k, (i ^ dj) * sources + (k ^ (dg * ways)))
                for i in range(pieces)
                for k in range(sources)
            ]
            blocks[n] = lax.ppermute(blocks[n], ("dp", "expert"), pairs)
    state = pl.pallas_call(
        fetch_kernel,
        out_shape=[shape((high, across), f32)] * 3,
        in_specs=[whole(pl.ANY)] + [hbm] * 3,
        out_specs=[whole()] * 3,
        scratch_shapes=[pltpu.SemaphoreType.DMA((3,))],
        compiler_params=params(),
        cost_estimate=cost(0, high * across * 24),
        name="fetch",
    )(hidden, pinned(master_weight), pinned(first_moment), pinned(second_moment))
    order = [*range(pieces // 2, len(offsets)), *range(1, pieces // 2), 0]
    turned, state = lax.optimization_barrier(([blocks[n] for n in order], state))
    blocks = [turned[order.index(n)] for n in range(len(offsets))]
    other = pl.pallas_call(
        functools.partial(share_kernel, order),
        out_shape=shape((len(offsets), slots, high), bf16),
        in_specs=[whole()] * len(offsets),
        out_specs=whole(),
        compiler_params=params(),
        name="share",
    )(*[blocks[n] for n in order])
    mine = pl.pallas_call(
        functools.partial(pack_kernel, spans),
        out_shape=[shape((2 * len(offsets), slots, stop - start), bf16) for start, stop in spans],
        in_specs=[whole()] * (1 + len(offsets)),
        out_specs=[whole()] * len(spans),
        compiler_params=params(),
        name="pack",
    )(over_dp(other, 1), *blocks)
    top = pieces // 2

    def spread(entries, first):
        step = first
        while step:
            entries = entries + [(d ^ step, *span, over_dp(x, step)) for d, *span, x in entries]
            step //= 2
        return entries

    hiddens = [entry[1] for entry in sorted(spread([(0, hidden)], top), key=lambda e: e[0])]
    right = pl.pallas_call(
        order_kernel,
        out_shape=shape((ways, flight, pieces, slots, across), bf16),
        in_specs=[whole()] * pieces,
        out_specs=whole(),
        compiler_params=params(),
        name="order",
    )(*hiddens)
    rows = []
    for piece in mine:
        rows.append(
            [piece]
            + [
                lax.ppermute(piece, "expert", [(k, k ^ d) for k in range(sources)])
                for d in turns(ways)[1:]
            ]
        )

    fresh, news = [], []
    for c, (start, stop) in enumerate(spans):
        out = pl.pallas_call(
            functools.partial(update_kernel, start, stop),
            out_shape=[shape((stop - start, across), bf16)]
            + [shape((stop - start, across), f32)] * 3,
            in_specs=[whole()] * (ways + 4),
            out_specs=[whole()] * 4,
            scratch_shapes=[pltpu.VMEM((stop - start, across), f32)],
            compiler_params=params(),
            cost_estimate=cost(2 * ways * count * (stop - start) * across, high * across * 26),
            name="update",
        )(*rows[c], right, *state)
        fresh.append(out[0])
        news += out[1:]
    crossed = [over_dp(piece, top) for piece in fresh]

    part = (ways, flight, slots, across)
    bit = 1
    kept = [[d for d in range(pieces) if not d & bit], [d for d in range(pieces) if d & bit]]
    keep, send, own_fresh = pl.pallas_call(
        functools.partial(partial_kernel, spans, kept),
        out_shape=[
            shape((pieces // 2, *part), f32),
            shape((pieces // 2, *part), bf16),
            shape((high, across), bf16),
        ],
        in_specs=[whole()] * ((ways + 1) * len(spans) + 1),
        out_specs=[whole()] * 3,
        scratch_shapes=[pltpu.VMEM((ways, flight, pieces, slots, across), f32)],
        compiler_params=params(),
        cost_estimate=cost(2 * ways * count * high * across, high * across * 12),
        name="partial",
    )(*[block for chunk in rows for block in chunk], *fresh, state[0])
    arrived = over_dp(send, bit)
    while bit < top:
        bit *= 2
        left = kept[0]
        kept = [[d for d in left if not d & bit], [d for d in left if d & bit]]
        chosen = [[left.index(d) for d in half] for half in kept]
        keep, send = pl.pallas_call(
            functools.partial(halve_kernel, chosen),
            out_shape=[
                shape((len(kept[0]), *part), f32),
                shape((len(kept[1]), *part), bf16),
            ],
            in_specs=[whole()] * 2,
            out_specs=[whole()] * 2,
            compiler_params=params(),
            name="halve",
        )(keep, arrived)
        arrived = over_dp(send, bit)
    if len(spans) > 1:
        crossed[0], keep = lax.optimization_barrier((crossed[0], keep))
    d_gate, d_up = pl.pallas_call(
        gate_kernel,
        out_shape=[shape(gate_stash.shape, bf16)] * 2,
        in_specs=[whole()] * 4,
        out_specs=[whole()] * 2,
        compiler_params=params(),
        name="gates",
    )(gate_stash, up_stash, keep, arrived)

    states = pl.pallas_call(
        functools.partial(store_kernel, spans),
        out_shape=[shape((high, across), f32)] * 3,
        in_specs=[whole()] * len(news),
        out_specs=[hbm] * 3,
        scratch_shapes=[pltpu.SemaphoreType.DMA((len(spans), 3))],
        compiler_params=params(),
        cost_estimate=cost(0, high * across * 24),
        name="store",
    )(*news)

    def join(entries, before):
        return pl.pallas_call(
            functools.partial(join_kernel, high, [entry[:3] for entry in entries]),
            out_shape=shape((pieces * high, across), bf16),
            in_specs=[whole(pl.ANY)] * len(entries) + [hbm] * len(before),
            out_specs=hbm,
            input_output_aliases={len(entries): 0} if before else {},
            scratch_shapes=[pltpu.SemaphoreType.DMA((len(entries),))],
            compiler_params=params(),
            name="join",
        )(*[entry[3] for entry in entries], *before)

    near, *far = spread([(0, 0, high, own_fresh)], top // 2)
    early, late = [near], far
    for (start, stop), piece in zip(spans[:-1], crossed[:-1]):
        near, *far = spread([(top, start, stop, piece)], top // 2)
        early.append(near)
        late += far
    joined = join(early, [])
    crossed[-1], joined, states, arrived = lax.optimization_barrier(
        (crossed[-1], joined, states, arrived)
    )
    joined = join(late + spread([(top, *spans[-1], crossed[-1])], top // 2), [joined])
    return (d_gate, d_up, *states, joined)


def solution(mesh):
    placed = (
        P("dp", "expert", None, None),
        P("dp", "expert", None),
        P("dp", "expert"),
        P("dp", None, "expert"),
        P("dp", None, "expert"),
        P("dp", "expert"),
        P("dp", "expert"),
        P("dp", "expert"),
    )
    return jax.shard_map(
        local,
        mesh=mesh,
        in_specs=placed,
        out_specs=(
            P("dp", None, "expert"),
            P("dp", None, "expert"),
            P("dp", "expert"),
            P("dp", "expert"),
            P("dp", "expert"),
            P(None, "expert"),
        ),
        check_vma=False,
    )
```
